128 devices in a mesh: lat: 8 (over x_lo, z), lon: 16 (over x_hi, y, core).
Axes of the slice: x: 4 (x_hi: 2, x_lo: 2; x = x_hi * 2 + x_lo), y: 4, z: 4, core: 2. Of those that a mesh axis runs over, the one named last changes fastest.
Arguments:
- tokens: bfloat16 [4, 48, 384, 512], P(None, 'lat', 'lon'), may hold values from -6 to 6
- cotangent: bfloat16 [4, 48, 384, 512], P(None, 'lat', 'lon'), may hold values from -6 to 6
- region_ids: int32 [4, 48, 384], P(None, 'lat', 'lon'), may hold values from 0 to 3
- norm_gain: float32 [512], replicated, may hold values from 0.1 to 1.9
- qkv_weight: bfloat16 [512, 1536], replicated
- out_weight: bfloat16 [512, 512], replicated, may hold values from -0.25 to 0.25
Outputs:
- result: bfloat16 [4, 48, 384, 512], P(None, 'lat', 'lon')
- grad_input: bfloat16 [4, 48, 384, 512], P(None, 'lat', 'lon')
- grad_qkv: float32 [512, 1536], P('lat', 'lon')
- grad_out: float32 [512, 512], P('lat', 'lon')
The draws below stay inside these ranges and needn't reach their ends.
All inputs are finite; a program needn't handle non-finite values.
Results may differ from the reference program's by a relative error of at most 0.0059.
The reference program's roundings to bfloat16 on the way (of `normed_bf`, `projected`, `weights_bf`, `attended`, `shifted_out`, `grad_projected` and `grad_shifted`) count: a program that leaves them out, or rounds other values in their place, can miss the bound.
Values may be sent and summed in bfloat16 or wider, within the bound.
A program may use at most 128 MiB of HBM per device.

```python
import jax
import jax.numpy as jnp
from jax import lax

D = 512
HEADS = 8
LEV = 4
LAT = 48
LON = 384


def draw_qkv_weight(key, part):
    key = jax.random.fold_in(key, 7)
    base = jnp.clip(jax.random.normal(key, (D, 3 * D), jnp.float32), -6.0, 6.0) * D ** (-0.5)
    return base.astype(jnp.bfloat16)


def plant(values, key, low, top_value):
    dims = values.shape
    place = [jax.random.randint(jax.random.fold_in(key, axis), (), 0, dims[axis]) for axis in range(len(dims))]
    values = values.at[tuple(place)].set(low)
    longest = dims.index(max(dims))
    place[longest] = (place[longest] + 1) % dims[longest]
    return values.at[tuple(place)].set(top_value)


def strengthened(values, stream_key, source, target, blocks, factor):
    owner, partner = [(jnp.arange(values.shape[position]) // (values.shape[position] // blocks)).reshape([-1 if axis == position else 1 for axis in range(values.ndim)]) for position in (source, target)]
    chosen = jax.random.permutation(stream_key, blocks)[partner]
    strong = (owner == chosen) | (owner == (partner + blocks // 2) % blocks)
    return jnp.where(strong, factor * values, values)


def block_scale(own_key, extent, cuts, least, largest):
    level, own = 1.0, jax.random.fold_in(own_key, 6)
    for axis_at, shards_of in cuts:
        draws = jnp.exp(jax.random.uniform(jax.random.fold_in(own, axis_at), (shards_of,), jnp.float32, least / len(cuts), largest / len(cuts)))
        level = level * jnp.repeat(draws, extent[axis_at] // shards_of).reshape([-1 if axis == axis_at else 1 for axis in range(len(extent))])
    return level


def gaussian(rng, shape, scale, bound, split=(), dtype=jnp.bfloat16):
    values = scale * jax.random.normal(rng, shape, jnp.float32)
    if split:
        values = values * block_scale(rng, shape, split, -0.22, 0.18)
    return jnp.clip(values, -bound, bound).astype(dtype)


def noise_with(key, extent, scale, bound, cuts, heavy, kind=jnp.bfloat16):
    entries = scale * jax.random.normal(key, extent, jnp.float32)
    if cuts:
        entries = entries * block_scale(key, extent, cuts, -0.22, 0.18)
    return jnp.clip(strengthened(entries, jax.random.fold_in(key, 3), *heavy), -bound, bound).astype(kind)


def setup_inputs(seed: int = 0) -> dict:
    seeds = jax.random.split(jax.random.key(seed), 7)
    tokens = gaussian(seeds[0], (LEV, LAT, LON, D), 1.0, 6.0, ((1, 8), (2, 16)))
    cotangent = noise_with(seeds[1], (LEV, LAT, LON, D), 1.0, 6.0, ((1, 8), (2, 16)), (2, 3, 16, 2.0))
    region_ids = plant(jax.random.randint(seeds[2], (LEV, LAT, LON), 0, 4), jax.random.fold_in(seeds[2], 1), 0, 3).astype(jnp.int32)
    norm_gain = jnp.clip(1.0 + 0.18 * jax.random.normal(seeds[3], (D,), jnp.float32), 0.1, 1.9)
    qkv_weight = draw_qkv_weight(jax.random.fold_in(seeds[6], 71), 0)
    out_weight = gaussian(seeds[5], (D, D), D ** -0.5, 0.25)
    return dict(tokens=tokens, cotangent=cotangent, region_ids=region_ids, norm_gain=norm_gain, qkv_weight=qkv_weight, out_weight=out_weight)


def einsum_f32(form, left, right):
    return jnp.einsum(form, left.astype(jnp.float32), right.astype(jnp.float32))

def flatten(array):
    return array.reshape(-1, array.shape[-1])

def window_split(array):
    levels, rows, columns = array.shape[:3]
    rest = array.shape[3:]
    sectioned = array.reshape((levels // 2, 2, rows // 6, 6, columns // 12, 12) + rest)
    order = (0, 2, 4, 1, 3, 5) + tuple(range(6, 6 + len(rest)))
    sectioned = sectioned.transpose(order)
    return sectioned.reshape((levels // 2 * (rows // 6), columns // 12, 144) + rest)

def window_join(array, levels, rows, columns):
    rest = array.shape[3:]
    sectioned = array.reshape((levels // 2, rows // 6, columns // 12, 2, 6, 12) + rest)
    order = (0, 3, 1, 4, 2, 5) + tuple(range(6, 6 + len(rest)))
    return sectioned.transpose(order).reshape((levels, rows, columns) + rest)

def roll_cells(array, sign):
    return jnp.roll(array, (sign * 1, sign * 3, sign * 6), (0, 1, 2))

def block_step(shifted, shifted_cot, region, norm_gain, qkv_weight, out_weight):
    windows, span, width = shifted.shape
    head_dim = width // HEADS
    factor = head_dim ** (-0.5)
    contract = (((0,), (0,)), ((), ()))
    against = (((1,), (1,)), ((), ()))
    inputs = shifted.astype(jnp.float32)
    center = lax.optimization_barrier(jnp.mean(inputs, -1, keepdims=True))
    centered = inputs - center
    variance = lax.optimization_barrier(jnp.mean(centered * centered, -1, keepdims=True))
    inv_std = lax.rsqrt(variance + 1e-05)
    normed = centered * inv_std
    normed_bf = (normed * norm_gain).astype(jnp.bfloat16)
    projected = jnp.dot(flatten(normed_bf), qkv_weight, preferred_element_type=jnp.float32).astype(jnp.bfloat16)
    projected = projected.reshape(windows, span, 3, HEADS, head_dim)
    queries, key_rows, values = (projected[:, :, 0], projected[:, :, 1], projected[:, :, 2])
    scores = einsum_f32('wqhe,wkhe->whqk', queries, key_rows) * factor
    allowed = (region[:, :, None] == region[:, None, :])[:, None]
    scores = jnp.where(allowed, scores, -1e+30)
    row_max = lax.optimization_barrier(jnp.max(scores, -1, keepdims=True))
    powers = jnp.exp(scores - row_max)
    attn_weights = powers / lax.optimization_barrier(jnp.sum(powers, -1, keepdims=True))
    weights_bf = attn_weights.astype(jnp.bfloat16)
    attended = einsum_f32('whqk,wkhe->wqhe', weights_bf, values).astype(jnp.bfloat16)
    attended_flat = attended.reshape(windows * span, width)
    branch = jnp.dot(attended_flat, out_weight, preferred_element_type=jnp.float32)
    shifted_out = (inputs + branch.reshape(windows, span, width)).astype(jnp.bfloat16)
    cot_flat = flatten(shifted_cot)
    grad_attended = lax.dot_general(cot_flat, out_weight, against, preferred_element_type=jnp.float32).astype(jnp.bfloat16)
    grad_out = lax.dot_general(attended_flat, cot_flat, contract, preferred_element_type=jnp.float32)
    grad_heads = grad_attended.reshape(windows, span, HEADS, head_dim)
    grad_values = einsum_f32('whqk,wqhe->wkhe', weights_bf, grad_heads).astype(jnp.bfloat16)
    grad_weights = einsum_f32('wqhe,wkhe->whqk', grad_heads, values)
    inner = lax.optimization_barrier(jnp.sum(grad_weights * attn_weights, -1, keepdims=True))
    grad_scores = (attn_weights * (grad_weights - inner) * factor).astype(jnp.bfloat16)
    grad_queries = einsum_f32('whqk,wkhe->wqhe', grad_scores, key_rows).astype(jnp.bfloat16)
    grad_keys = einsum_f32('whqk,wqhe->wkhe', grad_scores, queries).astype(jnp.bfloat16)
    grad_projected = jnp.stack([grad_queries, grad_keys, grad_values], 2).reshape(windows * span, 3 * width)
    grad_qkv = lax.dot_general(flatten(normed_bf), grad_projected, contract, preferred_element_type=jnp.float32)
    grad_normed = lax.dot_general(grad_projected, qkv_weight, against, preferred_element_type=jnp.float32)
    grad_hat = grad_normed.reshape(windows, span, width) * norm_gain
    grad_shifted = inv_std * (grad_hat - lax.optimization_barrier(jnp.mean(grad_hat, -1, keepdims=True)) - normed * lax.optimization_barrier(jnp.mean(grad_hat * normed, -1, keepdims=True)))
    return (shifted_out, grad_shifted.astype(jnp.bfloat16), grad_qkv, grad_out)

def reference(tokens, cotangent, region_ids, norm_gain, qkv_weight, out_weight):
    levels, rows, columns = tokens.shape[:3]
    win_tokens = window_split(roll_cells(tokens, 1))
    win_cot = window_split(roll_cells(cotangent, 1))
    win_region = window_split(region_ids)

    def group_step(pieces):
        return block_step(pieces[0], pieces[1], pieces[2], norm_gain, qkv_weight, out_weight)
    outputs, grads_in, grads_qkv, grads_out = lax.map(group_step, (win_tokens, win_cot, win_region))
    result = roll_cells(window_join(outputs, levels, rows, columns), -1)
    returned = roll_cells(window_join(grads_in, levels, rows, columns), -1)
    grad_input = (cotangent.astype(jnp.float32) + returned.astype(jnp.float32)).astype(jnp.bfloat16)
    return (result, grad_input, lax.optimization_barrier(jnp.sum(grads_qkv, 0)), lax.optimization_barrier(jnp.sum(grads_out, 0)))
```

```python
import jax
import jax.numpy as jnp
from jax import lax
import numpy as np
from jax.experimental import pallas as pl
from jax.experimental.pallas import tpu as pltpu
from jax.sharding import PartitionSpec as P

SPAN = 144
NN = (((1,), (0,)), ((), ()))
NT = (((1,), (1,)), ((), ()))
BF = jnp.bfloat16
F32 = jnp.float32


def from_behind(array, axis, by):
    count = lax.axis_size(axis)
    return lax.ppermute(array, axis, [(i, (i + by) % count) for i in range(count)])


def window_split(array):
    levels, rows, columns = array.shape[:3]
    rest = array.shape[3:]
    sectioned = array.reshape((levels // 2, 2, rows // 6, 6, columns // 12, 12) + rest)
    order = (0, 2, 4, 1, 3, 5) + tuple(range(6, 6 + len(rest)))
    sectioned = sectioned.transpose(order)
    return sectioned.reshape((levels // 2 * (rows // 6) * (columns // 12), 144) + rest)


def window_join(array, levels, rows, columns):
    rest = array.shape[2:]
    sectioned = array.reshape((levels // 2, rows // 6, columns // 12, 2, 6, 12) + rest)
    order = (0, 3, 1, 4, 2, 5) + tuple(range(6, 6 + len(rest)))
    return sectioned.transpose(order).reshape((levels, rows, columns) + rest)


def roll_ahead(block):
    block = jnp.roll(block, 1, 0)
    came = from_behind(block[:, -3:], "lat", 1)
    block = jnp.concatenate([came, block[:, :-3]], 1)
    came = from_behind(block[:, :, -6:], "lon", 1)
    return jnp.concatenate([came, block[:, :, :-6]], 2)


def roll_behind(block):
    block = jnp.roll(block, -1, 0)
    came = from_behind(block[:, :3], "lat", -1)
    block = jnp.concatenate([block[:, 3:], came], 1)
    came = from_behind(block[:, :, :6], "lon", -1)
    return jnp.concatenate([block[:, :, 6:], came], 2)


def dot(a, b, dims=NN):
    return lax.dot_general(a, b, dims, preferred_element_type=F32)


def compute_kernel(x_ref, cot_ref, hot_ref, gain_ref, w_ref, wo_ref, eye_ref,
                   out_ref, gs_ref, gqkv_ref, gout_ref,
                   normed_ref, nbf_ref, inv_ref, proj_ref, att_ref, ga_ref, gp_ref, tr_ref):
    tokens, width = x_ref.shape
    windows = tokens // SPAN
    gain = gain_ref[...]
    for w in range(windows):
        rows = pl.ds(w * SPAN, SPAN)
        x = x_ref[rows, :].astype(F32)
        centered = x - jnp.mean(x, -1, keepdims=True)
        var = jnp.mean(centered * centered, -1, keepdims=True)
        inv = lax.rsqrt(var + 1e-5)
        normed = centered * inv
        normed_ref[rows, :] = normed
        inv_ref[rows, :] = inv
        nbf_ref[rows, :] = (normed * gain).astype(BF)
    for c in range(6):
        cols = pl.ds(c * 256, 256)
        proj_ref[:, cols] = dot(nbf_ref[...], w_ref[:, cols]).astype(BF)
    for c in range(2):
        ga_ref[:, pl.ds(c * 256, 256)] = dot(cot_ref[...], wo_ref[pl.ds(c * 256, 256), :], NT).astype(BF)

    lane = lax.broadcasted_iota(jnp.int32, (1, 128), 1)
    masks = [jnp.where((lane < 64) == (h == 0), 1.0, 0.0).astype(BF) for h in range(2)]
    eighths = [(m * 0.125).astype(BF) for m in masks]
    eye = eye_ref[...]
    eye128 = eye_ref[:128, :128]

    def pair(p, _):
        at = pl.multiple_of(p * 128, 128)
        for w in range(windows):
            rows = pl.ds(w * SPAN, SPAN)
            q2 = proj_ref[rows, pl.ds(at, 128)]
            k2 = proj_ref[rows, pl.ds(pl.multiple_of(512 + at, 128), 128)]
            v2 = proj_ref[rows, pl.ds(pl.multiple_of(1024 + at, 128), 128)]
            g2 = ga_ref[rows, pl.ds(at, 128)]
            hot = hot_ref[rows, :]
            qx = jnp.concatenate([q2, hot * jnp.array(-1e30, BF)], 1)
            off = (1.0 - hot.astype(F32)).astype(BF)
            qt = dot(eye128, q2 * jnp.array(0.125, BF), NT).astype(BF)
            gt = dot(eye128, g2, NT).astype(BF)
            att = []
            gq = None
            gkt = []
            gvt = []
            for h in range(2):
                kh = k2 * eighths[h]
                s = dot(qx, jnp.concatenate([kh, off], 1), NT)
                m = jnp.max(s, -1, keepdims=True)
                e = jnp.exp(s - m)
                a = e * (1.0 / jnp.sum(e, -1, keepdims=True))
                abf = a.astype(BF)
                att.append(dot(abf, v2))
                gw = dot(g2, v2 * masks[h], NT)
                prod = gw * a
                inner = jnp.sum(prod, -1, keepdims=True)
                ds = (prod - a * inner).astype(BF)
                part = dot(ds, kh)
                gq = part if gq is None else gq + part
                gkt.append(dot(qt[64 * h:64 * h + 64], ds))
                gvt.append(dot(gt[64 * h:64 * h + 64], abf))
            att_ref[rows, pl.ds(at, 128)] = jnp.where(lane < 64, att[0], att[1]).astype(BF)
            gp_ref[rows, pl.ds(at, 128)] = gq.astype(BF)
            gk = dot(eye, jnp.concatenate(gkt, 0).astype(BF), NT)
            gv = dot(eye, jnp.concatenate(gvt, 0).astype(BF), NT)
            gp_ref[rows, pl.ds(pl.multiple_of(512 + at, 128), 128)] = gk.astype(BF)
            gp_ref[rows, pl.ds(pl.multiple_of(1024 + at, 128), 128)] = gv.astype(BF)
        return 0

    lax.fori_loop(0, 4, pair, 0)

    for w in range(windows):
        rows = pl.ds(w * SPAN, SPAN)
        branch = dot(att_ref[rows, :], wo_ref[...])
        out_ref[rows, :] = (x_ref[rows, :].astype(F32) + branch).astype(BF)
        gh = dot(gp_ref[rows, :], w_ref[...], NT) * gain
        normed = normed_ref[rows, :]
        gs = inv_ref[rows, :] * (gh - jnp.mean(gh, -1, keepdims=True)
                                 - normed * jnp.mean(gh * normed, -1, keepdims=True))
        gs_ref[rows, :] = gs.astype(BF)
    tr_ref[...] = nbf_ref[...].T
    for c in range(6):
        cols = pl.ds(c * 256, 256)
        gqkv_ref[:, cols] = dot(tr_ref[...], gp_ref[:, cols])
    tr_ref[...] = att_ref[...].T
    for c in range(2):
        cols = pl.ds(c * 256, 256)
        gout_ref[:, cols] = dot(tr_ref[...], cot_ref[:, cols])


def compute(x, cot, hot, gain, w, wo):
    tokens, width = x.shape
    eye = jnp.asarray(np.eye(SPAN), BF)
    vm = pl.BlockSpec(memory_space=pltpu.VMEM)
    return pl.pallas_call(
        compute_kernel,
        out_shape=(
            jax.ShapeDtypeStruct((tokens, width), BF),
            jax.ShapeDtypeStruct((tokens, width), BF),
            jax.ShapeDtypeStruct((width, 3 * width), F32),
            jax.ShapeDtypeStruct((width, width), F32),
        ),
        in_specs=[vm] * 7,
        out_specs=(vm,) * 4,
        scratch_shapes=[
            pltpu.VMEM((tokens, width), F32),
            pltpu.VMEM((tokens, width), BF),
            pltpu.VMEM((tokens, 1), F32),
            pltpu.VMEM((tokens, 3 * width), BF),
            pltpu.VMEM((tokens, width), BF),
            pltpu.VMEM((tokens, width), BF),
            pltpu.VMEM((tokens, 3 * width), BF),
            pltpu.VMEM((width, tokens), BF),
        ],
        compiler_params=pltpu.CompilerParams(vmem_limit_bytes=48 << 20),
    )(x, cot, hot, gain, w, wo, eye)


def on_device(tokens, cotangent, region_ids, norm_gain, qkv_weight, out_weight):
    levels, rows, columns, width = tokens.shape
    rolled = roll_ahead(jnp.concatenate([tokens, cotangent], -1))
    shifted = window_split(rolled[..., :width])
    shifted_cot = window_split(rolled[..., width:])
    region = window_split(region_ids)
    hot = (region.reshape(-1, 1) == jnp.arange(128)[None]).astype(BF)
    shifted_out, grad_shifted, grad_qkv, grad_out = compute(
        shifted.reshape(-1, width), shifted_cot.reshape(-1, width), hot, norm_gain.reshape(1, -1), qkv_weight, out_weight
    )
    shifted_out, grad_shifted = shifted_out.reshape(4, SPAN, width), grad_shifted.reshape(4, SPAN, width)
    joined = jnp.concatenate(
        [
            window_join(shifted_out, levels, rows, columns),
            window_join(grad_shifted, levels, rows, columns),
        ],
        -1,
    )
    returned = roll_behind(joined)
    result = returned[..., :width]
    grad_input = (cotangent.astype(jnp.float32) + returned[..., width:].astype(jnp.float32)).astype(
        jnp.bfloat16
    )
    first_qkv, first_out = (
        lax.psum_scatter(grad_qkv, "lat", scatter_dimension=0, tiled=True),
        lax.psum_scatter(grad_out, "lat", scatter_dimension=0, tiled=True),
    )
    owned_qkv, owned_out = (
        lax.psum_scatter(first_qkv, "lon", scatter_dimension=1, tiled=True),
        lax.psum_scatter(first_out, "lon", scatter_dimension=1, tiled=True),
    )
    return (result, grad_input, owned_qkv, owned_out)


def solution(mesh):
    placed = (
        P(None, "lat", "lon", None),
        P(None, "lat", "lon", None),
        P(None, "lat", "lon"),
        P(),
        P(),
        P(),
    )
    return jax.shard_map(
        on_device,
        mesh=mesh,
        in_specs=placed,
        out_specs=(
            P(None, "lat", "lon", None),
            P(None, "lat", "lon", None),
            P("lat", "lon"),
            P("lat", "lon"),
        ),
        check_vma=False,
    )
```

```python
import functools

import jax
import jax.numpy as jnp
import numpy as np
from jax import lax
from jax.experimental import pallas as pl
from jax.experimental.pallas import tpu as pltpu
from jax.sharding import PartitionSpec as P

SPAN = 144
TOKENS = 576
PACKED = 640
WIDTH = 512
NN = (((1,), (0,)), ((), ()))
NT = (((1,), (1,)), ((), ()))
BF = jnp.bfloat16
F32 = jnp.float32
MESH = pl.DeviceIdType.MESH

SECTIONS = (
    ("local", 0, 224, (0, 0)),
    ("lat+", 224, 112, (1, 0)),
    ("lat-", 336, 112, (-1, 0)),
    ("lon+", 448, 48, (0, 1)),
    ("lon-", 496, 48, (0, -1)),
    ("diag+", 544, 48, (1, 1)),
    ("diag-", 592, 48, (-1, -1)),
)
GOES = {
    (0, 0, 1): "local", (0, 1, 1): "lat+", (0, 0, 0): "local",
    (0, 0, 2): "lon+", (0, 1, 0): "lat+", (0, 1, 2): "diag+",
    (1, 1, 1): "local", (1, 0, 1): "lat-", (1, 1, 2): "local",
    (1, 1, 0): "lon-", (1, 0, 2): "lat-", (1, 0, 0): "diag-",
}
ORDERS = ((2, 1, 0), (1, 0, 2), (0, 2, 1), (0, 1, 2))


def constants():
    pack = np.zeros((PACKED, TOKENS), np.float32)
    window = np.zeros((TOKENS, PACKED), np.float32)
    first = {name: row for name, row, _, _ in SECTIONS}
    filled = dict.fromkeys(first, 0)
    for t in range(TOKENS):
        l, a, o = t // 144, t // 24 % 6, t % 24
        level = (l + 1) % 4
        piece = 0 if o < 6 else 1 if o < 18 else 2
        name = GOES[level // 2, a // 3, piece]
        row = first[name] + filled[name]
        filled[name] += 1
        pack[row, t] = 1
        column = (o + 6) % 12
        which = level // 2 * 2 + (0 if piece == 1 else 1)
        window[which * SPAN + level % 2 * 72 + (a + 3) % 6 * 12 + column, row] = 1
    row_of = np.zeros((TOKENS, 48), np.float32)
    column_of = np.zeros((TOKENS, 128), np.float32)
    for which in range(4):
        source = (0, 0, 1, 2)[which]
        for n in range(SPAN):
            t = which * SPAN + n
            row_of[t, (source * 2 + n // 72) * 8 + n // 12 % 6] = 1
            column_of[t, n % 12 + (12 if which % 2 == 0 else 0)] = 1
    mix = np.zeros((512, 512), np.float32)
    for jj in range(4):
        for r in range(96):
            mix[96 * jj + r, 128 * jj + r] = 1
        for r in range(32):
            mix[384 + 32 * jj + r, 128 * jj + 96 + r] = 1
    eye = np.eye(SPAN, dtype=np.float32)
    made = pack, window, pack.T, window.T, row_of, column_of, mix, eye
    return [jnp.asarray(m, BF) for m in made]


def dot(a, b, dims=NN):
    return lax.dot_general(a, b, dims, preferred_element_type=F32)


def kernel(x_hbm, cot_hbm, region_ref, gain_ref, w_hbm, wo_hbm,
           pack_hbm, window_hbm, unpack_hbm, unwindow_hbm, row_ref, column_ref, mix_hbm, eye_ref,
           result_ref, grad_ref, owned_ref,
           x_ref, cot_ref, w_ref, wo_ref, pack_ref, window_ref, unpack_ref, unwindow_ref, mix_ref,
           px_ref, pc_ref, rx_ref, rc_ref, regions_ref, rr_ref, hot_ref,
           xw_ref, cw_ref, normed_ref, nbf_ref, inv_ref, proj_ref, aw_ref, att_ref, ga_ref, gp_ref, tr_ref,
           po_ref, pg_ref, ro_ref, rg_ref,
           gb_ref, r0_ref, s0_ref, r1_ref, s1_ref, r2_ref, s2_ref, r3_ref,
           load_sem, halo_send, halo_recv, region_send, region_recv, rs_send, rs_recv):
    lat, lon = lax.axis_index("lat"), lax.axis_index("lon")
    core = lon % 2
    at = (lon // 8 * 2 + lat // 4, lon // 2 % 4, lat % 4)

    def near(step):
        return ((lat + step[0] + 8) % 8, (lon + step[1] + 16) % 16)

    def chip(x, y, z, c):
        return (x % 2 * 4 + z, (x // 2 * 4 + y) * 2 + c)

    def along(axis, k):
        there = list(at)
        there[axis] = (at[axis] + k) % 4
        return chip(*there, core)

    partners = [near(step) for _, _, _, step in SECTIONS[1:]]
    partners += [chip(*at, 1 - core)]
    partners += [along(axis, k) for axis in range(3) for k in (1, 2, 3)]
    barrier = pltpu.get_barrier_semaphore()
    for partner in partners:
        pl.semaphore_signal(barrier, inc=1, device_id=partner, device_id_type=MESH)

    loads = [
        pltpu.make_async_copy(src, dst, load_sem.at[n])
        for n, (src, dst) in enumerate((
            (pack_hbm, pack_ref), (x_hbm, x_ref), (cot_hbm, cot_ref), (window_hbm, window_ref), (w_hbm, w_ref),
            (wo_hbm, wo_ref), (unwindow_hbm, unwindow_ref), (mix_hbm, mix_ref), (unpack_hbm, unpack_ref),
        ))
    ]
    for load in loads:
        load.start()

    def halo(which, src, dst, back):
        made = []
        for n, (_, row, rows, step) in enumerate(SECTIONS[1:]):
            to = near((-step[0], -step[1])) if back else near(step)
            made.append(pltpu.make_async_remote_copy(
                src_ref=src.at[pl.ds(row, rows)], dst_ref=dst.at[pl.ds(row, rows)],
                send_sem=halo_send.at[which, n], recv_sem=halo_recv.at[which, n],
                device_id=to, device_id_type=MESH))
        return made

    loads[0].wait()
    loads[1].wait()
    px_ref[...] = dot(pack_ref[...], x_ref[...]).astype(BF)
    pl.semaphore_wait(barrier, len(partners))
    go_x = halo(0, px_ref, rx_ref, False)
    for copy in go_x:
        copy.start()
    go_regions = [
        pltpu.make_async_remote_copy(
            src_ref=region_ref.at[pl.ds(2, 2)], dst_ref=regions_ref.at[n],
            send_sem=region_send.at[n], recv_sem=region_recv.at[n],
            device_id=near(step), device_id_type=MESH)
        for n, step in enumerate(((-1, 0), (-1, -1)))
    ]
    for copy in go_regions:
        copy.start()
    loads[2].wait()
    pc_ref[...] = dot(pack_ref[...], cot_ref[...]).astype(BF)
    go_cot = halo(1, pc_ref, rc_ref, False)
    for copy in go_cot:
        copy.start()
    rx_ref[pl.ds(0, 224), :] = px_ref[pl.ds(0, 224), :]
    rc_ref[pl.ds(0, 224), :] = pc_ref[pl.ds(0, 224), :]

    for copy in go_regions:
        copy.wait_recv()
    rr_ref[...] = jnp.zeros_like(rr_ref)
    for n in range(6):
        piece = region_ref[n % 2] if n < 2 else regions_ref[n // 2 - 1, n % 2]
        rr_ref[pl.ds(8 * n, 6), pl.ds(0, 24)] = piece.astype(F32)
    picked = dot(row_ref[...], rr_ref[...].astype(BF)) * column_ref[...].astype(F32)
    value = dot(picked.astype(BF), jnp.ones((128, 128), BF))
    lanes = lax.broadcasted_iota(jnp.int32, (TOKENS, 128), 1).astype(F32)
    hot_ref[...] = jnp.where(value == lanes, 1.0, 0.0).astype(BF)

    gain = gain_ref[...]
    loads[3].wait()
    for copy in go_x:
        copy.wait_recv()
    for w in range(4):
        rows = pl.ds(w * SPAN, SPAN)
        x = dot(window_ref[rows, :], rx_ref[...])
        xw_ref[rows, :] = x.astype(BF)
        centered = x - jnp.mean(x, -1, keepdims=True)
        var = jnp.mean(centered * centered, -1, keepdims=True)
        inv = lax.rsqrt(var + 1e-5)
        normed = centered * inv
        normed_ref[rows, :] = normed
        inv_ref[rows, :] = inv
        nbf_ref[rows, :] = (normed * gain).astype(BF)
    loads[4].wait()
    for c in range(6):
        cols = pl.ds(c * 256, 256)
        proj_ref[:, cols] = dot(nbf_ref[...], w_ref[:, cols]).astype(BF)

    lane = lax.broadcasted_iota(jnp.int32, (1, 128), 1)
    masks = [jnp.where((lane < 64) == (h == 0), 1.0, 0.0).astype(BF) for h in range(2)]
    eighths = [(m * 0.125).astype(BF) for m in masks]

    def forward(p, _):
        col = pl.multiple_of(p * 128, 128)
        for w in range(4):
            rows = pl.ds(w * SPAN, SPAN)
            q2 = proj_ref[rows, pl.ds(col, 128)]
            k2 = proj_ref[rows, pl.ds(pl.multiple_of(512 + col, 128), 128)]
            v2 = proj_ref[rows, pl.ds(pl.multiple_of(1024 + col, 128), 128)]
            hot = hot_ref[rows, :]
            qx = jnp.concatenate([q2, hot * jnp.array(-1e30, BF)], 1)
            off = (1.0 - hot.astype(F32)).astype(BF)
            att = []
            for h in range(2):
                s = dot(qx, jnp.concatenate([k2 * eighths[h], off], 1), NT)
                e = jnp.exp(s - jnp.max(s, -1, keepdims=True))
                a = e * (1.0 / jnp.sum(e, -1, keepdims=True))
                aw_ref[p, w, h] = a
                att.append(dot(a.astype(BF), v2))
            att_ref[rows, pl.ds(col, 128)] = jnp.where(lane < 64, att[0], att[1]).astype(BF)
        return 0

    lax.fori_loop(0, 4, forward, 0)

    loads[5].wait()
    for w in range(4):
        rows = pl.ds(w * SPAN, SPAN)
        branch = dot(att_ref[rows, :], wo_ref[...])
        xw_ref[rows, :] = (xw_ref[rows, :].astype(F32) + branch).astype(BF)
    loads[6].wait()
    po_ref[...] = dot(unwindow_ref[...], xw_ref[...]).astype(BF)
    go_out = halo(2, po_ref, ro_ref, True)
    for copy in go_out:
        copy.start()
    ro_ref[pl.ds(0, 224), :] = po_ref[pl.ds(0, 224), :]

    for copy in go_cot:
        copy.wait_recv()
    cw_ref[...] = dot(window_ref[...], rc_ref[...]).astype(BF)
    for c in range(2):
        ga_ref[:, pl.ds(c * 256, 256)] = dot(cw_ref[...], wo_ref[pl.ds(c * 256, 256), :], NT).astype(BF)
    eye = eye_ref[...]
    eye128 = eye_ref[:128, :128]

    def backward(p, _):
        col = pl.multiple_of(p * 128, 128)
        for w in range(4):
            rows = pl.ds(w * SPAN, SPAN)
            q2 = proj_ref[rows, pl.ds(col, 128)]
            k2 = proj_ref[rows, pl.ds(pl.multiple_of(512 + col, 128), 128)]
            v2 = proj_ref[rows, pl.ds(pl.multiple_of(1024 + col, 128), 128)]
            g2 = ga_ref[rows, pl.ds(col, 128)]
            qt = dot(eye128, q2 * jnp.array(0.125, BF), NT).astype(BF)
            gt = dot(eye128, g2, NT).astype(BF)
            gq = None
            gkt = []
            gvt = []
            for h in range(2):
                a = aw_ref[p, w, h]
                gw = dot(g2, v2 * masks[h], NT)
                prod = gw * a
                inner = jnp.sum(prod, -1, keepdims=True)
                ds = (prod - a * inner).astype(BF)
                part = dot(ds, k2 * eighths[h])
                gq = part if gq is None else gq + part
                gkt.append(dot(qt[64 * h:64 * h + 64], ds))
                gvt.append(dot(gt[64 * h:64 * h + 64], a.astype(BF)))
            gk = dot(eye, jnp.concatenate(gkt, 0).astype(BF), NT)
            gv = dot(eye, jnp.concatenate(gvt, 0).astype(BF), NT)
            gp_ref[rows, pl.ds(col, 128)] = gq.astype(BF)
            gp_ref[rows, pl.ds(pl.multiple_of(512 + col, 128), 128)] = gk.astype(BF)
            gp_ref[rows, pl.ds(pl.multiple_of(1024 + col, 128), 128)] = gv.astype(BF)
        return 0

    lax.fori_loop(0, 4, backward, 0)

    tr_ref[0] = nbf_ref[...].T
    tr_ref[1] = att_ref[...].T
    loads[7].wait()
    for m in range(4):
        gm = dot(tr_ref[0], gp_ref[:, pl.ds(384 * m, 384)]).astype(BF)
        om = dot(tr_ref[1], cw_ref[:, pl.ds(128 * m, 128)]).astype(BF)
        mixed = dot(jnp.concatenate([gm, om], 1), mix_ref[...]).astype(BF)
        for jj in range(4):
            j = 4 * m + jj
            for i in range(8):
                gb_ref[j % 2, j // 8 * 2 + i // 4, j // 2 % 4, i % 4] = mixed[64 * i:64 * i + 64, 128 * jj:128 * jj + 128]

    def swap(n):
        return pltpu.make_async_remote_copy(
            src_ref=gb_ref.at[1 - core, n], dst_ref=r0_ref.at[n],
            send_sem=rs_send.at[n], recv_sem=rs_recv.at[n],
            device_id=chip(*at, 1 - core), device_id_type=MESH)

    swaps = [swap(n) for n in range(4)]
    for copy in swaps:
        copy.start()

    for w in range(4):
        rows = pl.ds(w * SPAN, SPAN)
        gh = dot(gp_ref[rows, :], w_ref[...], NT) * gain
        normed = normed_ref[rows, :]
        gs = inv_ref[rows, :] * (gh - jnp.mean(gh, -1, keepdims=True)
                                 - normed * jnp.mean(gh * normed, -1, keepdims=True))
        nbf_ref[rows, :] = gs.astype(BF)
    pg_ref[...] = dot(unwindow_ref[...], nbf_ref[...]).astype(BF)
    go_grad = halo(3, pg_ref, rg_ref, True)
    for copy in go_grad:
        copy.start()
    rg_ref[pl.ds(0, 224), :] = pg_ref[pl.ds(0, 224), :]

    for n in range(4):
        swaps[n].wait_recv()

        def add(y, _, n=n):
            s0_ref[n, y] = (gb_ref[core, n, y].astype(F32) + r0_ref[n, y].astype(F32)).astype(BF)
            return 0

        lax.fori_loop(0, 4, add, 0)

    def scatter(stage, s, k, src, dst):
        n = 4 + (stage * 4 + s) * 3 + k - 1
        return pltpu.make_async_remote_copy(
            src_ref=src, dst_ref=dst, send_sem=rs_send.at[n], recv_sem=rs_recv.at[n],
            device_id=along(ORDERS[s][stage], k), device_id_type=MESH)

    def quarter(s, axis, index):
        rows = pl.ds(16 * s, 16)
        if axis == 0:
            return s0_ref.at[index, :, :, rows]
        if axis == 1:
            return s0_ref.at[:, index, :, rows]
        return s0_ref.at[:, :, index, rows]

    sent = []
    first = [[scatter(0, s, k, quarter(s, ORDERS[s][0], (at[ORDERS[s][0]] + k) % 4), r1_ref.at[s, k - 1])
              for k in (1, 2, 3)] for s in range(4)]
    for k in range(3):
        for s in range(4):
            first[s][k].start()
    loads[8].wait()
    for copy in go_out:
        copy.wait_recv()
    result_ref[...] = dot(unpack_ref[...], ro_ref[...]).astype(BF)

    second = []
    for s in range(4):
        axis, nxt = ORDERS[s][0], ORDERS[s][1]
        for copy in first[s]:
            copy.wait_recv()
        total = quarter(s, axis, at[axis])[...].astype(F32)
        for k in range(3):
            total = total + r1_ref[s, k].astype(F32)
        s1_ref[s] = total
        copies = []
        for k in (1, 2, 3):
            there = (at[nxt] + k) % 4
            left = [a for a in range(3) if a != axis]
            src = s1_ref.at[s, there] if left[0] == nxt else s1_ref.at[s, :, there]
            copies.append(scatter(1, s, k, src, r2_ref.at[s, k - 1]))
            copies[-1].start()
        second.append(copies)
    third = []
    for s in range(4):
        axis, nxt, last = ORDERS[s]
        for copy in second[s]:
            copy.wait_recv()
        left = [a for a in range(3) if a != axis]
        total = s1_ref[s, at[nxt]] if left[0] == nxt else s1_ref[s, :, at[nxt]]
        for k in range(3):
            total = total + r2_ref[s, k]
        s2_ref[s] = total
        copies = []
        for k in (1, 2, 3):
            copies.append(scatter(2, s, k, s2_ref.at[s, (at[last] + k) % 4], r3_ref.at[s, k - 1]))
            copies[-1].start()
        third.append(copies)
    for copy in go_grad:
        copy.wait_recv()
    grad_ref[...] = (cot_ref[...].astype(F32) + dot(unpack_ref[...], rg_ref[...])).astype(BF)
    for s in range(4):
        for copy in third[s]:
            copy.wait_recv()
        total = s2_ref[s, at[ORDERS[s][2]]]
        for k in range(3):
            total = total + r3_ref[s, k]
        owned_ref[pl.ds(16 * s, 16), :] = total

    started = go_x + go_regions + go_cot + go_out + go_grad + swaps
    for copies in first + second + third:
        started += copies
    for copy in started:
        copy.wait_send()


def on_device(tokens, cotangent, region_ids, norm_gain, qkv_weight, out_weight):
    pack, window, unpack, unwindow, row_of, column_of, mix, eye = constants()
    vm = pl.BlockSpec(memory_space=pltpu.VMEM)
    hbm = pl.BlockSpec(memory_space=pl.ANY)

    def bf(*shape):
        return pltpu.VMEM(shape, BF)

    def f32(*shape):
        return pltpu.VMEM(shape, F32)

    result, grad, owned = pl.pallas_call(
        kernel,
        out_shape=(
            jax.ShapeDtypeStruct((TOKENS, WIDTH), BF),
            jax.ShapeDtypeStruct((TOKENS, WIDTH), BF),
            jax.ShapeDtypeStruct((64, 128), F32),
        ),
        in_specs=[hbm, hbm, vm, vm, hbm, hbm, hbm, hbm, hbm, hbm, vm, vm, hbm, vm],
        out_specs=(vm, vm, vm),
        scratch_shapes=[
            bf(TOKENS, WIDTH), bf(TOKENS, WIDTH), bf(WIDTH, 3 * WIDTH), bf(WIDTH, WIDTH),
            bf(PACKED, TOKENS), bf(TOKENS, PACKED), bf(TOKENS, PACKED), bf(PACKED, TOKENS), bf(512, 512),
            bf(PACKED, WIDTH), bf(PACKED, WIDTH), bf(PACKED, WIDTH), bf(PACKED, WIDTH),
            pltpu.VMEM((2, 2, 6, 24), jnp.int32), f32(48, 128), bf(TOKENS, 128),
            bf(TOKENS, WIDTH), bf(TOKENS, WIDTH), f32(TOKENS, WIDTH), bf(TOKENS, WIDTH), f32(TOKENS, 1),
            bf(TOKENS, 3 * WIDTH), f32(4, 4, 2, SPAN, SPAN), bf(TOKENS, WIDTH), bf(TOKENS, WIDTH),
            bf(TOKENS, 3 * WIDTH), bf(2, WIDTH, TOKENS),
            bf(PACKED, WIDTH), bf(PACKED, WIDTH), bf(PACKED, WIDTH), bf(PACKED, WIDTH),
            bf(2, 4, 4, 4, 64, 128), bf(4, 4, 4, 64, 128), bf(4, 4, 4, 64, 128),
            bf(4, 3, 4, 4, 16, 128), f32(4, 4, 4, 16, 128),
            f32(4, 3, 4, 16, 128), f32(4, 4, 16, 128), f32(4, 3, 16, 128),
            pltpu.SemaphoreType.DMA((9,)),
            pltpu.SemaphoreType.DMA((4, 6)), pltpu.SemaphoreType.DMA((4, 6)),
            pltpu.SemaphoreType.DMA((2,)), pltpu.SemaphoreType.DMA((2,)),
            pltpu.SemaphoreType.DMA((40,)), pltpu.SemaphoreType.DMA((40,)),
        ],
        compiler_params=pltpu.CompilerParams(
            vmem_limit_bytes=56 << 20, collective_id=0, has_side_effects=True),
        cost_estimate=pl.CostEstimate(flops=6 * 10**9, bytes_accessed=10**7, transcendentals=0),
    )(
        tokens.reshape(TOKENS, WIDTH), cotangent.reshape(TOKENS, WIDTH), region_ids, norm_gain.reshape(1, WIDTH),
        qkv_weight, out_weight, pack, window, unpack, unwindow, row_of, column_of, mix, eye,
    )
    return (result.reshape(tokens.shape), grad.reshape(tokens.shape), owned[:, :96], owned[:, 96:])


def solution(mesh):
    placed = (
        P(None, "lat", "lon", None),
        P(None, "lat", "lon", None),
        P(None, "lat", "lon"),
        P(),
        P(),
        P(),
    )
    return jax.shard_map(
        on_device,
        mesh=mesh,
        in_specs=placed,
        out_specs=(
            P(None, "lat", "lon", None),
            P(None, "lat", "lon", None),
            P("lat", "lon"),
            P("lat", "lon"),
        ),
        check_vma=False,
    )
```

```python
import functools

import jax
import jax.numpy as jnp
import numpy as np
from jax import lax
from jax.experimental import pallas as pl
from jax.experimental.pallas import tpu as pltpu
from jax.sharding import PartitionSpec as P

SPAN = 144
TOKENS = 576
PACKED = 640
WIDTH = 512
NN = (((1,), (0,)), ((), ()))
NT = (((1,), (1,)), ((), ()))
BF = jnp.bfloat16
F32 = jnp.float32
MESH = pl.DeviceIdType.MESH

SECTIONS = (
    ("local", 0, 224, (0, 0)),
    ("lat+", 224, 112, (1, 0)),
    ("lat-", 336, 112, (-1, 0)),
    ("lon+", 448, 48, (0, 1)),
    ("lon-", 496, 48, (0, -1)),
    ("diag+", 544, 48, (1, 1)),
    ("diag-", 592, 48, (-1, -1)),
)
GOES = {
    (0, 0, 1): "local", (0, 1, 1): "lat+", (0, 0, 0): "local",
    (0, 0, 2): "lon+", (0, 1, 0): "lat+", (0, 1, 2): "diag+",
    (1, 1, 1): "local", (1, 0, 1): "lat-", (1, 1, 2): "local",
    (1, 1, 0): "lon-", (1, 0, 2): "lat-", (1, 0, 0): "diag-",
}
ORDERS = ((2, 1, 0), (1, 0, 2), (0, 2, 1), (0, 1, 2))


def constants():
    pack = np.zeros((PACKED, TOKENS), np.float32)
    window = np.zeros((TOKENS, PACKED), np.float32)
    first = {name: row for name, row, _, _ in SECTIONS}
    filled = dict.fromkeys(first, 0)
    for t in range(TOKENS):
        l, a, o = t // 144, t // 24 % 6, t % 24
        level = (l + 1) % 4
        piece = 0 if o < 6 else 1 if o < 18 else 2
        name = GOES[level // 2, a // 3, piece]
        row = first[name] + filled[name]
        filled[name] += 1
        pack[row, t] = 1
        column = (o + 6) % 12
        which = level // 2 * 2 + (0 if piece == 1 else 1)
        window[which * SPAN + level % 2 * 72 + (a + 3) % 6 * 12 + column, row] = 1
    row_of = np.zeros((TOKENS, 144), np.float32)
    column_of = np.zeros((TOKENS, 128), np.float32)
    for which in range(4):
        source = (0, 0, 1, 2)[which]
        for n in range(SPAN):
            t = which * SPAN + n
            row_of[t, (source * 6 + n // 12 % 6) * 8 + n // 72 + (2 if source else 0)] = 1
            column_of[t, n % 12 + (12 if which % 2 == 0 else 0)] = 1
    made = pack, window, pack.T, window.T, row_of, column_of
    return [jnp.asarray(m, BF) for m in made]


def dot(a, b, dims=NN):
    return lax.dot_general(a, b, dims, preferred_element_type=F32)


def kernel(x_hbm, cot_hbm, region_ref, gain_ref, w_hbm, wo_hbm,
           pack_hbm, window_hbm, unpack_hbm, unwindow_hbm, row_ref, column_ref,
           result_ref, grad_ref, gq_ref, go_ref,
           x_ref, cot_ref, w_ref, wo_ref, pack_ref, window_ref, unpack_ref, unwindow_ref,
           px_ref, pc_ref, rx_ref, rc_ref, regions_ref, rr_ref, hot_ref,
           xw_ref, cw_ref, normed_ref, nbf_ref, inv_ref, proj_ref, aw_ref, att_ref, ga_ref, gp_ref, tr_ref,
           po_ref, pg_ref, ro_ref, rg_ref,
           gw_ref, r0_ref, s0_ref, r1_ref, s1_ref, r2_ref, s2_ref, r3_ref, fin_ref, all_ref,
           load_sem, halo_send, halo_recv, region_send, region_recv, rs_send, rs_recv):
    lat, lon = lax.axis_index("lat"), lax.axis_index("lon")
    core = lon % 2
    at = (lon // 8 * 2 + lat // 4, lon // 2 % 4, lat % 4)

    def near(step):
        return ((lat + step[0] + 8) % 8, (lon + step[1] + 16) % 16)

    def chip(x, y, z, c):
        return (x % 2 * 4 + z, (x // 2 * 4 + y) * 2 + c)

    def along(axis, k):
        there = list(at)
        there[axis] = (at[axis] + k) % 4
        return chip(*there, core)

    partners = [near(step) for _, _, _, step in SECTIONS[1:]]
    partners += [chip(*at, 1 - core)]
    partners += [along(axis, k) for axis in range(3) for k in (1, 2, 3)]
    loads = [
        pltpu.make_async_copy(src, dst, load_sem.at[n])
        for n, (src, dst) in enumerate((
            (pack_hbm, pack_ref), (x_hbm, x_ref), (cot_hbm, cot_ref), (window_hbm, window_ref), (w_hbm, w_ref),
            (wo_hbm, wo_ref), (unwindow_hbm, unwindow_ref), (unpack_hbm, unpack_ref),
        ))
    ]
    for load in loads:
        load.start()

    barrier = pltpu.get_barrier_semaphore()
    for partner in partners:
        pl.semaphore_signal(barrier, inc=1, device_id=partner, device_id_type=MESH)

    def halo(which, src, dst, back):
        made = []
        for n, (_, row, rows, step) in enumerate(SECTIONS[1:]):
            to = near((-step[0], -step[1])) if back else near(step)
            made.append(pltpu.make_async_remote_copy(
                src_ref=src.at[pl.ds(row, rows)], dst_ref=dst.at[pl.ds(row, rows)],
                send_sem=halo_send.at[which, n], recv_sem=halo_recv.at[which, n],
                device_id=to, device_id_type=MESH))
        return made

    loads[0].wait()
    loads[1].wait()
    px_ref[...] = dot(pack_ref[...], x_ref[...]).astype(BF)
    pl.semaphore_wait(barrier, len(partners))
    go_x = halo(0, px_ref, rx_ref, False)
    for copy in go_x:
        copy.start()
    go_regions = [
        pltpu.make_async_remote_copy(
            src_ref=region_ref, dst_ref=regions_ref.at[n],
            send_sem=region_send.at[n], recv_sem=region_recv.at[n],
            device_id=near(step), device_id_type=MESH)
        for n, step in enumerate(((-1, 0), (-1, -1)))
    ]
    for copy in go_regions:
        copy.start()
    loads[2].wait()
    pc_ref[...] = dot(pack_ref[...], cot_ref[...]).astype(BF)
    go_cot = halo(1, pc_ref, rc_ref, False)
    for copy in go_cot:
        copy.start()
    rx_ref[pl.ds(0, 224), :] = px_ref[pl.ds(0, 224), :]
    rc_ref[pl.ds(0, 224), :] = pc_ref[pl.ds(0, 224), :]

    for copy in go_regions:
        copy.wait_recv()
    rr_ref[...] = jnp.zeros_like(rr_ref)
    for n in range(18):
        piece = region_ref[n % 6] if n < 6 else regions_ref[n // 6 - 1, n % 6]
        rr_ref[pl.ds(8 * n, 4), pl.ds(0, 24)] = piece.astype(F32)
    picked = dot(row_ref[...], rr_ref[...].astype(BF)) * column_ref[...].astype(F32)
    value = dot(picked.astype(BF), jnp.ones((128, 128), BF))
    lanes = lax.broadcasted_iota(jnp.int32, (TOKENS, 128), 1).astype(F32)
    hot_ref[...] = jnp.where(value == lanes, 1.0, 0.0).astype(BF)

    gain = gain_ref[...]
    loads[3].wait()
    for copy in go_x:
        copy.wait_recv()
    for w in range(4):
        rows = pl.ds(w * SPAN, SPAN)
        x = dot(window_ref[rows, :], rx_ref[...])
        xw_ref[rows, :] = x.astype(BF)
        centered = x - jnp.mean(x, -1, keepdims=True)
        var = jnp.mean(centered * centered, -1, keepdims=True)
        inv = lax.rsqrt(var + 1e-5)
        normed = centered * inv
        normed_ref[rows, :] = normed
        inv_ref[rows, :] = inv
        nbf_ref[rows, :] = (normed * gain).astype(BF)
    loads[4].wait()
    for c in range(6):
        cols = pl.ds(c * 256, 256)
        proj_ref[:, cols] = dot(nbf_ref[...], w_ref[:, cols]).astype(BF)

    lane = lax.broadcasted_iota(jnp.int32, (1, 128), 1)
    masks = [jnp.where((lane < 64) == (h == 0), 1.0, 0.0).astype(BF) for h in range(2)]
    eighths = [(m * 0.125).astype(BF) for m in masks]

    def forward(p):
        col = p * 128
        for w in range(4):
            rows = pl.ds(w * SPAN, SPAN)
            q2 = proj_ref[rows, pl.ds(col, 128)]
            k2 = proj_ref[rows, pl.ds(512 + col, 128)]
            v2 = proj_ref[rows, pl.ds(1024 + col, 128)]
            hot = hot_ref[rows, :]
            qx = jnp.concatenate([q2, hot * jnp.array(-1e30, BF)], 1)
            off = (1.0 - hot.astype(F32)).astype(BF)
            att = []
            for h in range(2):
                s = dot(qx, jnp.concatenate([k2 * eighths[h], off], 1), NT)
                e = jnp.exp(s - jnp.max(s, -1, keepdims=True))
                a = e * (1.0 / jnp.sum(e, -1, keepdims=True))
                aw_ref[p, w, h] = a
                att.append(dot(a.astype(BF), v2))
            att_ref[rows, pl.ds(col, 128)] = jnp.where(lane < 64, att[0], att[1]).astype(BF)

    for p in range(4):
        forward(p)

    loads[5].wait()
    for w in range(4):
        rows = pl.ds(w * SPAN, SPAN)
        branch = dot(att_ref[rows, :], wo_ref[...])
        xw_ref[rows, :] = (xw_ref[rows, :].astype(F32) + branch).astype(BF)
    loads[6].wait()
    po_ref[...] = dot(unwindow_ref[...], xw_ref[...]).astype(BF)
    go_out = halo(2, po_ref, ro_ref, True)
    for copy in go_out:
        copy.start()
    ro_ref[pl.ds(0, 224), :] = po_ref[pl.ds(0, 224), :]

    for copy in go_cot:
        copy.wait_recv()
    cw_ref[...] = dot(window_ref[...], rc_ref[...]).astype(BF)
    for c in range(2):
        ga_ref[:, pl.ds(c * 256, 256)] = dot(cw_ref[...], wo_ref[pl.ds(c * 256, 256), :], NT).astype(BF)
    def backward(p):
        col = p * 128
        for w in range(4):
            rows = pl.ds(w * SPAN, SPAN)
            q2 = proj_ref[rows, pl.ds(col, 128)]
            k2 = proj_ref[rows, pl.ds(512 + col, 128)]
            v2 = proj_ref[rows, pl.ds(1024 + col, 128)]
            g2 = ga_ref[rows, pl.ds(col, 128)]
            qt = (q2 * jnp.array(0.125, BF)).T
            gt = g2.T
            gq = None
            gkt = []
            gvt = []
            for h in range(2):
                a = aw_ref[p, w, h]
                gw = dot(g2, v2 * masks[h], NT)
                prod = gw * a
                inner = jnp.sum(prod, -1, keepdims=True)
                ds = (prod - a * inner).astype(BF)
                part = dot(ds, k2 * eighths[h])
                gq = part if gq is None else gq + part
                gkt.append(dot(qt[64 * h:64 * h + 64], ds))
                gvt.append(dot(gt[64 * h:64 * h + 64], a.astype(BF)))
            gp_ref[rows, pl.ds(col, 128)] = gq.astype(BF)
            gp_ref[rows, pl.ds(512 + col, 128)] = jnp.concatenate(gkt, 0).astype(BF).T
            gp_ref[rows, pl.ds(1024 + col, 128)] = jnp.concatenate(gvt, 0).astype(BF).T

    def swap(first, count):
        return pltpu.make_async_remote_copy(
            src_ref=gw_ref.at[pl.ds(first, count), :, 1 - core], dst_ref=r0_ref.at[pl.ds(first, count)],
            send_sem=rs_send.at[first], recv_sem=rs_recv.at[first],
            device_id=chip(*at, 1 - core), device_id_type=MESH)

    tr_ref[0] = nbf_ref[...].T
    tr_ref[1] = att_ref[...].T
    for m in range(4):
        block = pltpu.roll(dot(tr_ref[1], cw_ref[:, pl.ds(128 * m, 128)]), 64, 1)
        gw_ref[12 + m] = block.reshape(8, 2, 32, 128)
    swaps = [swap(12, 4)]
    swaps[0].start()
    for p in range(4):
        backward(p)
        pieces = jnp.concatenate([gp_ref[:, pl.ds(512 * t + 128 * p, 128)] for t in range(3)], 1)
        grads = dot(tr_ref[0], pieces)
        for t in range(3):
            gw_ref[4 * t + p] = grads[:, 128 * t:128 * t + 128].reshape(8, 2, 32, 128)
            swaps.append(swap(4 * t + p, 1))
            swaps[-1].start()

    for w in range(4):
        rows = pl.ds(w * SPAN, SPAN)
        gh = dot(gp_ref[rows, :], w_ref[...], NT) * gain
        normed = normed_ref[rows, :]
        gs = inv_ref[rows, :] * (gh - jnp.mean(gh, -1, keepdims=True)
                                 - normed * jnp.mean(gh * normed, -1, keepdims=True))
        nbf_ref[rows, :] = gs.astype(BF)
    for copy in swaps:
        copy.wait_recv()
    for m in range(4):
        whole = [gw_ref[b, :, core] + r0_ref[b] for b in (3 * m, 3 * m + 1, 3 * m + 2, 12 + m)]
        left = lane < 64
        for n, parts in ((0, (whole[0], jnp.where(left, whole[1], whole[3]))),
                         (1, (whole[2], jnp.where(left, whole[3], whole[1])))):
            for half in range(2):
                for x_lo in range(2):
                    s0_ref[m // 2 * 2 + x_lo, m % 2 * 2 + n, :, half] = parts[half][4 * x_lo:4 * x_lo + 4].astype(BF)

    def scatter(stage, s, k, src, dst):
        n = 16 + (stage * 4 + s) * 3 + k - 1
        return pltpu.make_async_remote_copy(
            src_ref=src, dst_ref=dst, send_sem=rs_send.at[n], recv_sem=rs_recv.at[n],
            device_id=along(ORDERS[s][stage], k), device_id_type=MESH)

    def quarter(s, axis, index):
        half, rows = s // 2, pl.ds(s % 2 * 16, 16)
        if axis == 0:
            return s0_ref.at[index, :, :, half, rows]
        if axis == 1:
            return s0_ref.at[:, index, :, half, rows]
        return s0_ref.at[:, :, index, half, rows]

    first = [[scatter(0, s, k, quarter(s, ORDERS[s][0], (at[ORDERS[s][0]] + k) % 4), r1_ref.at[s, k - 1])
              for k in (1, 2, 3)] for s in range(4)]
    for k in range(3):
        for s in range(4):
            first[s][k].start()
    pg_ref[...] = dot(unwindow_ref[...], nbf_ref[...]).astype(BF)
    go_grad = halo(3, pg_ref, rg_ref, True)
    for copy in go_grad:
        copy.start()
    rg_ref[pl.ds(0, 224), :] = pg_ref[pl.ds(0, 224), :]

    loads[7].wait()
    for copy in go_out:
        copy.wait_recv()
    result_ref[...] = dot(unpack_ref[...], ro_ref[...]).astype(BF)

    second = []
    for s in range(4):
        axis, nxt = ORDERS[s][0], ORDERS[s][1]
        for copy in first[s]:
            copy.wait_recv()
        total = quarter(s, axis, at[axis])[...].astype(F32)
        for k in range(3):
            total = total + r1_ref[s, k].astype(F32)
        s1_ref[s] = total
        copies = []
        for k in (1, 2, 3):
            there = (at[nxt] + k) % 4
            left = [a for a in range(3) if a != axis]
            src = s1_ref.at[s, there] if left[0] == nxt else s1_ref.at[s, :, there]
            copies.append(scatter(1, s, k, src, r2_ref.at[s, k - 1]))
            copies[-1].start()
        second.append(copies)
    third = []
    for s in range(4):
        axis, nxt, last = ORDERS[s]
        for copy in second[s]:
            copy.wait_recv()
        left = [a for a in range(3) if a != axis]
        total = s1_ref[s, at[nxt]] if left[0] == nxt else s1_ref[s, :, at[nxt]]
        for k in range(3):
            total = total + r2_ref[s, k]
        s2_ref[s] = total
        copies = []
        for k in (1, 2, 3):
            copies.append(scatter(2, s, k, s2_ref.at[s, (at[last] + k) % 4], r3_ref.at[s, k - 1]))
            copies[-1].start()
        third.append(copies)
    for copy in go_grad:
        copy.wait_recv()
    grad_ref[...] = (cot_ref[...].astype(F32) + dot(unpack_ref[...], rg_ref[...])).astype(BF)
    for s in range(4):
        for copy in third[s]:
            copy.wait_recv()
        total = s2_ref[s, at[ORDERS[s][2]]]
        for k in range(3):
            total = total + r3_ref[s, k]
        fin_ref[pl.ds(s % 2 * 16, 16), pl.ds(s // 2 * 128, 128)] = total
    last = pltpu.make_async_remote_copy(
        src_ref=fin_ref, dst_ref=all_ref.at[core], send_sem=rs_send.at[52], recv_sem=rs_recv.at[52],
        device_id=chip(*at, 1 - core), device_id_type=MESH)
    last.start()
    all_ref[core] = fin_ref[...]
    last.wait_recv()
    whole = all_ref[...].reshape(64, 256)
    whole = jnp.where(at[1] % 2 == 1, pltpu.roll(whole, 64, 1), whole)
    gq_ref[...] = jnp.where(core == 1, pltpu.roll(whole, 160, 1), whole)[:, :96]
    outs = whole[:, 128:]
    go_ref[...] = jnp.where(core == 1, pltpu.roll(outs, 32, 1), pltpu.roll(outs, 64, 1)).T[:32]

    started = go_x + go_regions + go_cot + go_out + go_grad + swaps + [last]
    for copies in first + second + third:
        started += copies
    for copy in started:
        copy.wait_send()


def hand_over(*refs):
    copies = [pltpu.make_async_copy(refs[n], refs[4 + n], refs[8].at[n]) for n in range(4)]
    for copy in copies:
        copy.start()
    for copy in copies:
        copy.wait()


def on_device(tokens, cotangent, region_ids, norm_gain, qkv_weight, out_weight):
    pack, window, unpack, unwindow, row_of, column_of = constants()
    vm = pl.BlockSpec(memory_space=pltpu.VMEM)
    hbm = pl.BlockSpec(memory_space=pl.ANY)

    def bf(*shape):
        return pltpu.VMEM(shape, BF)

    def f32(*shape):
        return pltpu.VMEM(shape, F32)

    sums = pl.pallas_call(
        kernel,
        out_shape=(
            jax.ShapeDtypeStruct((TOKENS, WIDTH), BF),
            jax.ShapeDtypeStruct((TOKENS, WIDTH), BF),
            jax.ShapeDtypeStruct((64, 96), F32),
            jax.ShapeDtypeStruct((32, 64), F32),
        ),
        in_specs=[hbm, hbm, vm, vm, hbm, hbm, hbm, hbm, hbm, hbm, vm, vm],
        out_specs=(vm, vm, vm, vm),
        scratch_shapes=[
            bf(TOKENS, WIDTH), bf(TOKENS, WIDTH), bf(WIDTH, 3 * WIDTH), bf(WIDTH, WIDTH),
            bf(PACKED, TOKENS), bf(TOKENS, PACKED), bf(TOKENS, PACKED), bf(PACKED, TOKENS),
            bf(PACKED, WIDTH), bf(PACKED, WIDTH), bf(PACKED, WIDTH), bf(PACKED, WIDTH),
            pltpu.VMEM((2, 6, 4, 24), jnp.int32), f32(144, 128), bf(TOKENS, 128),
            bf(TOKENS, WIDTH), bf(TOKENS, WIDTH), f32(TOKENS, WIDTH), bf(TOKENS, WIDTH), f32(TOKENS, 1),
            bf(TOKENS, 3 * WIDTH), f32(4, 4, 2, SPAN, SPAN), bf(TOKENS, WIDTH), bf(TOKENS, WIDTH),
            bf(TOKENS, 3 * WIDTH), bf(2, WIDTH, TOKENS),
            bf(PACKED, WIDTH), bf(PACKED, WIDTH), bf(PACKED, WIDTH), bf(PACKED, WIDTH),
            f32(16, 8, 2, 32, 128), f32(16, 8, 32, 128), bf(4, 4, 4, 2, 32, 128),
            bf(4, 3, 4, 4, 16, 128), f32(4, 4, 4, 16, 128),
            f32(4, 3, 4, 16, 128), f32(4, 4, 16, 128), f32(4, 3, 16, 128), f32(32, 256), f32(2, 32, 256),
            pltpu.SemaphoreType.DMA((8,)),
            pltpu.SemaphoreType.DMA((4, 6)), pltpu.SemaphoreType.DMA((4, 6)),
            pltpu.SemaphoreType.DMA((2,)), pltpu.SemaphoreType.DMA((2,)),
            pltpu.SemaphoreType.DMA((53,)), pltpu.SemaphoreType.DMA((53,)),
        ],
        compiler_params=pltpu.CompilerParams(
            vmem_limit_bytes=56 << 20, collective_id=0, has_side_effects=True),
        cost_estimate=pl.CostEstimate(flops=6 * 10**9, bytes_accessed=10**7, transcendentals=0),
    )(
        tokens.reshape(TOKENS, WIDTH), cotangent.reshape(TOKENS, WIDTH), region_ids.transpose(1, 0, 2), norm_gain.reshape(1, WIDTH),
        qkv_weight, out_weight, pack, window, unpack, unwindow, row_of, column_of,
    )
    result, grad, gq, go = pl.pallas_call(
        hand_over,
        out_shape=tuple(jax.ShapeDtypeStruct(a.shape, a.dtype) for a in sums),
        in_specs=[hbm] * 4,
        out_specs=(hbm,) * 4,
        scratch_shapes=[pltpu.SemaphoreType.DMA((4,))],
    )(*sums)
    return (result.reshape(tokens.shape), grad.reshape(tokens.shape), gq, go.T)


def solution(mesh):
    placed = (
        P(None, "lat", "lon", None),
        P(None, "lat", "lon", None),
        P(None, "lat", "lon"),
        P(),
        P(),
        P(),
    )
    return jax.shard_map(
        on_device,
        mesh=mesh,
        in_specs=placed,
        out_specs=(
            P(None, "lat", "lon", None),
            P(None, "lat", "lon", None),
            P("lat", "lon"),
            P("lat", "lon"),
        ),
        check_vma=False,
    )
```

```python
import functools

import jax
import jax.numpy as jnp
import numpy as np
from jax import lax
from jax.experimental import pallas as pl
from jax.experimental.pallas import tpu as pltpu
from jax.sharding import PartitionSpec as P

SPAN = 144
TOKENS = 576
PACKED = 640
WIDTH = 512
NN = (((1,), (0,)), ((), ()))
NT = (((1,), (1,)), ((), ()))
BF = jnp.bfloat16
F32 = jnp.float32
MESH = pl.DeviceIdType.MESH

SECTIONS = (
    ("local", 0, 224, (0, 0)),
    ("lat+", 224, 112, (1, 0)),
    ("lat-", 336, 112, (-1, 0)),
    ("lon+", 448, 48, (0, 1)),
    ("lon-", 496, 48, (0, -1)),
    ("diag+", 544, 48, (1, 1)),
    ("diag-", 592, 48, (-1, -1)),
)
GOES = {
    (0, 0, 1): "local", (0, 1, 1): "lat+", (0, 0, 0): "local",
    (0, 0, 2): "lon+", (0, 1, 0): "lat+", (0, 1, 2): "diag+",
    (1, 1, 1): "local", (1, 0, 1): "lat-", (1, 1, 2): "local",
    (1, 1, 0): "lon-", (1, 0, 2): "lat-", (1, 0, 0): "diag-",
}
ORDERS = ((2, 1, 0), (1, 0, 2), (0, 2, 1), (0, 1, 2))


def constants():
    pack = np.zeros((PACKED, TOKENS), np.float32)
    window = np.zeros((TOKENS, PACKED), np.float32)
    first = {name: row for name, row, _, _ in SECTIONS}
    filled = dict.fromkeys(first, 0)
    for t in range(TOKENS):
        l, a, o = t // 144, t // 24 % 6, t % 24
        level = (l + 1) % 4
        piece = 0 if o < 6 else 1 if o < 18 else 2
        name = GOES[level // 2, a // 3, piece]
        row = first[name] + filled[name]
        filled[name] += 1
        pack[row, t] = 1
        column = (o + 6) % 12
        which = level // 2 * 2 + (0 if piece == 1 else 1)
        window[which * SPAN + level % 2 * 72 + (a + 3) % 6 * 12 + column, row] = 1
    row_of = np.zeros((TOKENS, 144), np.float32)
    column_of = np.zeros((TOKENS, 128), np.float32)
    for which in range(4):
        source = (0, 0, 1, 2)[which]
        for n in range(SPAN):
            t = which * SPAN + n
            row_of[t, (source * 6 + n // 12 % 6) * 8 + n // 72 + (2 if source else 0)] = 1
            column_of[t, n % 12 + (12 if which % 2 == 0 else 0)] = 1
    made = pack, window, pack.T, window.T, row_of, column_of
    return [jnp.asarray(m, BF) for m in made]


def dot(a, b, dims=NN):
    return lax.dot_general(a, b, dims, preferred_element_type=F32)


def kernel(x_hbm, cot_hbm, region_ref, gain_ref, w_hbm, wo_hbm,
           pack_hbm, window_hbm, unpack_hbm, unwindow_hbm, row_ref, column_ref,
           result_ref, grad_ref, gq_ref, go_ref,
           x_ref, cot_ref, w_ref, wo_ref, pack_ref, window_ref, unpack_ref, unwindow_ref,
           px_ref, pc_ref, rx_ref, rc_ref, regions_ref, rr_ref, hot_ref,
           xw_ref, cw_ref, normed_ref, nbf_ref, inv_ref, proj_ref, aw_ref, att_ref, ga_ref, gp_ref, tr_ref,
           po_ref, pg_ref, ro_ref, rg_ref,
           gw_ref, r0_ref, s0_ref, r1_ref, s1_ref, r2_ref, s2_ref, r3_ref, fin_ref, all_ref,
           load_sem, halo_send, halo_recv, region_send, region_recv, rs_send, rs_recv):
    lat, lon = lax.axis_index("lat"), lax.axis_index("lon")
    core = lon % 2
    at = (lon // 8 * 2 + lat // 4, lon // 2 % 4, lat % 4)

    def near(step):
        return ((lat + step[0] + 8) % 8, (lon + step[1] + 16) % 16)

    def chip(x, y, z, c):
        return (x % 2 * 4 + z, (x // 2 * 4 + y) * 2 + c)

    def along(axis, k):
        there = list(at)
        there[axis] = (at[axis] + k) % 4
        return chip(*there, core)

    partners = [near(step) for _, _, _, step in SECTIONS[1:]]
    partners += [chip(*at, 1 - core)]
    partners += [along(axis, k) for axis in range(3) for k in (1, 2, 3)]
    loads = [
        pltpu.make_async_copy(src, dst, load_sem.at[n])
        for n, (src, dst) in enumerate((
            (pack_hbm, pack_ref), (x_hbm, x_ref), (cot_hbm, cot_ref), (window_hbm, window_ref), (w_hbm, w_ref),
            (wo_hbm, wo_ref), (unwindow_hbm, unwindow_ref), (unpack_hbm, unpack_ref),
        ))
    ]
    for load in loads:
        load.start()

    barrier = pltpu.get_barrier_semaphore()
    for partner in partners:
        pl.semaphore_signal(barrier, inc=1, device_id=partner, device_id_type=MESH)

    def halo(which, src, dst, back):
        made = []
        for n, (_, row, rows, step) in enumerate(SECTIONS[1:]):
            to = near((-step[0], -step[1])) if back else near(step)
            made.append(pltpu.make_async_remote_copy(
                src_ref=src.at[pl.ds(row, rows)], dst_ref=dst.at[pl.ds(row, rows)],
                send_sem=halo_send.at[which, n], recv_sem=halo_recv.at[which, n],
                device_id=to, device_id_type=MESH))
        return made

    loads[0].wait()
    loads[1].wait()
    px_ref[...] = dot(pack_ref[...], x_ref[...]).astype(BF)
    pl.semaphore_wait(barrier, len(partners))
    go_x = halo(0, px_ref, rx_ref, False)
    for copy in go_x:
        copy.start()
    go_regions = [
        pltpu.make_async_remote_copy(
            src_ref=region_ref, dst_ref=regions_ref.at[n],
            send_sem=region_send.at[n], recv_sem=region_recv.at[n],
            device_id=near(step), device_id_type=MESH)
        for n, step in enumerate(((-1, 0), (-1, -1)))
    ]
    for copy in go_regions:
        copy.start()
    loads[2].wait()
    pc_ref[...] = dot(pack_ref[...], cot_ref[...]).astype(BF)
    go_cot = halo(1, pc_ref, rc_ref, False)
    for copy in go_cot:
        copy.start()
    rx_ref[pl.ds(0, 224), :] = px_ref[pl.ds(0, 224), :]
    rc_ref[pl.ds(0, 224), :] = pc_ref[pl.ds(0, 224), :]

    for copy in go_regions:
        copy.wait_recv()
    rr_ref[...] = jnp.zeros_like(rr_ref)
    for n in range(18):
        piece = region_ref[n % 6] if n < 6 else regions_ref[n // 6 - 1, n % 6]
        rr_ref[pl.ds(8 * n, 4), pl.ds(0, 24)] = piece.astype(F32)
    picked = dot(row_ref[...], rr_ref[...].astype(BF)) * column_ref[...].astype(F32)
    value = dot(picked.astype(BF), jnp.ones((128, 128), BF))
    lanes = lax.broadcasted_iota(jnp.int32, (TOKENS, 128), 1).astype(F32)
    hot_ref[...] = jnp.where(value == lanes, 1.0, 0.0).astype(BF)

    gain = gain_ref[...]
    loads[3].wait()
    for copy in go_x:
        copy.wait_recv()
    for w in range(4):
        rows = pl.ds(w * SPAN, SPAN)
        x = dot(window_ref[rows, :], rx_ref[...])
        xw_ref[rows, :] = x.astype(BF)
        centered = x - jnp.mean(x, -1, keepdims=True)
        var = jnp.mean(centered * centered, -1, keepdims=True)
        inv = lax.rsqrt(var + 1e-5)
        normed = centered * inv
        normed_ref[rows, :] = normed
        inv_ref[rows, :] = inv
        nbf_ref[rows, :] = (normed * gain).astype(BF)
    loads[4].wait()
    for c in range(6):
        cols = pl.ds(c * 256, 256)
        proj_ref[:, cols] = dot(nbf_ref[...], w_ref[:, cols]).astype(BF)

    lane = lax.broadcasted_iota(jnp.int32, (1, 128), 1)
    masks = [jnp.where((lane < 64) == (h == 0), 1.0, 0.0).astype(BF) for h in range(2)]
    eighths = [(m * 0.125).astype(BF) for m in masks]

    def forward(p):
        col = p * 128
        for w in range(4):
            rows = pl.ds(w * SPAN, SPAN)
            q2 = proj_ref[rows, pl.ds(col, 128)]
            k2 = proj_ref[rows, pl.ds(512 + col, 128)]
            v2 = proj_ref[rows, pl.ds(1024 + col, 128)]
            hot = hot_ref[rows, :]
            qx = jnp.concatenate([q2, hot * jnp.array(-1e30, BF)], 1)
            off = (1.0 - hot.astype(F32)).astype(BF)
            att = []
            for h in range(2):
                s = dot(qx, jnp.concatenate([k2 * eighths[h], off], 1), NT)
                e = jnp.exp(s - jnp.max(s, -1, keepdims=True))
                a = e * (1.0 / jnp.sum(e, -1, keepdims=True))
                aw_ref[p, w, h] = a
                att.append(dot(a.astype(BF), v2))
            att_ref[rows, pl.ds(col, 128)] = jnp.where(lane < 64, att[0], att[1]).astype(BF)

    for p in range(4):
        forward(p)

    loads[5].wait()
    for copy in go_cot:
        copy.wait_recv()
    cw_ref[...] = dot(window_ref[...], rc_ref[...]).astype(BF)
    for c in range(2):
        ga_ref[:, pl.ds(c * 256, 256)] = dot(cw_ref[...], wo_ref[pl.ds(c * 256, 256), :], NT).astype(BF)
    def backward(p):
        col = p * 128
        for w in range(4):
            rows = pl.ds(w * SPAN, SPAN)
            q2 = proj_ref[rows, pl.ds(col, 128)]
            k2 = proj_ref[rows, pl.ds(512 + col, 128)]
            v2 = proj_ref[rows, pl.ds(1024 + col, 128)]
            g2 = ga_ref[rows, pl.ds(col, 128)]
            qt = (q2 * jnp.array(0.125, BF)).T
            gt = g2.T
            gq = None
            gkt = []
            gvt = []
            for h in range(2):
                a = aw_ref[p, w, h]
                gw = dot(g2, v2 * masks[h], NT)
                prod = gw * a
                inner = jnp.sum(prod, -1, keepdims=True)
                ds = (prod - a * inner).astype(BF)
                part = dot(ds, k2 * eighths[h])
                gq = part if gq is None else gq + part
                gkt.append(dot(qt[64 * h:64 * h + 64], ds))
                gvt.append(dot(gt[64 * h:64 * h + 64], a.astype(BF)))
            gp_ref[rows, pl.ds(col, 128)] = gq.astype(BF)
            gp_ref[rows, pl.ds(512 + col, 128)] = jnp.concatenate(gkt, 0).astype(BF).T
            gp_ref[rows, pl.ds(1024 + col, 128)] = jnp.concatenate(gvt, 0).astype(BF).T

    def swap(first, count):
        return pltpu.make_async_remote_copy(
            src_ref=gw_ref.at[pl.ds(first, count), :, 1 - core], dst_ref=r0_ref.at[pl.ds(first, count)],
            send_sem=rs_send.at[first], recv_sem=rs_recv.at[first],
            device_id=chip(*at, 1 - core), device_id_type=MESH)

    tr_ref[0] = nbf_ref[...].T
    tr_ref[1] = att_ref[...].T
    for m in range(4):
        block = pltpu.roll(dot(tr_ref[1], cw_ref[:, pl.ds(128 * m, 128)]), 64, 1)
        gw_ref[12 + m] = block.reshape(8, 2, 32, 128)
    swaps = [swap(12, 4)]
    swaps[0].start()
    for p in range(4):
        backward(p)
        pieces = jnp.concatenate([gp_ref[:, pl.ds(512 * t + 128 * p, 128)] for t in range(3)], 1)
        grads = dot(tr_ref[0], pieces)
        for t in range(3):
            gw_ref[4 * t + p] = grads[:, 128 * t:128 * t + 128].reshape(8, 2, 32, 128)
            swaps.append(swap(4 * t + p, 1))
            swaps[-1].start()

    for w in range(4):
        rows = pl.ds(w * SPAN, SPAN)
        branch = dot(att_ref[rows, :], wo_ref[...])
        xw_ref[rows, :] = (xw_ref[rows, :].astype(F32) + branch).astype(BF)
    for copy in swaps:
        copy.wait_recv()
    for m in range(4):
        whole = [gw_ref[b, :, core] + r0_ref[b] for b in (3 * m, 3 * m + 1, 3 * m + 2, 12 + m)]
        left = lane < 64
        for n, parts in ((0, (whole[0], jnp.where(left, whole[1], whole[3]))),
                         (1, (whole[2], jnp.where(left, whole[3], whole[1])))):
            for half in range(2):
                for x_lo in range(2):
                    s0_ref[m // 2 * 2 + x_lo, m % 2 * 2 + n, :, half] = parts[half][4 * x_lo:4 * x_lo + 4].astype(BF)

    def scatter(stage, s, k, src, dst):
        n = 16 + (stage * 4 + s) * 3 + k - 1
        return pltpu.make_async_remote_copy(
            src_ref=src, dst_ref=dst, send_sem=rs_send.at[n], recv_sem=rs_recv.at[n],
            device_id=along(ORDERS[s][stage], k), device_id_type=MESH)

    def quarter(s, axis, index):
        half, rows = s // 2, pl.ds(s % 2 * 16, 16)
        if axis == 0:
            return s0_ref.at[index, :, :, half, rows]
        if axis == 1:
            return s0_ref.at[:, index, :, half, rows]
        return s0_ref.at[:, :, index, half, rows]

    first = [[scatter(0, s, k, quarter(s, ORDERS[s][0], (at[ORDERS[s][0]] + k) % 4), r1_ref.at[s, k - 1])
              for k in (1, 2, 3)] for s in range(4)]
    for k in range(3):
        for s in range(4):
            first[s][k].start()
    loads[6].wait()
    po_ref[...] = dot(unwindow_ref[...], xw_ref[...]).astype(BF)
    go_out = halo(2, po_ref, ro_ref, True)
    for copy in go_out:
        copy.start()
    ro_ref[pl.ds(0, 224), :] = po_ref[pl.ds(0, 224), :]
    for w in range(4):
        rows = pl.ds(w * SPAN, SPAN)
        gh = dot(gp_ref[rows, :], w_ref[...], NT) * gain
        normed = normed_ref[rows, :]
        gs = inv_ref[rows, :] * (gh - jnp.mean(gh, -1, keepdims=True)
                                 - normed * jnp.mean(gh * normed, -1, keepdims=True))
        nbf_ref[rows, :] = gs.astype(BF)
    pg_ref[...] = dot(unwindow_ref[...], nbf_ref[...]).astype(BF)
    go_grad = halo(3, pg_ref, rg_ref, True)
    for copy in go_grad:
        copy.start()
    rg_ref[pl.ds(0, 224), :] = pg_ref[pl.ds(0, 224), :]

    second = []
    for s in range(4):
        axis, nxt = ORDERS[s][0], ORDERS[s][1]
        for copy in first[s]:
            copy.wait_recv()
        total = quarter(s, axis, at[axis])[...].astype(F32)
        for k in range(3):
            total = total + r1_ref[s, k].astype(F32)
        s1_ref[s] = total
        copies = []
        for k in (1, 2, 3):
            there = (at[nxt] + k) % 4
            left = [a for a in range(3) if a != axis]
            src = s1_ref.at[s, there] if left[0] == nxt else s1_ref.at[s, :, there]
            copies.append(scatter(1, s, k, src, r2_ref.at[s, k - 1]))
            copies[-1].start()
        second.append(copies)
    loads[7].wait()
    for copy in go_out:
        copy.wait_recv()
    result_ref[...] = dot(unpack_ref[...], ro_ref[...]).astype(BF)

    third = []
    for s in range(4):
        axis, nxt, last = ORDERS[s]
        for copy in second[s]:
            copy.wait_recv()
        left = [a for a in range(3) if a != axis]
        total = s1_ref[s, at[nxt]] if left[0] == nxt else s1_ref[s, :, at[nxt]]
        for k in range(3):
            total = total + r2_ref[s, k]
        s2_ref[s] = total
        copies = []
        for k in (1, 2, 3):
            copies.append(scatter(2, s, k, s2_ref.at[s, (at[last] + k) % 4], r3_ref.at[s, k - 1]))
            copies[-1].start()
        third.append(copies)
    for copy in go_grad:
        copy.wait_recv()
    grad_ref[...] = (cot_ref[...].astype(F32) + dot(unpack_ref[...], rg_ref[...])).astype(BF)
    for s in range(4):
        for copy in third[s]:
            copy.wait_recv()
        total = s2_ref[s, at[ORDERS[s][2]]]
        for k in range(3):
            total = total + r3_ref[s, k]
        fin_ref[pl.ds(s % 2 * 16, 16), pl.ds(s // 2 * 128, 128)] = total
    last = pltpu.make_async_remote_copy(
        src_ref=fin_ref, dst_ref=all_ref.at[core], send_sem=rs_send.at[52], recv_sem=rs_recv.at[52],
        device_id=chip(*at, 1 - core), device_id_type=MESH)
    last.start()
    all_ref[core] = fin_ref[...]
    last.wait_recv()
    whole = all_ref[...].reshape(64, 256)
    whole = jnp.where(at[1] % 2 == 1, pltpu.roll(whole, 64, 1), whole)
    gq_ref[...] = jnp.where(core == 1, pltpu.roll(whole, 160, 1), whole)[:, :96]
    outs = whole[:, 128:]
    go_ref[...] = jnp.where(core == 1, pltpu.roll(outs, 32, 1), pltpu.roll(outs, 64, 1)).T[:32]

    started = go_x + go_regions + go_cot + go_out + go_grad + swaps + [last]
    for copies in first + second + third:
        started += copies
    for copy in started:
        copy.wait_send()


def hand_over(*refs):
    for n in range(4):
        refs[4 + n][...] = refs[n][...]


def on_device(tokens, cotangent, region_ids, norm_gain, qkv_weight, out_weight):
    pack, window, unpack, unwindow, row_of, column_of = constants()
    vm = pl.BlockSpec(memory_space=pltpu.VMEM)
    hbm = pl.BlockSpec(memory_space=pl.ANY)

    def bf(*shape):
        return pltpu.VMEM(shape, BF)

    def f32(*shape):
        return pltpu.VMEM(shape, F32)

    sums = pl.pallas_call(
        kernel,
        out_shape=(
            jax.ShapeDtypeStruct((TOKENS, WIDTH), BF),
            jax.ShapeDtypeStruct((TOKENS, WIDTH), BF),
            jax.ShapeDtypeStruct((64, 96), F32),
            jax.ShapeDtypeStruct((32, 64), F32),
        ),
        in_specs=[hbm, hbm, vm, vm, hbm, hbm, hbm, hbm, hbm, hbm, vm, vm],
        out_specs=(vm, vm, vm, vm),
        scratch_shapes=[
            bf(TOKENS, WIDTH), bf(TOKENS, WIDTH), bf(WIDTH, 3 * WIDTH), bf(WIDTH, WIDTH),
            bf(PACKED, TOKENS), bf(TOKENS, PACKED), bf(TOKENS, PACKED), bf(PACKED, TOKENS),
            bf(PACKED, WIDTH), bf(PACKED, WIDTH), bf(PACKED, WIDTH), bf(PACKED, WIDTH),
            pltpu.VMEM((2, 6, 4, 24), jnp.int32), f32(144, 128), bf(TOKENS, 128),
            bf(TOKENS, WIDTH), bf(TOKENS, WIDTH), f32(TOKENS, WIDTH), bf(TOKENS, WIDTH), f32(TOKENS, 1),
            bf(TOKENS, 3 * WIDTH), f32(4, 4, 2, SPAN, SPAN), bf(TOKENS, WIDTH), bf(TOKENS, WIDTH),
            bf(TOKENS, 3 * WIDTH), bf(2, WIDTH, TOKENS),
            bf(PACKED, WIDTH), bf(PACKED, WIDTH), bf(PACKED, WIDTH), bf(PACKED, WIDTH),
            f32(16, 8, 2, 32, 128), f32(16, 8, 32, 128), bf(4, 4, 4, 2, 32, 128),
            bf(4, 3, 4, 4, 16, 128), f32(4, 4, 4, 16, 128),
            f32(4, 3, 4, 16, 128), f32(4, 4, 16, 128), f32(4, 3, 16, 128), f32(32, 256), f32(2, 32, 256),
            pltpu.SemaphoreType.DMA((8,)),
            pltpu.SemaphoreType.DMA((4, 6)), pltpu.SemaphoreType.DMA((4, 6)),
            pltpu.SemaphoreType.DMA((2,)), pltpu.SemaphoreType.DMA((2,)),
            pltpu.SemaphoreType.DMA((53,)), pltpu.SemaphoreType.DMA((53,)),
        ],
        compiler_params=pltpu.CompilerParams(
            vmem_limit_bytes=56 << 20, collective_id=0, has_side_effects=True),
        cost_estimate=pl.CostEstimate(flops=6 * 10**9, bytes_accessed=10**7, transcendentals=0),
    )(
        tokens.reshape(TOKENS, WIDTH), cotangent.reshape(TOKENS, WIDTH), region_ids.transpose(1, 0, 2), norm_gain.reshape(1, WIDTH),
        qkv_weight, out_weight, pack, window, unpack, unwindow, row_of, column_of,
    )
    result, grad, gq, go = pl.pallas_call(
        hand_over,
        out_shape=tuple(jax.ShapeDtypeStruct(a.shape, a.dtype) for a in sums),
        in_specs=[vm] * 4,
        out_specs=(vm,) * 4,
    )(*sums)
    return (result.reshape(tokens.shape), grad.reshape(tokens.shape), gq, go.T)


def solution(mesh):
    placed = (
        P(None, "lat", "lon", None),
        P(None, "lat", "lon", None),
        P(None, "lat", "lon"),
        P(),
        P(),
        P(),
    )
    return jax.shard_map(
        on_device,
        mesh=mesh,
        in_specs=placed,
        out_specs=(
            P(None, "lat", "lon", None),
            P(None, "lat", "lon", None),
            P("lat", "lon"),
            P("lat", "lon"),
        ),
        check_vma=False,
    )
```

```python
import functools

import jax
import jax.numpy as jnp
import numpy as np
from jax import lax
from jax.experimental import pallas as pl
from jax.experimental.pallas import tpu as pltpu
from jax.sharding import PartitionSpec as P

SPAN = 144
TOKENS = 576
PACKED = 640
WIDTH = 512
NN = (((1,), (0,)), ((), ()))
NT = (((1,), (1,)), ((), ()))
BF = jnp.bfloat16
F32 = jnp.float32
MESH = pl.DeviceIdType.MESH

SECTIONS = (
    ("local", 0, 224, (0, 0)),
    ("lat+", 224, 112, (1, 0)),
    ("lat-", 336, 112, (-1, 0)),
    ("lon+", 448, 48, (0, 1)),
    ("lon-", 496, 48, (0, -1)),
    ("diag+", 544, 48, (1, 1)),
    ("diag-", 592, 48, (-1, -1)),
)
GOES = {
    (0, 0, 1): "local", (0, 1, 1): "lat+", (0, 0, 0): "local",
    (0, 0, 2): "lon+", (0, 1, 0): "lat+", (0, 1, 2): "diag+",
    (1, 1, 1): "local", (1, 0, 1): "lat-", (1, 1, 2): "local",
    (1, 1, 0): "lon-", (1, 0, 2): "lat-", (1, 0, 0): "diag-",
}

def constants():
    pack = np.zeros((PACKED, TOKENS), np.float32)
    window = np.zeros((TOKENS, PACKED), np.float32)
    first = {name: row for name, row, _, _ in SECTIONS}
    filled = dict.fromkeys(first, 0)
    for t in range(TOKENS):
        l, a, o = t // 144, t // 24 % 6, t % 24
        level = (l + 1) % 4
        piece = 0 if o < 6 else 1 if o < 18 else 2
        name = GOES[level // 2, a // 3, piece]
        row = first[name] + filled[name]
        filled[name] += 1
        pack[row, t] = 1
        column = (o + 6) % 12
        which = level // 2 * 2 + (0 if piece == 1 else 1)
        window[which * SPAN + level % 2 * 72 + (a + 3) % 6 * 12 + column, row] = 1
    row_of = np.zeros((TOKENS, 144), np.float32)
    column_of = np.zeros((TOKENS, 128), np.float32)
    for which in range(4):
        source = (0, 0, 1, 2)[which]
        for n in range(SPAN):
            t = which * SPAN + n
            row_of[t, (source * 6 + n // 12 % 6) * 8 + n // 72 + (2 if source else 0)] = 1
            column_of[t, n % 12 + (12 if which % 2 == 0 else 0)] = 1
    made = pack, window, pack.T, window.T, row_of, column_of
    return [jnp.asarray(m, BF) for m in made]


def dot(a, b, dims=NN):
    return lax.dot_general(a, b, dims, preferred_element_type=F32)


def kernel(x_hbm, cot_hbm, region_ref, gain_ref, w_hbm, wo_hbm,
           pack_hbm, window_hbm, unpack_hbm, unwindow_hbm, row_ref, column_ref,
           result_ref, grad_ref, gq_ref, go_ref,
           x_ref, cot_ref, w_ref, wo_ref, pack_ref, window_ref, unpack_ref, unwindow_ref,
           px_ref, pc_ref, rx_ref, rc_ref, regions_ref, rr_ref, hot_ref,
           xw_ref, cw_ref, normed_ref, nbf_ref, inv_ref, proj_ref, aw_ref, att_ref, ga_ref, gp_ref, tr_ref,
           po_ref, pg_ref, ro_ref, rg_ref,
           gw_ref, r0_ref, zs_ref, zr_ref, ps_ref, pr_ref, fin_ref, all_ref,
           load_sem, halo_send, halo_recv, region_send, region_recv, rs_send, rs_recv):
    lat, lon = lax.axis_index("lat"), lax.axis_index("lon")
    core = lon % 2
    at = (lon // 8 * 2 + lat // 4, lon // 2 % 4, lat % 4)

    def near(step):
        return ((lat + step[0] + 8) % 8, (lon + step[1] + 16) % 16)

    def chip(x, y, z, c):
        return (x % 2 * 4 + z, (x // 2 * 4 + y) * 2 + c)

    def ahead(dx, dy, dz):
        return chip((at[0] + dx) % 4, (at[1] + dy) % 4, (at[2] + dz) % 4, core)

    steps = [(dx, dy) for dx in range(4) for dy in range(4) if dx or dy]
    partners = [near(step) for _, _, _, step in SECTIONS[1:]]
    partners += [chip(*at, 1 - core)]
    partners += [ahead(0, 0, k) for k in (1, 2, 3)]
    partners += [ahead(dx, dy, 0) for dx, dy in steps]
    loads = [
        pltpu.make_async_copy(src, dst, load_sem.at[n])
        for n, (src, dst) in enumerate((
            (pack_hbm, pack_ref), (x_hbm, x_ref), (cot_hbm, cot_ref), (window_hbm, window_ref), (w_hbm, w_ref),
            (wo_hbm, wo_ref), (unwindow_hbm, unwindow_ref), (unpack_hbm, unpack_ref),
        ))
    ]
    for load in loads:
        load.start()

    barrier = pltpu.get_barrier_semaphore()
    for partner in partners:
        pl.semaphore_signal(barrier, inc=1, device_id=partner, device_id_type=MESH)

    def halo(which, src, dst, back):
        made = []
        for n, (_, row, rows, step) in enumerate(SECTIONS[1:]):
            to = near((-step[0], -step[1])) if back else near(step)
            made.append(pltpu.make_async_remote_copy(
                src_ref=src.at[pl.ds(row, rows)], dst_ref=dst.at[pl.ds(row, rows)],
                send_sem=halo_send.at[which, n], recv_sem=halo_recv.at[which, n],
                device_id=to, device_id_type=MESH))
        return made

    loads[0].wait()
    loads[1].wait()
    px_ref[...] = dot(pack_ref[...], x_ref[...]).astype(BF)
    pl.semaphore_wait(barrier, len(partners))
    go_x = halo(0, px_ref, rx_ref, False)
    for copy in go_x:
        copy.start()
    go_regions = [
        pltpu.make_async_remote_copy(
            src_ref=region_ref, dst_ref=regions_ref.at[n],
            send_sem=region_send.at[n], recv_sem=region_recv.at[n],
            device_id=near(step), device_id_type=MESH)
        for n, step in enumerate(((-1, 0), (-1, -1)))
    ]
    for copy in go_regions:
        copy.start()
    loads[2].wait()
    pc_ref[...] = dot(pack_ref[...], cot_ref[...]).astype(BF)
    go_cot = halo(1, pc_ref, rc_ref, False)
    for copy in go_cot:
        copy.start()
    rx_ref[pl.ds(0, 224), :] = px_ref[pl.ds(0, 224), :]
    rc_ref[pl.ds(0, 224), :] = pc_ref[pl.ds(0, 224), :]

    for copy in go_regions:
        copy.wait_recv()
    rr_ref[...] = jnp.zeros_like(rr_ref)
    for n in range(18):
        piece = region_ref[n % 6] if n < 6 else regions_ref[n // 6 - 1, n % 6]
        rr_ref[pl.ds(8 * n, 4), pl.ds(0, 24)] = piece.astype(F32)
    picked = dot(row_ref[...], rr_ref[...].astype(BF)) * column_ref[...].astype(F32)
    value = dot(picked.astype(BF), jnp.ones((128, 128), BF))
    lanes = lax.broadcasted_iota(jnp.int32, (TOKENS, 128), 1).astype(F32)
    hot_ref[...] = jnp.where(value == lanes, 1.0, 0.0).astype(BF)

    gain = gain_ref[...]
    loads[3].wait()
    for copy in go_x:
        copy.wait_recv()
    for w in range(4):
        rows = pl.ds(w * SPAN, SPAN)
        x = dot(window_ref[rows, :], rx_ref[...])
        xw_ref[rows, :] = x.astype(BF)
        centered = x - jnp.mean(x, -1, keepdims=True)
        var = jnp.mean(centered * centered, -1, keepdims=True)
        inv = lax.rsqrt(var + 1e-5)
        normed = centered * inv
        normed_ref[rows, :] = normed
        inv_ref[rows, :] = inv
        nbf_ref[rows, :] = (normed * gain).astype(BF)
    loads[4].wait()
    for c in range(6):
        cols = pl.ds(c * 256, 256)
        proj_ref[:, cols] = dot(nbf_ref[...], w_ref[:, cols]).astype(BF)

    lane = lax.broadcasted_iota(jnp.int32, (1, 128), 1)
    masks = [jnp.where((lane < 64) == (h == 0), 1.0, 0.0).astype(BF) for h in range(2)]
    eighths = [(m * 0.125).astype(BF) for m in masks]

    def forward(p):
        col = p * 128
        for w in range(4):
            rows = pl.ds(w * SPAN, SPAN)
            q2 = proj_ref[rows, pl.ds(col, 128)]
            k2 = proj_ref[rows, pl.ds(512 + col, 128)]
            v2 = proj_ref[rows, pl.ds(1024 + col, 128)]
            hot = hot_ref[rows, :]
            qx = jnp.concatenate([q2, hot * jnp.array(-1e30, BF)], 1)
            off = (1.0 - hot.astype(F32)).astype(BF)
            att = []
            for h in range(2):
                s = dot(qx, jnp.concatenate([k2 * eighths[h], off], 1), NT)
                e = jnp.exp(s - jnp.max(s, -1, keepdims=True))
                a = e * (1.0 / jnp.sum(e, -1, keepdims=True))
                aw_ref[p, w, h] = a
                att.append(dot(a.astype(BF), v2))
            att_ref[rows, pl.ds(col, 128)] = jnp.where(lane < 64, att[0], att[1]).astype(BF)

    for p in range(4):
        forward(p)

    loads[5].wait()
    for w in range(4):
        rows = pl.ds(w * SPAN, SPAN)
        branch = dot(att_ref[rows, :], wo_ref[...])
        xw_ref[rows, :] = (xw_ref[rows, :].astype(F32) + branch).astype(BF)
    loads[6].wait()
    po_ref[...] = dot(unwindow_ref[...], xw_ref[...]).astype(BF)
    go_out = halo(2, po_ref, ro_ref, True)
    for copy in go_out:
        copy.start()
    ro_ref[pl.ds(0, 224), :] = po_ref[pl.ds(0, 224), :]

    for copy in go_cot:
        copy.wait_recv()
    cw_ref[...] = dot(window_ref[...], rc_ref[...]).astype(BF)
    for c in range(2):
        ga_ref[:, pl.ds(c * 256, 256)] = dot(cw_ref[...], wo_ref[pl.ds(c * 256, 256), :], NT).astype(BF)

    def backward(p):
        col = p * 128
        for w in range(4):
            rows = pl.ds(w * SPAN, SPAN)
            q2 = proj_ref[rows, pl.ds(col, 128)]
            k2 = proj_ref[rows, pl.ds(512 + col, 128)]
            v2 = proj_ref[rows, pl.ds(1024 + col, 128)]
            g2 = ga_ref[rows, pl.ds(col, 128)]
            qt = (q2 * jnp.array(0.125, BF)).T
            gt = g2.T
            gq = None
            gkt = []
            gvt = []
            for h in range(2):
                a = aw_ref[p, w, h]
                gw = dot(g2, v2 * masks[h], NT)
                prod = gw * a
                inner = jnp.sum(prod, -1, keepdims=True)
                ds = (prod - a * inner).astype(BF)
                part = dot(ds, k2 * eighths[h])
                gq = part if gq is None else gq + part
                gkt.append(dot(qt[64 * h:64 * h + 64], ds))
                gvt.append(dot(gt[64 * h:64 * h + 64], a.astype(BF)))
            gp_ref[rows, pl.ds(col, 128)] = gq.astype(BF)
            gp_ref[rows, pl.ds(512 + col, 128)] = jnp.concatenate(gkt, 0).astype(BF).T
            gp_ref[rows, pl.ds(1024 + col, 128)] = jnp.concatenate(gvt, 0).astype(BF).T
            if w == 1:
                z_sends.append(z_stage(p - 1 if p else 4))

    def group(g):
        return pl.ds(3 * g, 3 if g < 4 else 4)

    def swap(g):
        return pltpu.make_async_remote_copy(
            src_ref=gw_ref.at[group(g), 1 - core], dst_ref=r0_ref.at[group(g)],
            send_sem=rs_send.at[g], recv_sem=rs_recv.at[g],
            device_id=chip(*at, 1 - core), device_id_type=MESH)

    def z_stage(g):
        swaps[g].wait_recv()
        for b in range(3 * g, 3 * g + (3 if g < 4 else 4)):
            zs_ref[b] = (gw_ref[b, core] + r0_ref[b]).astype(BF).reshape(2, 4, 32, 128)
        copies = []
        for k in (1, 2, 3):
            n = 2 + 3 * g + k
            copies.append(pltpu.make_async_remote_copy(
                src_ref=zs_ref.at[group(g), :, (at[2] + k) % 4], dst_ref=zr_ref.at[k - 1, group(g)],
                send_sem=rs_send.at[n + 2], recv_sem=rs_recv.at[n + 2],
                device_id=ahead(0, 0, k), device_id_type=MESH))
            copies[-1].start()
        return copies

    def gradient(w):
        rows = pl.ds(w * SPAN, SPAN)
        gh = dot(gp_ref[rows, :], w_ref[...], NT) * gain
        normed = normed_ref[rows, :]
        gs = inv_ref[rows, :] * (gh - jnp.mean(gh, -1, keepdims=True)
                                 - normed * jnp.mean(gh * normed, -1, keepdims=True))
        nbf_ref[rows, :] = gs.astype(BF)

    tr_ref[0] = nbf_ref[...].T
    tr_ref[1] = att_ref[...].T
    swaps = {g: swap(g) for g in range(5)}
    z_sends = []

    def keep(b, grads):
        halves = grads.reshape(8, 2, 32, 128)
        gw_ref[b, 0] = halves[:, 0]
        gw_ref[b, 1] = halves[:, 1]

    for m in range(4):
        keep(12 + m, pltpu.roll(dot(tr_ref[1], cw_ref[:, pl.ds(128 * m, 128)]), 64, 1))
    swaps[4].start()
    for p in range(4):
        backward(p)
        pieces = jnp.concatenate([gp_ref[:, pl.ds(512 * t + 128 * p, 128)] for t in range(3)], 1)
        grads = dot(tr_ref[0], pieces)
        for t in range(3):
            keep(3 * p + t, grads[:, 128 * t:128 * t + 128])
        swaps[p].start()

    for w in range(3):
        gradient(w)
    z_sends.append(z_stage(3))
    gradient(3)
    pg_ref[...] = dot(unwindow_ref[...], nbf_ref[...]).astype(BF)
    go_grad = halo(3, pg_ref, rg_ref, True)
    for copy in go_grad:
        copy.start()
    rg_ref[pl.ds(0, 224), :] = pg_ref[pl.ds(0, 224), :]

    for copies in z_sends:
        for copy in copies:
            copy.wait_recv()

    def summed(b):
        total = zs_ref[b, :, at[2]].astype(F32)
        for k in range(3):
            total = total + zr_ref[k, b].astype(F32)
        return total

    left = lane < 64
    for m in range(4):
        whole = [summed(b % 4 * 3 + b // 4) for b in (3 * m, 3 * m + 1, 3 * m + 2)] + [summed(12 + m)]
        for n, parts in ((0, (whole[0], jnp.where(left, whole[1], whole[3]))),
                         (1, (whole[2], jnp.where(left, whole[3], whole[1])))):
            for half in range(2):
                for x_lo in range(2):
                    ps_ref[m // 2 * 2 + x_lo, m % 2 * 2 + n, half] = parts[half][x_lo]
    planes = []
    for n, (dx, dy) in enumerate(steps):
        planes.append(pltpu.make_async_remote_copy(
            src_ref=ps_ref.at[(at[0] + dx) % 4, (at[1] + dy) % 4], dst_ref=pr_ref.at[n],
            send_sem=rs_send.at[20 + n], recv_sem=rs_recv.at[20 + n],
            device_id=ahead(dx, dy, 0), device_id_type=MESH))
    for copy in planes:
        copy.start()

    loads[7].wait()
    for copy in go_out:
        copy.wait_recv()
    result_ref[...] = dot(unpack_ref[...], ro_ref[...]).astype(BF)

    for copy in go_grad:
        copy.wait_recv()
    grad_ref[...] = (cot_ref[...].astype(F32) + dot(unpack_ref[...], rg_ref[...])).astype(BF)
    for copy in planes:
        copy.wait_recv()
    total = ps_ref[at[0], at[1]]
    for n in range(15):
        total = total + pr_ref[n]
    fin_ref[...] = total
    last = pltpu.make_async_remote_copy(
        src_ref=fin_ref, dst_ref=all_ref.at[core], send_sem=rs_send.at[35], recv_sem=rs_recv.at[35],
        device_id=chip(*at, 1 - core), device_id_type=MESH)
    last.start()
    all_ref[core] = fin_ref[...]
    last.wait_recv()
    whole = jnp.concatenate([all_ref[:, half].reshape(64, 128) for half in range(2)], 1)
    whole = jnp.where(at[1] % 2 == 1, pltpu.roll(whole, 64, 1), whole)
    gq_ref[...] = jnp.where(core == 1, pltpu.roll(whole, 160, 1), whole)[:, :96]
    outs = whole[:, 128:]
    go_ref[...] = jnp.where(core == 1, pltpu.roll(outs, 32, 1), pltpu.roll(outs, 64, 1)).T[:32]

    started = go_x + go_regions + go_cot + go_out + go_grad + list(swaps.values()) + planes + [last]
    for copies in z_sends:
        started += copies
    for copy in started:
        copy.wait_send()


def hand_over(*refs):
    for n in range(4):
        refs[4 + n][...] = refs[n][...]


def on_device(tokens, cotangent, region_ids, norm_gain, qkv_weight, out_weight):
    pack, window, unpack, unwindow, row_of, column_of = constants()
    vm = pl.BlockSpec(memory_space=pltpu.VMEM)
    hbm = pl.BlockSpec(memory_space=pl.ANY)

    def bf(*shape):
        return pltpu.VMEM(shape, BF)

    def f32(*shape):
        return pltpu.VMEM(shape, F32)

    sums = pl.pallas_call(
        kernel,
        out_shape=(
            jax.ShapeDtypeStruct((TOKENS, WIDTH), BF),
            jax.ShapeDtypeStruct((TOKENS, WIDTH), BF),
            jax.ShapeDtypeStruct((64, 96), F32),
            jax.ShapeDtypeStruct((32, 64), F32),
        ),
        in_specs=[hbm, hbm, vm, vm, hbm, hbm, hbm, hbm, hbm, hbm, vm, vm],
        out_specs=(vm, vm, vm, vm),
        scratch_shapes=[
            bf(TOKENS, WIDTH), bf(TOKENS, WIDTH), bf(WIDTH, 3 * WIDTH), bf(WIDTH, WIDTH),
            bf(PACKED, TOKENS), bf(TOKENS, PACKED), bf(TOKENS, PACKED), bf(PACKED, TOKENS),
            bf(PACKED, WIDTH), bf(PACKED, WIDTH), bf(PACKED, WIDTH), bf(PACKED, WIDTH),
            pltpu.VMEM((2, 6, 4, 24), jnp.int32), f32(144, 128), bf(TOKENS, 128),
            bf(TOKENS, WIDTH), bf(TOKENS, WIDTH), f32(TOKENS, WIDTH), bf(TOKENS, WIDTH), f32(TOKENS, 1),
            bf(TOKENS, 3 * WIDTH), f32(4, 4, 2, SPAN, SPAN), bf(TOKENS, WIDTH), bf(TOKENS, WIDTH),
            bf(TOKENS, 3 * WIDTH), bf(2, WIDTH, TOKENS),
            bf(PACKED, WIDTH), bf(PACKED, WIDTH), bf(PACKED, WIDTH), bf(PACKED, WIDTH),
            f32(16, 2, 8, 32, 128), f32(16, 8, 32, 128), bf(16, 2, 4, 32, 128), bf(3, 16, 2, 32, 128),
            f32(4, 4, 2, 32, 128), f32(15, 2, 32, 128), f32(2, 32, 128), f32(2, 2, 32, 128),
            pltpu.SemaphoreType.DMA((8,)),
            pltpu.SemaphoreType.DMA((4, 6)), pltpu.SemaphoreType.DMA((4, 6)),
            pltpu.SemaphoreType.DMA((2,)), pltpu.SemaphoreType.DMA((2,)),
            pltpu.SemaphoreType.DMA((36,)), pltpu.SemaphoreType.DMA((36,)),
        ],
        compiler_params=pltpu.CompilerParams(
            vmem_limit_bytes=56 << 20, collective_id=0, has_side_effects=True),
        cost_estimate=pl.CostEstimate(flops=6 * 10**9, bytes_accessed=10**7, transcendentals=0),
    )(
        tokens.reshape(TOKENS, WIDTH), cotangent.reshape(TOKENS, WIDTH), region_ids.transpose(1, 0, 2), norm_gain.reshape(1, WIDTH),
        qkv_weight, out_weight, pack, window, unpack, unwindow, row_of, column_of,
    )
    result, grad, gq, go = pl.pallas_call(
        hand_over,
        out_shape=tuple(jax.ShapeDtypeStruct(a.shape, a.dtype) for a in sums),
        in_specs=[vm] * 4,
        out_specs=(vm,) * 4,
    )(*sums)
    return (result.reshape(tokens.shape), grad.reshape(tokens.shape), gq, go.T)


def solution(mesh):
    placed = (
        P(None, "lat", "lon", None),
        P(None, "lat", "lon", None),
        P(None, "lat", "lon"),
        P(),
        P(),
        P(),
    )
    return jax.shard_map(
        on_device,
        mesh=mesh,
        in_specs=placed,
        out_specs=(
            P(None, "lat", "lon", None),
            P(None, "lat", "lon", None),
            P("lat", "lon"),
            P("lat", "lon"),
        ),
        check_vma=False,
    )
```

```python
import functools

import jax
import jax.numpy as jnp
import numpy as np
from jax import lax
from jax.experimental import pallas as pl
from jax.experimental.pallas import tpu as pltpu
from jax.sharding import PartitionSpec as P

SPAN = 144
TOKENS = 576
PACKED = 640
WIDTH = 512
NN = (((1,), (0,)), ((), ()))
NT = (((1,), (1,)), ((), ()))
BF = jnp.bfloat16
F32 = jnp.float32
MESH = pl.DeviceIdType.MESH

SECTIONS = (
    ("local", 0, 224, (0, 0)),
    ("lat+", 224, 112, (1, 0)),
    ("lat-", 336, 112, (-1, 0)),
    ("lon+", 448, 48, (0, 1)),
    ("lon-", 496, 48, (0, -1)),
    ("diag+", 544, 48, (1, 1)),
    ("diag-", 592, 48, (-1, -1)),
)
GOES = {
    (0, 0, 1): "local", (0, 1, 1): "lat+", (0, 0, 0): "local",
    (0, 0, 2): "lon+", (0, 1, 0): "lat+", (0, 1, 2): "diag+",
    (1, 1, 1): "local", (1, 0, 1): "lat-", (1, 1, 2): "local",
    (1, 1, 0): "lon-", (1, 0, 2): "lat-", (1, 0, 0): "diag-",
}

def constants():
    pack = np.zeros((PACKED, TOKENS), np.float32)
    window = np.zeros((TOKENS, PACKED), np.float32)
    first = {name: row for name, row, _, _ in SECTIONS}
    filled = dict.fromkeys(first, 0)
    for t in range(TOKENS):
        l, a, o = t // 144, t // 24 % 6, t % 24
        level = (l + 1) % 4
        piece = 0 if o < 6 else 1 if o < 18 else 2
        name = GOES[level // 2, a // 3, piece]
        row = first[name] + filled[name]
        filled[name] += 1
        pack[row, t] = 1
        column = (o + 6) % 12
        which = level // 2 * 2 + (0 if piece == 1 else 1)
        window[which * SPAN + level % 2 * 72 + (a + 3) % 6 * 12 + column, row] = 1
    row_of = np.zeros((TOKENS, 144), np.float32)
    column_of = np.zeros((TOKENS, 128), np.float32)
    for which in range(4):
        source = (0, 0, 1, 2)[which]
        for n in range(SPAN):
            t = which * SPAN + n
            row_of[t, (source * 6 + n // 12 % 6) * 8 + n // 72 + (2 if source else 0)] = 1
            column_of[t, n % 12 + (12 if which % 2 == 0 else 0)] = 1
    made = pack, window, pack.T, window.T, row_of, column_of
    return [jnp.asarray(m, BF) for m in made]


def dot(a, b, dims=NN):
    return lax.dot_general(a, b, dims, preferred_element_type=F32)


def kernel(x_hbm, cot_hbm, region_ref, gain_ref, w_hbm, wo_hbm,
           pack_hbm, window_hbm, unpack_hbm, unwindow_hbm, row_ref, column_ref,
           result_hbm, grad_hbm, gq_ref, go_ref,
           x_ref, cot_ref, w_ref, wo_ref, pack_ref, window_ref, unpack_ref, unwindow_ref,
           px_ref, pc_ref, rx_ref, rc_ref, regions_ref, rr_ref, hot_ref,
           xw_ref, cw_ref, normed_ref, nbf_ref, inv_ref, proj_ref, aw_ref, att_ref, ga_ref, gp_ref, tr_ref,
           po_ref, pg_ref, ro_ref, rg_ref,
           gw_ref, r0_ref, zs_ref, zr_ref, ps_ref, pr_ref, fin_ref, all_ref, result_ref, grad_ref,
           load_sem, halo_send, halo_recv, region_send, region_recv, rs_send, rs_recv, out_sem):
    lat, lon = lax.axis_index("lat"), lax.axis_index("lon")
    core = lon % 2
    at = (lon // 8 * 2 + lat // 4, lon // 2 % 4, lat % 4)

    def near(step):
        return ((lat + step[0] + 8) % 8, (lon + step[1] + 16) % 16)

    def chip(x, y, z, c):
        return (x % 2 * 4 + z, (x // 2 * 4 + y) * 2 + c)

    def ahead(dx, dy, dz):
        return chip((at[0] + dx) % 4, (at[1] + dy) % 4, (at[2] + dz) % 4, core)

    steps = [(dx, dy) for dx in range(4) for dy in range(4) if dx or dy]
    partners = [near(step) for _, _, _, step in SECTIONS[1:]]
    partners += [chip(*at, 1 - core)]
    partners += [ahead(0, 0, k) for k in (1, 2, 3)]
    partners += [ahead(dx, dy, 0) for dx, dy in steps]
    loads = [
        pltpu.make_async_copy(src, dst, load_sem.at[n])
        for n, (src, dst) in enumerate((
            (pack_hbm, pack_ref), (x_hbm, x_ref), (cot_hbm, cot_ref), (window_hbm, window_ref), (w_hbm, w_ref),
            (wo_hbm, wo_ref), (unwindow_hbm, unwindow_ref), (unpack_hbm, unpack_ref),
        ))
    ]
    for load in loads:
        load.start()

    barrier = pltpu.get_barrier_semaphore()
    for partner in partners:
        pl.semaphore_signal(barrier, inc=1, device_id=partner, device_id_type=MESH)

    def halo(which, src, dst, back):
        made = []
        for n, (_, row, rows, step) in enumerate(SECTIONS[1:]):
            to = near((-step[0], -step[1])) if back else near(step)
            made.append(pltpu.make_async_remote_copy(
                src_ref=src.at[pl.ds(row, rows)], dst_ref=dst.at[pl.ds(row, rows)],
                send_sem=halo_send.at[which, n], recv_sem=halo_recv.at[which, n],
                device_id=to, device_id_type=MESH))
        return made

    loads[0].wait()
    loads[1].wait()
    def packed(src, dst, row, rows):
        dst[pl.ds(row, rows), :] = dot(pack_ref[pl.ds(row, rows), :], src[...]).astype(BF)

    go_x = halo(0, px_ref, rx_ref, False)
    packed(x_ref, px_ref, 224, 224)
    pl.semaphore_wait(barrier, len(partners))
    for copy in go_x[:2]:
        copy.start()
    packed(x_ref, px_ref, 448, 192)
    for copy in go_x[2:]:
        copy.start()
    go_regions = [
        pltpu.make_async_remote_copy(
            src_ref=region_ref, dst_ref=regions_ref.at[n],
            send_sem=region_send.at[n], recv_sem=region_recv.at[n],
            device_id=near(step), device_id_type=MESH)
        for n, step in enumerate(((-1, 0), (-1, -1)))
    ]
    for copy in go_regions:
        copy.start()
    loads[2].wait()
    go_cot = halo(1, pc_ref, rc_ref, False)
    packed(cot_ref, pc_ref, 224, 416)
    for copy in go_cot:
        copy.start()
    packed(x_ref, rx_ref, 0, 224)
    packed(cot_ref, rc_ref, 0, 224)

    for copy in go_regions:
        copy.wait_recv()
    rr_ref[...] = jnp.zeros_like(rr_ref)
    for n in range(18):
        piece = region_ref[n % 6] if n < 6 else regions_ref[n // 6 - 1, n % 6]
        rr_ref[pl.ds(8 * n, 4), pl.ds(0, 24)] = piece.astype(F32)
    picked = dot(row_ref[...], rr_ref[...].astype(BF)) * column_ref[...].astype(F32)
    value = dot(picked.astype(BF), jnp.ones((128, 128), BF))
    lanes = lax.broadcasted_iota(jnp.int32, (TOKENS, 128), 1).astype(F32)
    hot_ref[...] = jnp.where(value == lanes, 1.0, 0.0).astype(BF)

    gain = gain_ref[...]
    loads[3].wait()
    for copy in go_x:
        copy.wait_recv()
    for w in range(4):
        rows = pl.ds(w * SPAN, SPAN)
        x = dot(window_ref[rows, :], rx_ref[...])
        xw_ref[rows, :] = x.astype(BF)
        centered = x - jnp.mean(x, -1, keepdims=True)
        var = jnp.mean(centered * centered, -1, keepdims=True)
        inv = lax.rsqrt(var + 1e-5)
        normed = centered * inv
        normed_ref[rows, :] = normed
        inv_ref[rows, :] = inv
        nbf_ref[rows, :] = (normed * gain).astype(BF)
    loads[4].wait()
    for c in range(6):
        cols = pl.ds(c * 256, 256)
        proj_ref[:, cols] = dot(nbf_ref[...], w_ref[:, cols]).astype(BF)

    lane = lax.broadcasted_iota(jnp.int32, (1, 128), 1)
    masks = [jnp.where((lane < 64) == (h == 0), 1.0, 0.0).astype(BF) for h in range(2)]
    eighths = [(m * 0.125).astype(BF) for m in masks]

    def forward(p):
        col = p * 128
        for w in range(4):
            rows = pl.ds(w * SPAN, SPAN)
            q2 = proj_ref[rows, pl.ds(col, 128)]
            k2 = proj_ref[rows, pl.ds(512 + col, 128)]
            v2 = proj_ref[rows, pl.ds(1024 + col, 128)]
            hot = hot_ref[rows, :]
            qx = jnp.concatenate([q2, hot * jnp.array(-1e30, BF)], 1)
            off = (1.0 - hot.astype(F32)).astype(BF)
            att = []
            for h in range(2):
                s = dot(qx, jnp.concatenate([k2 * eighths[h], off], 1), NT)
                e = jnp.exp(s - jnp.max(s, -1, keepdims=True))
                a = e * (1.0 / jnp.sum(e, -1, keepdims=True))
                aw_ref[p, w, h] = a
                att.append(dot(a.astype(BF), v2))
            att_ref[rows, pl.ds(col, 128)] = jnp.where(lane < 64, att[0], att[1]).astype(BF)

    for p in range(4):
        forward(p)

    loads[5].wait()
    for w in range(4):
        rows = pl.ds(w * SPAN, SPAN)
        branch = dot(att_ref[rows, :], wo_ref[...])
        xw_ref[rows, :] = (xw_ref[rows, :].astype(F32) + branch).astype(BF)
    loads[6].wait()
    po_ref[...] = dot(unwindow_ref[...], xw_ref[...]).astype(BF)
    go_out = halo(2, po_ref, ro_ref, True)
    for copy in go_out:
        copy.start()
    ro_ref[pl.ds(0, 224), :] = po_ref[pl.ds(0, 224), :]

    for copy in go_cot:
        copy.wait_recv()
    cw_ref[...] = dot(window_ref[...], rc_ref[...]).astype(BF)
    for c in range(2):
        ga_ref[:, pl.ds(c * 256, 256)] = dot(cw_ref[...], wo_ref[pl.ds(c * 256, 256), :], NT).astype(BF)

    def backward(p):
        col = p * 128
        for w in range(4):
            rows = pl.ds(w * SPAN, SPAN)
            q2 = proj_ref[rows, pl.ds(col, 128)]
            k2 = proj_ref[rows, pl.ds(512 + col, 128)]
            v2 = proj_ref[rows, pl.ds(1024 + col, 128)]
            g2 = ga_ref[rows, pl.ds(col, 128)]
            qt = (q2 * jnp.array(0.125, BF)).T
            gt = g2.T
            gq = None
            gkt = []
            gvt = []
            for h in range(2):
                a = aw_ref[p, w, h]
                gw = dot(g2, v2 * masks[h], NT)
                prod = gw * a
                inner = jnp.sum(prod, -1, keepdims=True)
                ds = (prod - a * inner).astype(BF)
                part = dot(ds, k2 * eighths[h])
                gq = part if gq is None else gq + part
                gkt.append(dot(qt[64 * h:64 * h + 64], ds))
                gvt.append(dot(gt[64 * h:64 * h + 64], a.astype(BF)))
            gp_ref[rows, pl.ds(col, 128)] = gq.astype(BF)
            gp_ref[rows, pl.ds(512 + col, 128)] = jnp.concatenate(gkt, 0).astype(BF).T
            gp_ref[rows, pl.ds(1024 + col, 128)] = jnp.concatenate(gvt, 0).astype(BF).T
            if w == 1:
                z_sends.append(z_stage(p - 1 if p else 4))

    def group(g):
        return pl.ds(3 * g, 3 if g < 4 else 4)

    def swap(g):
        return pltpu.make_async_remote_copy(
            src_ref=gw_ref.at[group(g), 1 - core], dst_ref=r0_ref.at[group(g)],
            send_sem=rs_send.at[g], recv_sem=rs_recv.at[g],
            device_id=chip(*at, 1 - core), device_id_type=MESH)

    def z_stage(g):
        swaps[g].wait_recv()
        for b in range(3 * g, 3 * g + (3 if g < 4 else 4)):
            zs_ref[b] = (gw_ref[b, core] + r0_ref[b]).astype(BF).reshape(2, 4, 32, 128)
        copies = []
        for k in (1, 2, 3):
            n = 2 + 3 * g + k
            copies.append(pltpu.make_async_remote_copy(
                src_ref=zs_ref.at[group(g), :, (at[2] + k) % 4], dst_ref=zr_ref.at[k - 1, group(g)],
                send_sem=rs_send.at[n + 2], recv_sem=rs_recv.at[n + 2],
                device_id=ahead(0, 0, k), device_id_type=MESH))
            copies[-1].start()
        return copies

    def gradient(w):
        rows = pl.ds(w * SPAN, SPAN)
        gh = dot(gp_ref[rows, :], w_ref[...], NT) * gain
        normed = normed_ref[rows, :]
        gs = inv_ref[rows, :] * (gh - jnp.mean(gh, -1, keepdims=True)
                                 - normed * jnp.mean(gh * normed, -1, keepdims=True))
        nbf_ref[rows, :] = gs.astype(BF)

    tr_ref[0] = nbf_ref[...].T
    tr_ref[1] = att_ref[...].T
    swaps = {g: swap(g) for g in range(5)}
    z_sends = []

    def keep(b, grads):
        halves = grads.reshape(8, 2, 32, 128)
        gw_ref[b, 0] = halves[:, 0]
        gw_ref[b, 1] = halves[:, 1]

    for m in range(4):
        keep(12 + m, pltpu.roll(dot(tr_ref[1], cw_ref[:, pl.ds(128 * m, 128)]), 64, 1))
    swaps[4].start()
    for p in range(4):
        backward(p)
        pieces = jnp.concatenate([gp_ref[:, pl.ds(512 * t + 128 * p, 128)] for t in range(3)], 1)
        grads = dot(tr_ref[0], pieces)
        for t in range(3):
            keep(3 * p + t, grads[:, 128 * t:128 * t + 128])
        swaps[p].start()

    def summed(b):
        total = zs_ref[b, :, at[2]].astype(F32)
        for k in range(3):
            total = total + zr_ref[k, b].astype(F32)
        return total

    def place(pairs):
        for copies in [z_sends[p + 1] for p in pairs] + (z_sends[:1] if 0 in pairs else []):
            for copy in copies:
                copy.wait_recv()
        for b in range(12):
            if b % 4 not in pairs:
                continue
            m, whole = b // 3, summed(b % 4 * 3 + b // 4)
            if b % 3 == 1:
                out = summed(12 + m)
                targets = ((0, 1, jnp.where(lane < 64, whole, out)), (1, 1, jnp.where(lane < 64, out, whole)))
            else:
                targets = ((b % 3 // 2, 0, whole),)
            for n, half, part in targets:
                for x_lo in range(2):
                    ps_ref[m // 2 * 2 + x_lo, m % 2 * 2 + n, half] = part[x_lo]

    planes = []
    for n, (dx, dy) in enumerate(steps):
        planes.append([pltpu.make_async_remote_copy(
            src_ref=ps_ref.at[(at[0] + dx) % 4, (at[1] + dy) % 4, half], dst_ref=pr_ref.at[n, half],
            send_sem=rs_send.at[20 + 2 * n + half], recv_sem=rs_recv.at[20 + 2 * n + half],
            device_id=ahead(dx, dy, 0), device_id_type=MESH) for half in range(2)])

    def start_if(n, half, early):
        x_hi, y = (at[0] + steps[n][0]) % 4 // 2, (at[1] + steps[n][1]) % 4
        first = x_hi == (0 if half else (y + 1) % 4 // 2)

        @pl.when(first if early else jnp.logical_not(first))
        def _():
            planes[n][half].start()

    place((0, 1))
    for half in range(2):
        for n in range(15):
            start_if(n, half, True)

    z_sends.append(z_stage(3))
    for w in range(4):
        gradient(w)
    pg_ref[...] = dot(unwindow_ref[...], nbf_ref[...]).astype(BF)
    go_grad = halo(3, pg_ref, rg_ref, True)
    for copy in go_grad:
        copy.start()
    rg_ref[pl.ds(0, 224), :] = pg_ref[pl.ds(0, 224), :]

    place((2, 3))
    for half in range(2):
        for n in range(15):
            start_if(n, half, False)

    loads[7].wait()
    for copy in go_out:
        copy.wait_recv()
    result_ref[...] = dot(unpack_ref[...], ro_ref[...]).astype(BF)
    outs = [pltpu.make_async_copy(result_ref, result_hbm, out_sem.at[0]),
            pltpu.make_async_copy(grad_ref, grad_hbm, out_sem.at[1])]
    outs[0].start()

    for copy in go_grad:
        copy.wait_recv()
    grad_ref[...] = (cot_ref[...].astype(F32) + dot(unpack_ref[...], rg_ref[...])).astype(BF)
    outs[1].start()
    for copies in planes:
        for copy in copies:
            copy.wait_recv()
    total = ps_ref[at[0], at[1]]
    for n in range(15):
        total = total + pr_ref[n]
    fin_ref[...] = total
    last = pltpu.make_async_remote_copy(
        src_ref=fin_ref, dst_ref=all_ref.at[core], send_sem=rs_send.at[50], recv_sem=rs_recv.at[50],
        device_id=chip(*at, 1 - core), device_id_type=MESH)
    last.start()
    all_ref[core] = fin_ref[...]
    last.wait_recv()
    whole = jnp.concatenate([all_ref[:, half].reshape(64, 128) for half in range(2)], 1)
    whole = jnp.where(at[1] % 2 == 1, pltpu.roll(whole, 64, 1), whole)
    gq_ref[...] = jnp.where(core == 1, pltpu.roll(whole, 160, 1), whole)[:, :96]
    ours = whole[:, 128:]
    go_ref[...] = jnp.where(core == 1, pltpu.roll(ours, 32, 1), pltpu.roll(ours, 64, 1)).T[:32]

    started = go_x + go_regions + go_cot + go_out + go_grad + list(swaps.values()) + [last]
    for copies in z_sends + planes:
        started += copies
    for copy in started:
        copy.wait_send()
    for copy in outs:
        copy.wait()


def hand_over(*refs):
    for n in range(4):
        refs[4 + n][...] = refs[n][...]


def on_device(tokens, cotangent, region_ids, norm_gain, qkv_weight, out_weight):
    pack, window, unpack, unwindow, row_of, column_of = constants()
    vm = pl.BlockSpec(memory_space=pltpu.VMEM)
    hbm = pl.BlockSpec(memory_space=pl.ANY)

    def bf(*shape):
        return pltpu.VMEM(shape, BF)

    def f32(*shape):
        return pltpu.VMEM(shape, F32)

    sums = pl.pallas_call(
        kernel,
        out_shape=(
            jax.ShapeDtypeStruct((TOKENS, WIDTH), BF),
            jax.ShapeDtypeStruct((TOKENS, WIDTH), BF),
            jax.ShapeDtypeStruct((64, 96), F32),
            jax.ShapeDtypeStruct((32, 64), F32),
        ),
        in_specs=[hbm, hbm, vm, vm, hbm, hbm, hbm, hbm, hbm, hbm, vm, vm],
        out_specs=(hbm, hbm, vm, vm),
        scratch_shapes=[
            bf(TOKENS, WIDTH), bf(TOKENS, WIDTH), bf(WIDTH, 3 * WIDTH), bf(WIDTH, WIDTH),
            bf(PACKED, TOKENS), bf(TOKENS, PACKED), bf(TOKENS, PACKED), bf(PACKED, TOKENS),
            bf(PACKED, WIDTH), bf(PACKED, WIDTH), bf(PACKED, WIDTH), bf(PACKED, WIDTH),
            pltpu.VMEM((2, 6, 4, 24), jnp.int32), f32(144, 128), bf(TOKENS, 128),
            bf(TOKENS, WIDTH), bf(TOKENS, WIDTH), f32(TOKENS, WIDTH), bf(TOKENS, WIDTH), f32(TOKENS, 1),
            bf(TOKENS, 3 * WIDTH), f32(4, 4, 2, SPAN, SPAN), bf(TOKENS, WIDTH), bf(TOKENS, WIDTH),
            bf(TOKENS, 3 * WIDTH), bf(2, WIDTH, TOKENS),
            bf(PACKED, WIDTH), bf(PACKED, WIDTH), bf(PACKED, WIDTH), bf(PACKED, WIDTH),
            f32(16, 2, 8, 32, 128), f32(16, 8, 32, 128), bf(16, 2, 4, 32, 128), bf(3, 16, 2, 32, 128),
            f32(4, 4, 2, 32, 128), f32(15, 2, 32, 128), f32(2, 32, 128), f32(2, 2, 32, 128),
            bf(TOKENS, WIDTH), bf(TOKENS, WIDTH),
            pltpu.SemaphoreType.DMA((8,)),
            pltpu.SemaphoreType.DMA((4, 6)), pltpu.SemaphoreType.DMA((4, 6)),
            pltpu.SemaphoreType.DMA((2,)), pltpu.SemaphoreType.DMA((2,)),
            pltpu.SemaphoreType.DMA((51,)), pltpu.SemaphoreType.DMA((51,)),
            pltpu.SemaphoreType.DMA((2,)),
        ],
        compiler_params=pltpu.CompilerParams(
            vmem_limit_bytes=56 << 20, collective_id=0, has_side_effects=True),
        cost_estimate=pl.CostEstimate(flops=6 * 10**9, bytes_accessed=10**7, transcendentals=0),
    )(
        tokens.reshape(TOKENS, WIDTH), cotangent.reshape(TOKENS, WIDTH), region_ids.transpose(1, 0, 2), norm_gain.reshape(1, WIDTH),
        qkv_weight, out_weight, pack, window, unpack, unwindow, row_of, column_of,
    )
    result, grad, gq, go = pl.pallas_call(
        hand_over,
        out_shape=tuple(jax.ShapeDtypeStruct(a.shape, a.dtype) for a in sums),
        in_specs=[vm] * 4,
        out_specs=(vm,) * 4,
    )(*sums)
    return (result.reshape(tokens.shape), grad.reshape(tokens.shape), gq, go.T)


def solution(mesh):
    placed = (
        P(None, "lat", "lon", None),
        P(None, "lat", "lon", None),
        P(None, "lat", "lon"),
        P(),
        P(),
        P(),
    )
    return jax.shard_map(
        on_device,
        mesh=mesh,
        in_specs=placed,
        out_specs=(
            P(None, "lat", "lon", None),
            P(None, "lat", "lon", None),
            P("lat", "lon"),
            P("lat", "lon"),
        ),
        check_vma=False,
    )
```

```python
import functools

import jax
import jax.numpy as jnp
import numpy as np
from jax import lax
from jax.experimental import pallas as pl
from jax.experimental.pallas import tpu as pltpu
from jax.sharding import PartitionSpec as P

SPAN = 144
TOKENS = 576
PACKED = 640
WIDTH = 512
NN = (((1,), (0,)), ((), ()))
NT = (((1,), (1,)), ((), ()))
BF = jnp.bfloat16
F32 = jnp.float32
MESH = pl.DeviceIdType.MESH

SECTIONS = (
    ("local", 0, 224, (0, 0)),
    ("lat+", 224, 112, (1, 0)),
    ("lat-", 336, 112, (-1, 0)),
    ("lon+", 448, 48, (0, 1)),
    ("lon-", 496, 48, (0, -1)),
    ("diag+", 544, 48, (1, 1)),
    ("diag-", 592, 48, (-1, -1)),
)
GOES = {
    (0, 0, 1): "local", (0, 1, 1): "lat+", (0, 0, 0): "local",
    (0, 0, 2): "lon+", (0, 1, 0): "lat+", (0, 1, 2): "diag+",
    (1, 1, 1): "local", (1, 0, 1): "lat-", (1, 1, 2): "local",
    (1, 1, 0): "lon-", (1, 0, 2): "lat-", (1, 0, 0): "diag-",
}

def constants():
    pack = np.zeros((PACKED, TOKENS), np.float32)
    window = np.zeros((TOKENS, PACKED), np.float32)
    first = {name: row for name, row, _, _ in SECTIONS}
    filled = dict.fromkeys(first, 0)
    for t in range(TOKENS):
        l, a, o = t // 144, t // 24 % 6, t % 24
        level = (l + 1) % 4
        piece = 0 if o < 6 else 1 if o < 18 else 2
        name = GOES[level // 2, a // 3, piece]
        row = first[name] + filled[name]
        filled[name] += 1
        pack[row, t] = 1
        column = (o + 6) % 12
        which = level // 2 * 2 + (0 if piece == 1 else 1)
        window[which * SPAN + level % 2 * 72 + (a + 3) % 6 * 12 + column, row] = 1
    row_of = np.zeros((TOKENS, 144), np.float32)
    column_of = np.zeros((TOKENS, 128), np.float32)
    for which in range(4):
        source = (0, 0, 1, 2)[which]
        for n in range(SPAN):
            t = which * SPAN + n
            row_of[t, (source * 6 + n // 12 % 6) * 8 + n // 72 + (2 if source else 0)] = 1
            column_of[t, n % 12 + (12 if which % 2 == 0 else 0)] = 1
    made = pack, window, pack.T, window.T, row_of, column_of
    return [jnp.asarray(m, BF) for m in made]


def dot(a, b, dims=NN):
    return lax.dot_general(a, b, dims, preferred_element_type=F32)


def kernel(x_hbm, cot_hbm, region_hbm, gain_hbm, w_hbm, wo_hbm,
           pack_hbm, window_hbm, unpack_hbm, unwindow_hbm, row_hbm, column_hbm,
           result_hbm, grad_hbm, gq_ref, go_ref,
           region_ref, gain_ref, row_ref, column_ref,
           x_ref, cot_ref, w_ref, wo_ref, pack_ref, window_ref, unpack_ref, unwindow_ref,
           px_ref, pc_ref, rx_ref, rc_ref, regions_ref, rr_ref, hot_ref,
           xw_ref, cw_ref, normed_ref, nbf_ref, inv_ref, proj_ref, aw_ref, att_ref, ga_ref, gp_ref, tr_ref,
           po_ref, pg_ref, ro_ref, rg_ref,
           gw_ref, r0_ref, zs_ref, zr_ref, ps_ref, pr_ref, fin_ref, all_ref, result_ref, grad_ref,
           load_sem, halo_send, halo_recv, region_send, region_recv, rs_send, rs_recv, out_sem):
    lat, lon = lax.axis_index("lat"), lax.axis_index("lon")
    core = lon % 2
    at = (lon // 8 * 2 + lat // 4, lon // 2 % 4, lat % 4)

    def near(step):
        return ((lat + step[0] + 8) % 8, (lon + step[1] + 16) % 16)

    def chip(x, y, z, c):
        return (x % 2 * 4 + z, (x // 2 * 4 + y) * 2 + c)

    def ahead(dx, dy, dz):
        return chip((at[0] + dx) % 4, (at[1] + dy) % 4, (at[2] + dz) % 4, core)

    steps = [(dx, dy) for dx in range(4) for dy in range(4) if dx or dy]
    partners = [near(step) for _, _, _, step in SECTIONS[1:]]
    partners += [chip(*at, 1 - core)]
    partners += [ahead(0, 0, k) for k in (1, 2, 3)]
    partners += [ahead(dx, dy, 0) for dx, dy in steps]
    loads = [
        pltpu.make_async_copy(src, dst, load_sem.at[n])
        for n, (src, dst) in enumerate((
            (pack_hbm, pack_ref), (x_hbm, x_ref), (cot_hbm, cot_ref), (window_hbm, window_ref), (w_hbm, w_ref),
            (wo_hbm, wo_ref), (unwindow_hbm, unwindow_ref), (unpack_hbm, unpack_ref),
            (region_hbm, region_ref), (row_hbm, row_ref), (column_hbm, column_ref), (gain_hbm, gain_ref),
        ))
    ]
    for n in (0, 1, 2, 8, 9, 10, 11, 3, 4, 5, 6, 7):
        loads[n].start()

    barrier = pltpu.get_barrier_semaphore()
    for partner in partners:
        pl.semaphore_signal(barrier, inc=1, device_id=partner, device_id_type=MESH)

    def halo(which, src, dst, back):
        made = []
        for n, (_, row, rows, step) in enumerate(SECTIONS[1:]):
            to = near((-step[0], -step[1])) if back else near(step)
            made.append(pltpu.make_async_remote_copy(
                src_ref=src.at[pl.ds(row, rows)], dst_ref=dst.at[pl.ds(row, rows)],
                send_sem=halo_send.at[which, n], recv_sem=halo_recv.at[which, n],
                device_id=to, device_id_type=MESH))
        return made

    loads[0].wait()
    loads[1].wait()
    def packed(src, dst, row, rows):
        dst[pl.ds(row, rows), :] = dot(pack_ref[pl.ds(row, rows), :], src[...]).astype(BF)

    go_x = halo(0, px_ref, rx_ref, False)
    packed(x_ref, px_ref, 224, 224)
    pl.semaphore_wait(barrier, len(partners))
    for copy in go_x[:2]:
        copy.start()
    packed(x_ref, px_ref, 448, 192)
    for copy in go_x[2:]:
        copy.start()
    go_regions = [
        pltpu.make_async_remote_copy(
            src_ref=region_hbm, dst_ref=regions_ref.at[n],
            send_sem=region_send.at[n], recv_sem=region_recv.at[n],
            device_id=near(step), device_id_type=MESH)
        for n, step in enumerate(((-1, 0), (-1, -1)))
    ]
    for copy in go_regions:
        copy.start()
    loads[2].wait()
    go_cot = halo(1, pc_ref, rc_ref, False)
    packed(cot_ref, pc_ref, 224, 416)
    for copy in go_cot:
        copy.start()
    packed(x_ref, rx_ref, 0, 224)
    packed(cot_ref, rc_ref, 0, 224)

    for load in loads[8:]:
        load.wait()
    for copy in go_regions:
        copy.wait_recv()
    rr_ref[...] = jnp.zeros_like(rr_ref)
    for n in range(18):
        piece = region_ref[n % 6] if n < 6 else regions_ref[n // 6 - 1, n % 6]
        rr_ref[pl.ds(8 * n, 4), pl.ds(0, 24)] = piece.astype(F32)
    picked = dot(row_ref[...], rr_ref[...].astype(BF)) * column_ref[...].astype(F32)
    value = dot(picked.astype(BF), jnp.ones((128, 128), BF))
    lanes = lax.broadcasted_iota(jnp.int32, (TOKENS, 128), 1).astype(F32)
    hot_ref[...] = jnp.where(value == lanes, 1.0, 0.0).astype(BF)

    gain = gain_ref[...]
    loads[3].wait()
    for copy in go_x:
        copy.wait_recv()
    for w in range(4):
        rows = pl.ds(w * SPAN, SPAN)
        x = dot(window_ref[rows, :], rx_ref[...])
        xw_ref[rows, :] = x.astype(BF)
        centered = x - jnp.mean(x, -1, keepdims=True)
        var = jnp.mean(centered * centered, -1, keepdims=True)
        inv = lax.rsqrt(var + 1e-5)
        normed = centered * inv
        normed_ref[rows, :] = normed
        inv_ref[rows, :] = inv
        nbf_ref[rows, :] = (normed * gain).astype(BF)
    loads[4].wait()
    for c in range(6):
        cols = pl.ds(c * 256, 256)
        proj_ref[:, cols] = dot(nbf_ref[...], w_ref[:, cols]).astype(BF)

    lane = lax.broadcasted_iota(jnp.int32, (1, 128), 1)
    masks = [jnp.where((lane < 64) == (h == 0), 1.0, 0.0).astype(BF) for h in range(2)]
    eighths = [(m * 0.125).astype(BF) for m in masks]

    def forward(p):
        col = p * 128
        for w in range(4):
            rows = pl.ds(w * SPAN, SPAN)
            q2 = proj_ref[rows, pl.ds(col, 128)]
            k2 = proj_ref[rows, pl.ds(512 + col, 128)]
            v2 = proj_ref[rows, pl.ds(1024 + col, 128)]
            hot = hot_ref[rows, :]
            qx = jnp.concatenate([q2, hot * jnp.array(-1e30, BF)], 1)
            off = (1.0 - hot.astype(F32)).astype(BF)
            att = []
            for h in range(2):
                s = dot(qx, jnp.concatenate([k2 * eighths[h], off], 1), NT)
                e = jnp.exp(s - jnp.max(s, -1, keepdims=True))
                a = e * (1.0 / jnp.sum(e, -1, keepdims=True))
                aw_ref[p, w, h] = a
                att.append(dot(a.astype(BF), v2))
            att_ref[rows, pl.ds(col, 128)] = jnp.where(lane < 64, att[0], att[1]).astype(BF)

    for p in range(4):
        forward(p)

    loads[5].wait()
    for copy in go_cot:
        copy.wait_recv()
    cw_ref[...] = dot(window_ref[...], rc_ref[...]).astype(BF)
    for c in range(2):
        ga_ref[:, pl.ds(c * 256, 256)] = dot(cw_ref[...], wo_ref[pl.ds(c * 256, 256), :], NT).astype(BF)

    def backward(p):
        col = p * 128
        for w in range(4):
            rows = pl.ds(w * SPAN, SPAN)
            q2 = proj_ref[rows, pl.ds(col, 128)]
            k2 = proj_ref[rows, pl.ds(512 + col, 128)]
            v2 = proj_ref[rows, pl.ds(1024 + col, 128)]
            g2 = ga_ref[rows, pl.ds(col, 128)]
            qt = (q2 * jnp.array(0.125, BF)).T
            gt = g2.T
            gq = None
            gkt = []
            gvt = []
            for h in range(2):
                a = aw_ref[p, w, h]
                gw = dot(g2, v2 * masks[h], NT)
                prod = gw * a
                inner = jnp.sum(prod, -1, keepdims=True)
                ds = (prod - a * inner).astype(BF)
                part = dot(ds, k2 * eighths[h])
                gq = part if gq is None else gq + part
                gkt.append(dot(qt[64 * h:64 * h + 64], ds))
                gvt.append(dot(gt[64 * h:64 * h + 64], a.astype(BF)))
            gp_ref[rows, pl.ds(col, 128)] = gq.astype(BF)
            gp_ref[rows, pl.ds(512 + col, 128)] = jnp.concatenate(gkt, 0).astype(BF).T
            gp_ref[rows, pl.ds(1024 + col, 128)] = jnp.concatenate(gvt, 0).astype(BF).T
            if w == 1:
                z_sends.append(z_stage(p - 1 if p else 4))

    def group(g):
        return pl.ds(3 * g, 3 if g < 4 else 4)

    def swap(g):
        return pltpu.make_async_remote_copy(
            src_ref=gw_ref.at[group(g), 1 - core], dst_ref=r0_ref.at[group(g)],
            send_sem=rs_send.at[g], recv_sem=rs_recv.at[g],
            device_id=chip(*at, 1 - core), device_id_type=MESH)

    def z_stage(g):
        swaps[g].wait_recv()
        for b in range(3 * g, 3 * g + (3 if g < 4 else 4)):
            zs_ref[b] = (gw_ref[b, core] + r0_ref[b]).astype(BF).reshape(2, 4, 32, 128)
        copies = []
        for k in (1, 2, 3):
            n = 2 + 3 * g + k
            copies.append(pltpu.make_async_remote_copy(
                src_ref=zs_ref.at[group(g), :, (at[2] + k) % 4], dst_ref=zr_ref.at[k - 1, group(g)],
                send_sem=rs_send.at[n + 2], recv_sem=rs_recv.at[n + 2],
                device_id=ahead(0, 0, k), device_id_type=MESH))
            copies[-1].start()
        return copies

    def gradient(w):
        rows = pl.ds(w * SPAN, SPAN)
        gh = dot(gp_ref[rows, :], w_ref[...], NT) * gain
        normed = normed_ref[rows, :]
        gs = inv_ref[rows, :] * (gh - jnp.mean(gh, -1, keepdims=True)
                                 - normed * jnp.mean(gh * normed, -1, keepdims=True))
        nbf_ref[rows, :] = gs.astype(BF)

    tr_ref[0] = nbf_ref[...].T
    tr_ref[1] = att_ref[...].T
    swaps = {g: swap(g) for g in range(5)}
    z_sends = []

    def keep(b, grads):
        halves = grads.reshape(8, 2, 32, 128)
        gw_ref[b, 0] = halves[:, 0]
        gw_ref[b, 1] = halves[:, 1]

    for m in range(4):
        keep(12 + m, pltpu.roll(dot(tr_ref[1], cw_ref[:, pl.ds(128 * m, 128)]), 64, 1))
    swaps[4].start()
    for p in range(4):
        backward(p)
        pieces = jnp.concatenate([gp_ref[:, pl.ds(512 * t + 128 * p, 128)] for t in range(3)], 1)
        grads = dot(tr_ref[0], pieces)
        for t in range(3):
            keep(3 * p + t, grads[:, 128 * t:128 * t + 128])
        swaps[p].start()

    def summed(b):
        total = zs_ref[b, :, at[2]].astype(F32)
        for k in range(3):
            total = total + zr_ref[k, b].astype(F32)
        return total

    def place(pairs):
        for copies in [z_sends[p + 1] for p in pairs] + (z_sends[:1] if 0 in pairs else []):
            for copy in copies:
                copy.wait_recv()
        for b in range(12):
            if b % 4 not in pairs:
                continue
            m, whole = b // 3, summed(b % 4 * 3 + b // 4)
            if b % 3 == 1:
                out = summed(12 + m)
                targets = ((0, 1, jnp.where(lane < 64, whole, out)), (1, 1, jnp.where(lane < 64, out, whole)))
            else:
                targets = ((b % 3 // 2, 0, whole),)
            for n, half, part in targets:
                for x_lo in range(2):
                    ps_ref[m // 2 * 2 + x_lo, m % 2 * 2 + n, half] = part[x_lo]

    planes = []
    for n, (dx, dy) in enumerate(steps):
        planes.append([pltpu.make_async_remote_copy(
            src_ref=ps_ref.at[(at[0] + dx) % 4, (at[1] + dy) % 4, half], dst_ref=pr_ref.at[n, half],
            send_sem=rs_send.at[20 + 2 * n + half], recv_sem=rs_recv.at[20 + 2 * n + half],
            device_id=ahead(dx, dy, 0), device_id_type=MESH) for half in range(2)])

    def exchange(pairs):
        place(pairs)
        for half in range(2):
            for n in range(15):
                x_hi, y = (at[0] + steps[n][0]) % 4 // 2, (at[1] + steps[n][1]) % 4
                first = x_hi == (0 if half else (y + 1) % 4 // 2)
                low = y < 2
                if 0 in pairs:
                    mine = first
                elif 2 in pairs:
                    mine = jnp.logical_and(jnp.logical_not(first), jnp.logical_not(low) if half else low)
                else:
                    mine = jnp.logical_and(jnp.logical_not(first), low if half else jnp.logical_not(low))
                pl.when(mine)(planes[n][half].start)

    exchange((0, 1))

    z_sends.append(z_stage(3))
    for w in range(4):
        rows = pl.ds(w * SPAN, SPAN)
        branch = dot(att_ref[rows, :], wo_ref[...])
        xw_ref[rows, :] = (xw_ref[rows, :].astype(F32) + branch).astype(BF)
    loads[6].wait()
    po_ref[...] = dot(unwindow_ref[...], xw_ref[...]).astype(BF)
    go_out = halo(2, po_ref, ro_ref, True)
    for copy in go_out:
        copy.start()
    ro_ref[pl.ds(0, 224), :] = po_ref[pl.ds(0, 224), :]
    gradient(0)
    gradient(1)
    exchange((2,))
    gradient(2)
    gradient(3)
    pg_ref[...] = dot(unwindow_ref[...], nbf_ref[...]).astype(BF)
    go_grad = halo(3, pg_ref, rg_ref, True)
    for copy in go_grad:
        copy.start()
    rg_ref[pl.ds(0, 224), :] = pg_ref[pl.ds(0, 224), :]

    exchange((3,))

    loads[7].wait()
    for copy in go_out:
        copy.wait_recv()
    result_ref[...] = dot(unpack_ref[...], ro_ref[...]).astype(BF)
    outs = [pltpu.make_async_copy(result_ref, result_hbm, out_sem.at[0]),
            pltpu.make_async_copy(grad_ref, grad_hbm, out_sem.at[1])]
    outs[0].start()

    for copy in go_grad:
        copy.wait_recv()
    grad_ref[...] = (cot_ref[...].astype(F32) + dot(unpack_ref[...], rg_ref[...])).astype(BF)
    outs[1].start()
    for copies in planes:
        for copy in copies:
            copy.wait_recv()
    total = ps_ref[at[0], at[1]]
    for n in range(15):
        total = total + pr_ref[n]
    fin_ref[...] = total
    last = pltpu.make_async_remote_copy(
        src_ref=fin_ref, dst_ref=all_ref.at[core], send_sem=rs_send.at[50], recv_sem=rs_recv.at[50],
        device_id=chip(*at, 1 - core), device_id_type=MESH)
    last.start()
    all_ref[core] = fin_ref[...]
    last.wait_recv()
    whole = jnp.concatenate([all_ref[:, half].reshape(64, 128) for half in range(2)], 1)
    whole = jnp.where(at[1] % 2 == 1, pltpu.roll(whole, 64, 1), whole)
    gq_ref[...] = jnp.where(core == 1, pltpu.roll(whole, 160, 1), whole)[:, :96]
    ours = whole[:, 128:]
    go_ref[...] = jnp.where(core == 1, pltpu.roll(ours, 32, 1), pltpu.roll(ours, 64, 1)).T[:32]

    started = go_x + go_regions + go_cot + go_out + go_grad + list(swaps.values()) + [last]
    for copies in z_sends + planes:
        started += copies
    for copy in started:
        copy.wait_send()
    for copy in outs:
        copy.wait()


def hand_over(*refs):
    for n in range(4):
        refs[4 + n][...] = refs[n][...]


def on_device(tokens, cotangent, region_ids, norm_gain, qkv_weight, out_weight):
    pack, window, unpack, unwindow, row_of, column_of = constants()
    vm = pl.BlockSpec(memory_space=pltpu.VMEM)
    hbm = pl.BlockSpec(memory_space=pl.ANY)

    def bf(*shape):
        return pltpu.VMEM(shape, BF)

    def f32(*shape):
        return pltpu.VMEM(shape, F32)

    sums = pl.pallas_call(
        kernel,
        out_shape=(
            jax.ShapeDtypeStruct((TOKENS, WIDTH), BF),
            jax.ShapeDtypeStruct((TOKENS, WIDTH), BF),
            jax.ShapeDtypeStruct((64, 96), F32),
            jax.ShapeDtypeStruct((32, 64), F32),
        ),
        in_specs=[hbm] * 12,
        out_specs=(hbm, hbm, vm, vm),
        scratch_shapes=[
            pltpu.VMEM((6, 4, 24), jnp.int32), f32(1, WIDTH), bf(TOKENS, 144), bf(TOKENS, 128),
            bf(TOKENS, WIDTH), bf(TOKENS, WIDTH), bf(WIDTH, 3 * WIDTH), bf(WIDTH, WIDTH),
            bf(PACKED, TOKENS), bf(TOKENS, PACKED), bf(TOKENS, PACKED), bf(PACKED, TOKENS),
            bf(PACKED, WIDTH), bf(PACKED, WIDTH), bf(PACKED, WIDTH), bf(PACKED, WIDTH),
            pltpu.VMEM((2, 6, 4, 24), jnp.int32), f32(144, 128), bf(TOKENS, 128),
            bf(TOKENS, WIDTH), bf(TOKENS, WIDTH), f32(TOKENS, WIDTH), bf(TOKENS, WIDTH), f32(TOKENS, 1),
            bf(TOKENS, 3 * WIDTH), f32(4, 4, 2, SPAN, SPAN), bf(TOKENS, WIDTH), bf(TOKENS, WIDTH),
            bf(TOKENS, 3 * WIDTH), bf(2, WIDTH, TOKENS),
            bf(PACKED, WIDTH), bf(PACKED, WIDTH), bf(PACKED, WIDTH), bf(PACKED, WIDTH),
            f32(16, 2, 8, 32, 128), f32(16, 8, 32, 128), bf(16, 2, 4, 32, 128), bf(3, 16, 2, 32, 128),
            f32(4, 4, 2, 32, 128), f32(15, 2, 32, 128), f32(2, 32, 128), f32(2, 2, 32, 128),
            bf(TOKENS, WIDTH), bf(TOKENS, WIDTH),
            pltpu.SemaphoreType.DMA((12,)),
            pltpu.SemaphoreType.DMA((4, 6)), pltpu.SemaphoreType.DMA((4, 6)),
            pltpu.SemaphoreType.DMA((2,)), pltpu.SemaphoreType.DMA((2,)),
            pltpu.SemaphoreType.DMA((51,)), pltpu.SemaphoreType.DMA((51,)),
            pltpu.SemaphoreType.DMA((2,)),
        ],
        compiler_params=pltpu.CompilerParams(
            vmem_limit_bytes=56 << 20, collective_id=0, has_side_effects=True),
        cost_estimate=pl.CostEstimate(flops=6 * 10**9, bytes_accessed=10**7, transcendentals=0),
    )(
        tokens.reshape(TOKENS, WIDTH), cotangent.reshape(TOKENS, WIDTH), region_ids.transpose(1, 0, 2), norm_gain.reshape(1, WIDTH),
        qkv_weight, out_weight, pack, window, unpack, unwindow, row_of, column_of,
    )
    result, grad, gq, go = pl.pallas_call(
        hand_over,
        out_shape=tuple(jax.ShapeDtypeStruct(a.shape, a.dtype) for a in sums),
        in_specs=[vm] * 4,
        out_specs=(vm,) * 4,
    )(*sums)
    return (result.reshape(tokens.shape), grad.reshape(tokens.shape), gq, go.T)


def solution(mesh):
    placed = (
        P(None, "lat", "lon", None),
        P(None, "lat", "lon", None),
        P(None, "lat", "lon"),
        P(),
        P(),
        P(),
    )
    return jax.shard_map(
        on_device,
        mesh=mesh,
        in_specs=placed,
        out_specs=(
            P(None, "lat", "lon", None),
            P(None, "lat", "lon", None),
            P("lat", "lon"),
            P("lat", "lon"),
        ),
        check_vma=False,
    )
```

```python
import functools

import jax
import jax.numpy as jnp
import numpy as np
from jax import lax
from jax.experimental import pallas as pl
from jax.experimental.pallas import tpu as pltpu
from jax.sharding import PartitionSpec as P

SPAN = 144
TOKENS = 576
PACKED = 640
WIDTH = 512
NN = (((1,), (0,)), ((), ()))
NT = (((1,), (1,)), ((), ()))
BF = jnp.bfloat16
F32 = jnp.float32
MESH = pl.DeviceIdType.MESH

SECTIONS = (
    ("local", 0, 224, (0, 0)),
    ("lat+", 224, 112, (1, 0)),
    ("lat-", 336, 112, (-1, 0)),
    ("lon+", 448, 48, (0, 1)),
    ("lon-", 496, 48, (0, -1)),
    ("diag+", 544, 48, (1, 1)),
    ("diag-", 592, 48, (-1, -1)),
)
GOES = {
    (0, 0, 1): "local", (0, 1, 1): "lat+", (0, 0, 0): "local",
    (0, 0, 2): "lon+", (0, 1, 0): "lat+", (0, 1, 2): "diag+",
    (1, 1, 1): "local", (1, 0, 1): "lat-", (1, 1, 2): "local",
    (1, 1, 0): "lon-", (1, 0, 2): "lat-", (1, 0, 0): "diag-",
}

def constants():
    pack = np.zeros((PACKED, TOKENS), np.float32)
    window = np.zeros((TOKENS, PACKED), np.float32)
    first = {name: row for name, row, _, _ in SECTIONS}
    filled = dict.fromkeys(first, 0)
    for t in range(TOKENS):
        l, a, o = t // 144, t // 24 % 6, t % 24
        level = (l + 1) % 4
        piece = 0 if o < 6 else 1 if o < 18 else 2
        name = GOES[level // 2, a // 3, piece]
        row = first[name] + filled[name]
        filled[name] += 1
        pack[row, t] = 1
        column = (o + 6) % 12
        which = level // 2 * 2 + (0 if piece == 1 else 1)
        window[which * SPAN + level % 2 * 72 + (a + 3) % 6 * 12 + column, row] = 1
    row_of = np.zeros((TOKENS, 144), np.float32)
    column_of = np.zeros((TOKENS, 128), np.float32)
    for which in range(4):
        source = (0, 0, 1, 2)[which]
        for n in range(SPAN):
            t = which * SPAN + n
            row_of[t, (source * 6 + n // 12 % 6) * 8 + n // 72 + (2 if source else 0)] = 1
            column_of[t, n % 12 + (12 if which % 2 == 0 else 0)] = 1
    made = pack, window, pack.T, window.T, row_of, column_of
    return [jnp.asarray(m, BF) for m in made]


def dot(a, b, dims=NN):
    return lax.dot_general(a, b, dims, preferred_element_type=F32)


def kernel(x_hbm, cot_hbm, region_hbm, gain_hbm, w_hbm, wo_hbm,
           pack_hbm, window_hbm, unpack_hbm, unwindow_hbm, row_hbm, column_hbm,
           result_hbm, grad_hbm, gq_ref, go_ref,
           region_ref, gain_ref, row_ref, column_ref,
           x_ref, cot_ref, w_ref, wo_ref, pack_ref, window_ref, unpack_ref, unwindow_ref,
           px_ref, pc_ref, rx_ref, rc_ref, regions_ref, rr_ref, hot_ref,
           xw_ref, cw_ref, normed_ref, nbf_ref, inv_ref, proj_ref, aw_ref, att_ref, ga_ref, gp_ref, tr_ref,
           po_ref, pg_ref, ro_ref, rg_ref,
           gw_ref, r0_ref, zs_ref, zr_ref, ps_ref, pr_ref, fin_ref, all_ref, result_ref, grad_ref,
           load_sem, halo_send, halo_recv, region_send, region_recv, rs_send, rs_recv, out_sem):
    lat, lon = lax.axis_index("lat"), lax.axis_index("lon")
    core = lon % 2
    at = (lon // 8 * 2 + lat // 4, lon // 2 % 4, lat % 4)

    def near(step):
        return ((lat + step[0] + 8) % 8, (lon + step[1] + 16) % 16)

    def chip(x, y, z, c):
        return (x % 2 * 4 + z, (x // 2 * 4 + y) * 2 + c)

    def ahead(dx, dy, dz):
        return chip((at[0] + dx) % 4, (at[1] + dy) % 4, (at[2] + dz) % 4, core)

    steps = [(dx, dy) for dx in range(4) for dy in range(4) if dx or dy]
    partners = [near(step) for _, _, _, step in SECTIONS[1:]]
    partners += [chip(*at, 1 - core)]
    partners += [ahead(0, 0, k) for k in (1, 2, 3)]
    partners += [ahead(dx, dy, 0) for dx, dy in steps]
    loads = [
        pltpu.make_async_copy(src, dst, load_sem.at[n])
        for n, (src, dst) in enumerate((
            (pack_hbm, pack_ref), (x_hbm, x_ref), (cot_hbm, cot_ref), (window_hbm, window_ref), (w_hbm, w_ref),
            (wo_hbm, wo_ref), (unwindow_hbm, unwindow_ref), (unpack_hbm, unpack_ref),
            (region_hbm, region_ref), (row_hbm, row_ref), (column_hbm, column_ref), (gain_hbm, gain_ref),
        ))
    ]
    for n in (0, 1, 2, 8, 9, 10, 11, 3, 4, 5, 6, 7):
        loads[n].start()

    barrier = pltpu.get_barrier_semaphore()
    for partner in partners:
        pl.semaphore_signal(barrier, inc=1, device_id=partner, device_id_type=MESH)

    def halo(which, src, dst, back):
        made = []
        for n, (_, row, rows, step) in enumerate(SECTIONS[1:]):
            to = near((-step[0], -step[1])) if back else near(step)
            made.append(pltpu.make_async_remote_copy(
                src_ref=src.at[pl.ds(row, rows)], dst_ref=dst.at[pl.ds(row, rows)],
                send_sem=halo_send.at[which, n], recv_sem=halo_recv.at[which, n],
                device_id=to, device_id_type=MESH))
        return made

    loads[0].wait()
    loads[1].wait()
    def packed(src, dst, row, rows):
        dst[pl.ds(row, rows), :] = dot(pack_ref[pl.ds(row, rows), :], src[...]).astype(BF)

    go_x = halo(0, px_ref, rx_ref, False)
    packed(x_ref, px_ref, 224, 224)
    pl.semaphore_wait(barrier, len(partners))
    for copy in go_x[:2]:
        copy.start()
    packed(x_ref, px_ref, 448, 192)
    for copy in go_x[4:] + go_x[2:4]:
        copy.start()
    go_regions = [
        pltpu.make_async_remote_copy(
            src_ref=region_hbm, dst_ref=regions_ref.at[n],
            send_sem=region_send.at[n], recv_sem=region_recv.at[n],
            device_id=near(step), device_id_type=MESH)
        for n, step in enumerate(((-1, 0), (-1, -1)))
    ]
    for copy in go_regions:
        copy.start()
    loads[2].wait()
    go_cot = halo(1, pc_ref, rc_ref, False)
    packed(cot_ref, pc_ref, 224, 416)
    for copy in go_cot[4:] + go_cot[:4]:
        copy.start()
    packed(x_ref, rx_ref, 0, 224)
    packed(cot_ref, rc_ref, 0, 224)

    for load in loads[8:]:
        load.wait()
    for copy in go_regions:
        copy.wait_recv()
    rr_ref[...] = jnp.zeros_like(rr_ref)
    for n in range(18):
        piece = region_ref[n % 6] if n < 6 else regions_ref[n // 6 - 1, n % 6]
        rr_ref[pl.ds(8 * n, 4), pl.ds(0, 24)] = piece.astype(F32)
    picked = dot(row_ref[...], rr_ref[...].astype(BF)) * column_ref[...].astype(F32)
    value = dot(picked.astype(BF), jnp.ones((128, 128), BF))
    lanes = lax.broadcasted_iota(jnp.int32, (TOKENS, 128), 1).astype(F32)
    hot_ref[...] = jnp.where(value == lanes, 1.0, 0.0).astype(BF)

    gain = gain_ref[...]
    loads[3].wait()
    for copy in go_x:
        copy.wait_recv()
    for w in range(4):
        rows = pl.ds(w * SPAN, SPAN)
        x = dot(window_ref[rows, :], rx_ref[...])
        xw_ref[rows, :] = x.astype(BF)
        centered = x - jnp.mean(x, -1, keepdims=True)
        var = jnp.mean(centered * centered, -1, keepdims=True)
        inv = lax.rsqrt(var + 1e-5)
        normed = centered * inv
        normed_ref[rows, :] = normed
        inv_ref[rows, :] = inv
        nbf_ref[rows, :] = (normed * gain).astype(BF)
    loads[4].wait()
    for c in range(6):
        cols = pl.ds(c * 256, 256)
        proj_ref[:, cols] = dot(nbf_ref[...], w_ref[:, cols]).astype(BF)

    lane = lax.broadcasted_iota(jnp.int32, (1, 128), 1)
    masks = [jnp.where((lane < 64) == (h == 0), 1.0, 0.0).astype(BF) for h in range(2)]
    eighths = [(m * 0.125).astype(BF) for m in masks]

    def forward(p):
        col = p * 128
        for w in range(4):
            rows = pl.ds(w * SPAN, SPAN)
            q2 = proj_ref[rows, pl.ds(col, 128)]
            k2 = proj_ref[rows, pl.ds(512 + col, 128)]
            v2 = proj_ref[rows, pl.ds(1024 + col, 128)]
            hot = hot_ref[rows, :]
            qx = jnp.concatenate([q2, hot * jnp.array(-1e30, BF)], 1)
            off = (1.0 - hot.astype(F32)).astype(BF)
            att = []
            for h in range(2):
                s = dot(qx, jnp.concatenate([k2 * eighths[h], off], 1), NT)
                e = jnp.exp(s - jnp.max(s, -1, keepdims=True))
                a = e * (1.0 / jnp.sum(e, -1, keepdims=True))
                aw_ref[p, w, h] = a
                att.append(dot(a.astype(BF), v2))
            att_ref[rows, pl.ds(col, 128)] = jnp.where(lane < 64, att[0], att[1]).astype(BF)

    for p in range(4):
        forward(p)

    loads[5].wait()
    for w in range(4):
        rows = pl.ds(w * SPAN, SPAN)
        branch = dot(att_ref[rows, :], wo_ref[...])
        xw_ref[rows, :] = (xw_ref[rows, :].astype(F32) + branch).astype(BF)
    loads[6].wait()
    po_ref[...] = dot(unwindow_ref[...], xw_ref[...]).astype(BF)
    go_out = halo(2, po_ref, ro_ref, True)
    for copy in go_out[4:] + go_out[:4]:
        copy.start()
    ro_ref[pl.ds(0, 224), :] = po_ref[pl.ds(0, 224), :]

    for copy in go_cot:
        copy.wait_recv()
    cw_ref[...] = dot(window_ref[...], rc_ref[...]).astype(BF)
    for c in range(2):
        ga_ref[:, pl.ds(c * 256, 256)] = dot(cw_ref[...], wo_ref[pl.ds(c * 256, 256), :], NT).astype(BF)

    def backward(p):
        col = p * 128
        for w in range(4):
            rows = pl.ds(w * SPAN, SPAN)
            q2 = proj_ref[rows, pl.ds(col, 128)]
            k2 = proj_ref[rows, pl.ds(512 + col, 128)]
            v2 = proj_ref[rows, pl.ds(1024 + col, 128)]
            g2 = ga_ref[rows, pl.ds(col, 128)]
            qt = (q2 * jnp.array(0.125, BF)).T
            gt = g2.T
            gq = None
            gkt = []
            gvt = []
            for h in range(2):
                a = aw_ref[p, w, h]
                gw = dot(g2, v2 * masks[h], NT)
                prod = gw * a
                inner = jnp.sum(prod, -1, keepdims=True)
                ds = (prod - a * inner).astype(BF)
                part = dot(ds, k2 * eighths[h])
                gq = part if gq is None else gq + part
                gkt.append(dot(qt[64 * h:64 * h + 64], ds))
                gvt.append(dot(gt[64 * h:64 * h + 64], a.astype(BF)))
            gp_ref[rows, pl.ds(col, 128)] = gq.astype(BF)
            gp_ref[rows, pl.ds(512 + col, 128)] = jnp.concatenate(gkt, 0).astype(BF).T
            gp_ref[rows, pl.ds(1024 + col, 128)] = jnp.concatenate(gvt, 0).astype(BF).T
            if w == 1:
                z_sends.append(z_stage(p - 1 if p else 4))

    def group(g):
        return pl.ds(3 * g, 3 if g < 4 else 4)

    def swap(g):
        return pltpu.make_async_remote_copy(
            src_ref=gw_ref.at[group(g), 1 - core], dst_ref=r0_ref.at[group(g)],
            send_sem=rs_send.at[g], recv_sem=rs_recv.at[g],
            device_id=chip(*at, 1 - core), device_id_type=MESH)

    def z_stage(g):
        swaps[g].wait_recv()
        for b in range(3 * g, 3 * g + (3 if g < 4 else 4)):
            zs_ref[b] = (gw_ref[b, core] + r0_ref[b]).astype(BF).reshape(2, 4, 32, 128)
        copies = []
        for k in (1, 2, 3):
            n = 2 + 3 * g + k
            copies.append(pltpu.make_async_remote_copy(
                src_ref=zs_ref.at[group(g), :, (at[2] + k) % 4], dst_ref=zr_ref.at[k - 1, group(g)],
                send_sem=rs_send.at[n + 2], recv_sem=rs_recv.at[n + 2],
                device_id=ahead(0, 0, k), device_id_type=MESH))
            copies[-1].start()
        return copies

    def gradient(w):
        rows = pl.ds(w * SPAN, SPAN)
        gh = dot(gp_ref[rows, :], w_ref[...], NT) * gain
        normed = normed_ref[rows, :]
        gs = inv_ref[rows, :] * (gh - jnp.mean(gh, -1, keepdims=True)
                                 - normed * jnp.mean(gh * normed, -1, keepdims=True))
        nbf_ref[rows, :] = gs.astype(BF)

    tr_ref[0] = nbf_ref[...].T
    tr_ref[1] = att_ref[...].T
    swaps = {g: swap(g) for g in range(5)}
    z_sends = []

    def keep(b, grads):
        halves = grads.reshape(8, 2, 32, 128)
        gw_ref[b, 0] = halves[:, 0]
        gw_ref[b, 1] = halves[:, 1]

    for m in range(4):
        keep(12 + m, pltpu.roll(dot(tr_ref[1], cw_ref[:, pl.ds(128 * m, 128)]), 64, 1))
    swaps[4].start()
    for p in range(4):
        backward(p)
        pieces = jnp.concatenate([gp_ref[:, pl.ds(512 * t + 128 * p, 128)] for t in range(3)], 1)
        grads = dot(tr_ref[0], pieces)
        for t in range(3):
            keep(3 * p + t, grads[:, 128 * t:128 * t + 128])
        swaps[p].start()

    def summed(b):
        total = zs_ref[b, :, at[2]].astype(F32)
        for k in range(3):
            total = total + zr_ref[k, b].astype(F32)
        return total

    def place(pairs):
        for copies in [z_sends[p + 1] for p in pairs] + (z_sends[:1] if 0 in pairs else []):
            for copy in copies:
                copy.wait_recv()
        for b in range(12):
            if b % 4 not in pairs:
                continue
            m, whole = b // 3, summed(b % 4 * 3 + b // 4)
            if b % 3 == 1:
                out = summed(12 + m)
                targets = ((0, 1, jnp.where(lane < 64, whole, out)), (1, 1, jnp.where(lane < 64, out, whole)))
            else:
                targets = ((b % 3 // 2, 0, whole),)
            for n, half, part in targets:
                for x_lo in range(2):
                    ps_ref[m // 2 * 2 + x_lo, m % 2 * 2 + n, half] = part[x_lo]

    planes = []
    for n, (dx, dy) in enumerate(steps):
        planes.append([pltpu.make_async_remote_copy(
            src_ref=ps_ref.at[(at[0] + dx) % 4, (at[1] + dy) % 4, half], dst_ref=pr_ref.at[n, half],
            send_sem=rs_send.at[20 + 2 * n + half], recv_sem=rs_recv.at[20 + 2 * n + half],
            device_id=ahead(dx, dy, 0), device_id_type=MESH) for half in range(2)])

    def exchange(pairs):
        place(pairs)
        for half in range(2):
            for n in range(15):
                x_hi, y = (at[0] + steps[n][0]) % 4 // 2, (at[1] + steps[n][1]) % 4
                first = x_hi == (0 if half else (y + 1) % 4 // 2)
                mine = first if 0 in pairs else jnp.logical_not(first)
                pl.when(mine)(planes[n][half].start)

    gradient(0)
    gradient(1)
    gradient(2)
    z_sends.append(z_stage(3))
    exchange((0, 1))
    gradient(3)
    pg_ref[...] = dot(unwindow_ref[...], nbf_ref[...]).astype(BF)
    go_grad = halo(3, pg_ref, rg_ref, True)
    for copy in go_grad[4:] + go_grad[:4]:
        copy.start()
    rg_ref[pl.ds(0, 224), :] = pg_ref[pl.ds(0, 224), :]

    loads[7].wait()
    for copy in go_out:
        copy.wait_recv()
    result_ref[...] = dot(unpack_ref[...], ro_ref[...]).astype(BF)
    outs = [pltpu.make_async_copy(result_ref, result_hbm, out_sem.at[0]),
            pltpu.make_async_copy(grad_ref, grad_hbm, out_sem.at[1])]
    outs[0].start()

    exchange((2, 3))

    for copy in go_grad:
        copy.wait_recv()
    grad_ref[...] = (cot_ref[...].astype(F32) + dot(unpack_ref[...], rg_ref[...])).astype(BF)
    outs[1].start()
    for copies in planes:
        for copy in copies:
            copy.wait_recv()
    total = ps_ref[at[0], at[1]]
    for n in range(15):
        total = total + pr_ref[n]
    fin_ref[...] = total
    last = pltpu.make_async_remote_copy(
        src_ref=fin_ref, dst_ref=all_ref.at[core], send_sem=rs_send.at[50], recv_sem=rs_recv.at[50],
        device_id=chip(*at, 1 - core), device_id_type=MESH)
    last.start()
    all_ref[core] = fin_ref[...]
    last.wait_recv()
    whole = jnp.concatenate([all_ref[:, half].reshape(64, 128) for half in range(2)], 1)
    whole = jnp.where(at[1] % 2 == 1, pltpu.roll(whole, 64, 1), whole)
    gq_ref[...] = jnp.where(core == 1, pltpu.roll(whole, 160, 1), whole)[:, :96]
    ours = whole[:, 128:]
    go_ref[...] = jnp.where(core == 1, pltpu.roll(ours, 32, 1), pltpu.roll(ours, 64, 1)).T[:32]

    started = go_x + go_regions + go_cot + go_out + go_grad + list(swaps.values()) + [last]
    for copies in z_sends + planes:
        started += copies
    for copy in started:
        copy.wait_send()
    for copy in outs:
        copy.wait()


def hand_over(*refs):
    for n in range(4):
        refs[4 + n][...] = refs[n][...]


def on_device(tokens, cotangent, region_ids, norm_gain, qkv_weight, out_weight):
    pack, window, unpack, unwindow, row_of, column_of = constants()
    vm = pl.BlockSpec(memory_space=pltpu.VMEM)
    hbm = pl.BlockSpec(memory_space=pl.ANY)

    def bf(*shape):
        return pltpu.VMEM(shape, BF)

    def f32(*shape):
        return pltpu.VMEM(shape, F32)

    sums = pl.pallas_call(
        kernel,
        out_shape=(
            jax.ShapeDtypeStruct((TOKENS, WIDTH), BF),
            jax.ShapeDtypeStruct((TOKENS, WIDTH), BF),
            jax.ShapeDtypeStruct((64, 96), F32),
            jax.ShapeDtypeStruct((32, 64), F32),
        ),
        in_specs=[hbm] * 12,
        out_specs=(hbm, hbm, vm, vm),
        scratch_shapes=[
            pltpu.VMEM((6, 4, 24), jnp.int32), f32(1, WIDTH), bf(TOKENS, 144), bf(TOKENS, 128),
            bf(TOKENS, WIDTH), bf(TOKENS, WIDTH), bf(WIDTH, 3 * WIDTH), bf(WIDTH, WIDTH),
            bf(PACKED, TOKENS), bf(TOKENS, PACKED), bf(TOKENS, PACKED), bf(PACKED, TOKENS),
            bf(PACKED, WIDTH), bf(PACKED, WIDTH), bf(PACKED, WIDTH), bf(PACKED, WIDTH),
            pltpu.VMEM((2, 6, 4, 24), jnp.int32), f32(144, 128), bf(TOKENS, 128),
            bf(TOKENS, WIDTH), bf(TOKENS, WIDTH), f32(TOKENS, WIDTH), bf(TOKENS, WIDTH), f32(TOKENS, 1),
            bf(TOKENS, 3 * WIDTH), f32(4, 4, 2, SPAN, SPAN), bf(TOKENS, WIDTH), bf(TOKENS, WIDTH),
            bf(TOKENS, 3 * WIDTH), bf(2, WIDTH, TOKENS),
            bf(PACKED, WIDTH), bf(PACKED, WIDTH), bf(PACKED, WIDTH), bf(PACKED, WIDTH),
            f32(16, 2, 8, 32, 128), f32(16, 8, 32, 128), bf(16, 2, 4, 32, 128), bf(3, 16, 2, 32, 128),
            f32(4, 4, 2, 32, 128), f32(15, 2, 32, 128), f32(2, 32, 128), f32(2, 2, 32, 128),
            bf(TOKENS, WIDTH), bf(TOKENS, WIDTH),
            pltpu.SemaphoreType.DMA((12,)),
            pltpu.SemaphoreType.DMA((4, 6)), pltpu.SemaphoreType.DMA((4, 6)),
            pltpu.SemaphoreType.DMA((2,)), pltpu.SemaphoreType.DMA((2,)),
            pltpu.SemaphoreType.DMA((51,)), pltpu.SemaphoreType.DMA((51,)),
            pltpu.SemaphoreType.DMA((2,)),
        ],
        compiler_params=pltpu.CompilerParams(
            vmem_limit_bytes=56 << 20, collective_id=0, has_side_effects=True),
        cost_estimate=pl.CostEstimate(flops=6 * 10**9, bytes_accessed=10**7, transcendentals=0),
    )(
        tokens.reshape(TOKENS, WIDTH), cotangent.reshape(TOKENS, WIDTH), region_ids.transpose(1, 0, 2), norm_gain.reshape(1, WIDTH),
        qkv_weight, out_weight, pack, window, unpack, unwindow, row_of, column_of,
    )
    result, grad, gq, go = pl.pallas_call(
        hand_over,
        out_shape=tuple(jax.ShapeDtypeStruct(a.shape, a.dtype) for a in sums),
        in_specs=[vm] * 4,
        out_specs=(vm,) * 4,
    )(*sums)
    return (result.reshape(tokens.shape), grad.reshape(tokens.shape), gq, go.T)


def solution(mesh):
    placed = (
        P(None, "lat", "lon", None),
        P(None, "lat", "lon", None),
        P(None, "lat", "lon"),
        P(),
        P(),
        P(),
    )
    return jax.shard_map(
        on_device,
        mesh=mesh,
        in_specs=placed,
        out_specs=(
            P(None, "lat", "lon", None),
            P(None, "lat", "lon", None),
            P("lat", "lon"),
            P("lat", "lon"),
        ),
        check_vma=False,
    )
```

```python
import functools

import jax
import jax.numpy as jnp
import numpy as np
from jax import lax
from jax.experimental import pallas as pl
from jax.experimental.pallas import tpu as pltpu
from jax.sharding import PartitionSpec as P

SPAN = 144
TOKENS = 576
PACKED = 640
WIDTH = 512
NN = (((1,), (0,)), ((), ()))
NT = (((1,), (1,)), ((), ()))
BF = jnp.bfloat16
F32 = jnp.float32
MESH = pl.DeviceIdType.MESH

SECTIONS = (
    ("local", 0, 224, (0, 0)),
    ("lat+", 224, 112, (1, 0)),
    ("lat-", 336, 112, (-1, 0)),
    ("lon+", 448, 48, (0, 1)),
    ("lon-", 496, 48, (0, -1)),
    ("diag+", 544, 48, (1, 1)),
    ("diag-", 592, 48, (-1, -1)),
)
GOES = {
    (0, 0, 1): "local", (0, 1, 1): "lat+", (0, 0, 0): "local",
    (0, 0, 2): "lon+", (0, 1, 0): "lat+", (0, 1, 2): "diag+",
    (1, 1, 1): "local", (1, 0, 1): "lat-", (1, 1, 2): "local",
    (1, 1, 0): "lon-", (1, 0, 2): "lat-", (1, 0, 0): "diag-",
}

def constants():
    pack = np.zeros((PACKED, TOKENS), np.float32)
    window = np.zeros((TOKENS, PACKED), np.float32)
    first = {name: row for name, row, _, _ in SECTIONS}
    filled = dict.fromkeys(first, 0)
    for t in range(TOKENS):
        l, a, o = t // 144, t // 24 % 6, t % 24
        level = (l + 1) % 4
        piece = 0 if o < 6 else 1 if o < 18 else 2
        name = GOES[level // 2, a // 3, piece]
        row = first[name] + filled[name]
        filled[name] += 1
        pack[row, t] = 1
        column = (o + 6) % 12
        which = level // 2 * 2 + (0 if piece == 1 else 1)
        window[which * SPAN + level % 2 * 72 + (a + 3) % 6 * 12 + column, row] = 1
    row_of = np.zeros((TOKENS, 144), np.float32)
    column_of = np.zeros((TOKENS, 128), np.float32)
    for which in range(4):
        source = (0, 0, 1, 2)[which]
        for n in range(SPAN):
            t = which * SPAN + n
            row_of[t, (source * 6 + n // 12 % 6) * 8 + n // 72 + (2 if source else 0)] = 1
            column_of[t, n % 12 + (12 if which % 2 == 0 else 0)] = 1
    made = pack, window, pack.T, window.T, row_of, column_of
    return [jnp.asarray(m, BF) for m in made]


def dot(a, b, dims=NN):
    return lax.dot_general(a, b, dims, preferred_element_type=F32)


def kernel(x_hbm, cot_hbm, region_hbm, gain_hbm, w_hbm, wo_hbm,
           pack_hbm, window_hbm, unpack_hbm, unwindow_hbm, row_hbm, column_hbm,
           result_hbm, grad_hbm, gq_ref, go_ref,
           region_ref, gain_ref, row_ref, column_ref,
           x_ref, cot_ref, w_ref, wo_ref, pack_ref, window_ref, unpack_ref, unwindow_ref,
           px_ref, pc_ref, rx_ref, rc_ref, regions_ref, rr_ref, hot_ref,
           xw_ref, cw_ref, normed_ref, nbf_ref, inv_ref, proj_ref, aw_ref, att_ref, ga_ref, gp_ref, tr_ref,
           po_ref, pg_ref, ro_ref, rg_ref,
           gw_ref, r0_ref, zs_ref, zr_ref, ps_ref, pr_ref, fin_ref, all_ref, result_ref, grad_ref,
           load_sem, halo_send, halo_recv, region_send, region_recv, rs_send, rs_recv, out_sem):
    lat, lon = lax.axis_index("lat"), lax.axis_index("lon")
    core = lon % 2
    at = (lon // 8 * 2 + lat // 4, lon // 2 % 4, lat % 4)

    def near(step):
        return ((lat + step[0] + 8) % 8, (lon + step[1] + 16) % 16)

    def chip(x, y, z, c):
        return (x % 2 * 4 + z, (x // 2 * 4 + y) * 2 + c)

    def ahead(dx, dy, dz):
        return chip((at[0] + dx) % 4, (at[1] + dy) % 4, (at[2] + dz) % 4, core)

    steps = [(dx, dy) for dx in range(4) for dy in range(4) if dx or dy]
    partners = [near(step) for _, _, _, step in SECTIONS[1:]]
    partners += [chip(*at, 1 - core)]
    partners += [ahead(0, 0, k) for k in (1, 2, 3)]
    partners += [ahead(dx, dy, 0) for dx, dy in steps]
    loads = [
        pltpu.make_async_copy(src, dst, load_sem.at[n])
        for n, (src, dst) in enumerate((
            (pack_hbm, pack_ref), (x_hbm, x_ref), (cot_hbm, cot_ref), (window_hbm, window_ref), (w_hbm, w_ref),
            (wo_hbm, wo_ref), (unwindow_hbm, unwindow_ref), (unpack_hbm, unpack_ref),
            (region_hbm, region_ref), (row_hbm, row_ref), (column_hbm, column_ref), (gain_hbm, gain_ref),
        ))
    ]
    for n in (0, 1, 2, 8, 9, 10, 11, 3, 4, 5, 6, 7):
        loads[n].start()

    barrier = pltpu.get_barrier_semaphore()
    for partner in partners:
        pl.semaphore_signal(barrier, inc=1, device_id=partner, device_id_type=MESH)

    def halo(which, src, dst, back):
        made = []
        for n, (_, row, rows, step) in enumerate(SECTIONS[1:]):
            to = near((-step[0], -step[1])) if back else near(step)
            made.append(pltpu.make_async_remote_copy(
                src_ref=src.at[pl.ds(row, rows)], dst_ref=dst.at[pl.ds(row, rows)],
                send_sem=halo_send.at[which, n], recv_sem=halo_recv.at[which, n],
                device_id=to, device_id_type=MESH))
        return made

    loads[0].wait()
    loads[1].wait()
    def packed(src, dst, row, rows):
        dst[pl.ds(row, rows), :] = dot(pack_ref[pl.ds(row, rows), :], src[...]).astype(BF)

    go_x = halo(0, px_ref, rx_ref, False)
    packed(x_ref, px_ref, 224, 224)
    pl.semaphore_wait(barrier, len(partners))
    for copy in go_x[:2]:
        copy.start()
    packed(x_ref, px_ref, 448, 192)
    for copy in go_x[4:] + go_x[2:4]:
        copy.start()
    go_regions = [
        pltpu.make_async_remote_copy(
            src_ref=region_hbm, dst_ref=regions_ref.at[n],
            send_sem=region_send.at[n], recv_sem=region_recv.at[n],
            device_id=near(step), device_id_type=MESH)
        for n, step in enumerate(((-1, 0), (-1, -1)))
    ]
    for copy in go_regions:
        copy.start()
    loads[2].wait()
    go_cot = halo(1, pc_ref, rc_ref, False)
    packed(cot_ref, pc_ref, 224, 416)
    for copy in go_cot[4:] + go_cot[:4]:
        copy.start()
    packed(x_ref, rx_ref, 0, 224)
    packed(cot_ref, rc_ref, 0, 224)

    for load in loads[8:]:
        load.wait()
    for copy in go_regions:
        copy.wait_recv()
    rr_ref[...] = jnp.zeros_like(rr_ref)
    for n in range(18):
        piece = region_ref[n % 6] if n < 6 else regions_ref[n // 6 - 1, n % 6]
        rr_ref[pl.ds(8 * n, 4), pl.ds(0, 24)] = piece.astype(F32)
    picked = dot(row_ref[...], rr_ref[...].astype(BF)) * column_ref[...].astype(F32)
    value = dot(picked.astype(BF), jnp.ones((128, 128), BF))
    lanes = lax.broadcasted_iota(jnp.int32, (TOKENS, 128), 1).astype(F32)
    hot_ref[...] = jnp.where(value == lanes, 1.0, 0.0).astype(BF)

    gain = gain_ref[...]
    loads[3].wait()
    for copy in go_x:
        copy.wait_recv()
    for w in range(4):
        rows = pl.ds(w * SPAN, SPAN)
        x = dot(window_ref[rows, :], rx_ref[...])
        xw_ref[rows, :] = x.astype(BF)
        centered = x - jnp.mean(x, -1, keepdims=True)
        var = jnp.mean(centered * centered, -1, keepdims=True)
        inv = lax.rsqrt(var + 1e-5)
        normed = centered * inv
        normed_ref[rows, :] = normed
        inv_ref[rows, :] = inv
        nbf_ref[rows, :] = (normed * gain).astype(BF)
    loads[4].wait()
    for c in range(6):
        cols = pl.ds(c * 256, 256)
        proj_ref[:, cols] = dot(nbf_ref[...], w_ref[:, cols]).astype(BF)

    lane = lax.broadcasted_iota(jnp.int32, (1, 128), 1)
    masks = [jnp.where((lane < 64) == (h == 0), 1.0, 0.0).astype(BF) for h in range(2)]
    eighths = [(m * 0.125).astype(BF) for m in masks]

    def forward(p):
        col = p * 128
        for w in range(4):
            rows = pl.ds(w * SPAN, SPAN)
            q2 = proj_ref[rows, pl.ds(col, 128)]
            k2 = proj_ref[rows, pl.ds(512 + col, 128)]
            v2 = proj_ref[rows, pl.ds(1024 + col, 128)]
            hot = hot_ref[rows, :]
            qx = jnp.concatenate([q2, hot * jnp.array(-1e30, BF)], 1)
            off = (1.0 - hot.astype(F32)).astype(BF)
            att = []
            for h in range(2):
                s = dot(qx, jnp.concatenate([k2 * eighths[h], off], 1), NT)
                e = jnp.exp(s - jnp.max(s, -1, keepdims=True))
                a = e * (1.0 / jnp.sum(e, -1, keepdims=True))
                aw_ref[p, w, h] = a
                att.append(dot(a.astype(BF), v2))
            att_ref[rows, pl.ds(col, 128)] = jnp.where(lane < 64, att[0], att[1]).astype(BF)

    for p in range(4):
        forward(p)

    loads[5].wait()
    for w in range(4):
        rows = pl.ds(w * SPAN, SPAN)
        branch = dot(att_ref[rows, :], wo_ref[...])
        xw_ref[rows, :] = (xw_ref[rows, :].astype(F32) + branch).astype(BF)
    loads[6].wait()
    po_ref[...] = dot(unwindow_ref[...], xw_ref[...]).astype(BF)
    go_out = halo(2, po_ref, ro_ref, True)
    for copy in go_out[4:] + go_out[:4]:
        copy.start()
    ro_ref[pl.ds(0, 224), :] = po_ref[pl.ds(0, 224), :]

    for copy in go_cot:
        copy.wait_recv()
    cw_ref[...] = dot(window_ref[...], rc_ref[...]).astype(BF)
    for c in range(2):
        ga_ref[:, pl.ds(c * 256, 256)] = dot(cw_ref[...], wo_ref[pl.ds(c * 256, 256), :], NT).astype(BF)

    def backward(p):
        col = p * 128
        for w in range(4):
            rows = pl.ds(w * SPAN, SPAN)
            q2 = proj_ref[rows, pl.ds(col, 128)]
            k2 = proj_ref[rows, pl.ds(512 + col, 128)]
            v2 = proj_ref[rows, pl.ds(1024 + col, 128)]
            g2 = ga_ref[rows, pl.ds(col, 128)]
            qt = (q2 * jnp.array(0.125, BF)).T
            gt = g2.T
            gq = None
            gkt = []
            gvt = []
            for h in range(2):
                a = aw_ref[p, w, h]
                gw = dot(g2, v2 * masks[h], NT)
                prod = gw * a
                inner = jnp.sum(prod, -1, keepdims=True)
                ds = (prod - a * inner).astype(BF)
                part = dot(ds, k2 * eighths[h])
                gq = part if gq is None else gq + part
                gkt.append(dot(qt[64 * h:64 * h + 64], ds))
                gvt.append(dot(gt[64 * h:64 * h + 64], a.astype(BF)))
            gp_ref[rows, pl.ds(col, 128)] = gq.astype(BF)
            gp_ref[rows, pl.ds(512 + col, 128)] = jnp.concatenate(gkt, 0).astype(BF).T
            gp_ref[rows, pl.ds(1024 + col, 128)] = jnp.concatenate(gvt, 0).astype(BF).T
            if w == 1:
                z_sends.append(z_stage(p - 1 if p else 4))

    def group(g):
        return pl.ds(3 * g, 3 if g < 4 else 4)

    def swap(g):
        return pltpu.make_async_remote_copy(
            src_ref=gw_ref.at[group(g), 1 - core], dst_ref=r0_ref.at[group(g)],
            send_sem=rs_send.at[g], recv_sem=rs_recv.at[g],
            device_id=chip(*at, 1 - core), device_id_type=MESH)

    def z_stage(g):
        swaps[g].wait_recv()
        for b in range(3 * g, 3 * g + (3 if g < 4 else 4)):
            zs_ref[b] = (gw_ref[b, core] + r0_ref[b]).astype(BF).reshape(2, 4, 32, 128)
        copies = []
        for k in (1, 2, 3):
            n = 2 + 3 * g + k
            copies.append(pltpu.make_async_remote_copy(
                src_ref=zs_ref.at[group(g), :, (at[2] + k) % 4], dst_ref=zr_ref.at[k - 1, group(g)],
                send_sem=rs_send.at[n + 2], recv_sem=rs_recv.at[n + 2],
                device_id=ahead(0, 0, k), device_id_type=MESH))
            copies[-1].start()
        return copies

    def gradient(w):
        rows = pl.ds(w * SPAN, SPAN)
        gh = dot(gp_ref[rows, :], w_ref[...], NT) * gain
        normed = normed_ref[rows, :]
        gs = inv_ref[rows, :] * (gh - jnp.mean(gh, -1, keepdims=True)
                                 - normed * jnp.mean(gh * normed, -1, keepdims=True))
        nbf_ref[rows, :] = gs.astype(BF)

    tr_ref[0] = nbf_ref[...].T
    tr_ref[1] = att_ref[...].T
    swaps = {g: swap(g) for g in range(5)}
    z_sends = []

    def keep(b, grads):
        halves = grads.reshape(8, 2, 32, 128)
        gw_ref[b, 0] = halves[:, 0]
        gw_ref[b, 1] = halves[:, 1]

    for m in range(4):
        keep(12 + m, pltpu.roll(dot(tr_ref[1], cw_ref[:, pl.ds(128 * m, 128)]), 64, 1))
    swaps[4].start()
    for p in range(4):
        backward(p)
        pieces = jnp.concatenate([gp_ref[:, pl.ds(512 * t + 128 * p, 128)] for t in range(3)], 1)
        grads = dot(tr_ref[0], pieces)
        for t in range(3):
            keep(3 * p + t, grads[:, 128 * t:128 * t + 128])
        swaps[p].start()

    def summed(b):
        total = zs_ref[b, :, at[2]].astype(F32)
        for k in range(3):
            total = total + zr_ref[k, b].astype(F32)
        return total

    def place(pairs):
        for copies in [z_sends[p + 1] for p in pairs] + (z_sends[:1] if 0 in pairs else []):
            for copy in copies:
                copy.wait_recv()
        for b in range(12):
            if b % 4 not in pairs:
                continue
            m, whole = b // 3, summed(b % 4 * 3 + b // 4)
            if b % 3 == 1:
                out = summed(12 + m)
                targets = ((0, 1, jnp.where(lane < 64, whole, out)), (1, 1, jnp.where(lane < 64, out, whole)))
            else:
                targets = ((b % 3 // 2, 0, whole),)
            for n, half, part in targets:
                for x_lo in range(2):
                    ps_ref[m // 2 * 2 + x_lo, m % 2 * 2 + n, half] = part[x_lo]

    planes = []
    for n, (dx, dy) in enumerate(steps):
        planes.append([pltpu.make_async_remote_copy(
            src_ref=ps_ref.at[(at[0] + dx) % 4, (at[1] + dy) % 4, half], dst_ref=pr_ref.at[n, half],
            send_sem=rs_send.at[20 + 2 * n + half], recv_sem=rs_recv.at[20 + 2 * n + half],
            device_id=ahead(dx, dy, 0), device_id_type=MESH) for half in range(2)])

    def exchange(pairs):
        place(pairs)
        for half in range(2):
            for n in range(15):
                x_hi, y = (at[0] + steps[n][0]) % 4 // 2, (at[1] + steps[n][1]) % 4
                first = x_hi == (0 if half else (y + 1) % 4 // 2)
                low = y < 2
                if 0 in pairs:
                    mine = first
                elif 2 in pairs:
                    mine = jnp.logical_and(jnp.logical_not(first), jnp.logical_not(low) if half else low)
                else:
                    mine = jnp.logical_and(jnp.logical_not(first), low if half else jnp.logical_not(low))
                pl.when(mine)(planes[n][half].start)

    gradient(0)
    gradient(1)
    gradient(2)
    z_sends.append(z_stage(3))
    exchange((0, 1))
    gradient(3)
    pg_ref[...] = dot(unwindow_ref[...], nbf_ref[...]).astype(BF)
    go_grad = halo(3, pg_ref, rg_ref, True)
    for copy in go_grad[4:] + go_grad[:4]:
        copy.start()
    rg_ref[pl.ds(0, 224), :] = pg_ref[pl.ds(0, 224), :]

    loads[7].wait()
    for copy in go_out:
        copy.wait_recv()
    result_ref[...] = dot(unpack_ref[...], ro_ref[...]).astype(BF)
    outs = [pltpu.make_async_copy(result_ref, result_hbm, out_sem.at[0]),
            pltpu.make_async_copy(grad_ref, grad_hbm, out_sem.at[1])]
    outs[0].start()

    exchange((2,))
    exchange((3,))

    for copy in go_grad:
        copy.wait_recv()
    grad_ref[...] = (cot_ref[...].astype(F32) + dot(unpack_ref[...], rg_ref[...])).astype(BF)
    outs[1].start()
    for copies in planes:
        for copy in copies:
            copy.wait_recv()
    total = ps_ref[at[0], at[1]]
    for n in range(15):
        total = total + pr_ref[n]
    fin_ref[...] = total
    last = pltpu.make_async_remote_copy(
        src_ref=fin_ref, dst_ref=all_ref.at[core], send_sem=rs_send.at[50], recv_sem=rs_recv.at[50],
        device_id=chip(*at, 1 - core), device_id_type=MESH)
    last.start()
    all_ref[core] = fin_ref[...]
    last.wait_recv()
    whole = jnp.concatenate([all_ref[:, half].reshape(64, 128) for half in range(2)], 1)
    whole = jnp.where(at[1] % 2 == 1, pltpu.roll(whole, 64, 1), whole)
    gq_ref[...] = jnp.where(core == 1, pltpu.roll(whole, 160, 1), whole)[:, :96]
    ours = whole[:, 128:]
    go_ref[...] = jnp.where(core == 1, pltpu.roll(ours, 32, 1), pltpu.roll(ours, 64, 1)).T[:32]

    started = go_x + go_regions + go_cot + go_out + go_grad + list(swaps.values()) + [last]
    for copies in z_sends + planes:
        started += copies
    for copy in started:
        copy.wait_send()
    for copy in outs:
        copy.wait()


def hand_over(*refs):
    for n in range(4):
        refs[4 + n][...] = refs[n][...]


def on_device(tokens, cotangent, region_ids, norm_gain, qkv_weight, out_weight):
    pack, window, unpack, unwindow, row_of, column_of = constants()
    vm = pl.BlockSpec(memory_space=pltpu.VMEM)
    hbm = pl.BlockSpec(memory_space=pl.ANY)

    def bf(*shape):
        return pltpu.VMEM(shape, BF)

    def f32(*shape):
        return pltpu.VMEM(shape, F32)

    sums = pl.pallas_call(
        kernel,
        out_shape=(
            jax.ShapeDtypeStruct((TOKENS, WIDTH), BF),
            jax.ShapeDtypeStruct((TOKENS, WIDTH), BF),
            jax.ShapeDtypeStruct((64, 96), F32),
            jax.ShapeDtypeStruct((32, 64), F32),
        ),
        in_specs=[hbm] * 12,
        out_specs=(hbm, hbm, vm, vm),
        scratch_shapes=[
            pltpu.VMEM((6, 4, 24), jnp.int32), f32(1, WIDTH), bf(TOKENS, 144), bf(TOKENS, 128),
            bf(TOKENS, WIDTH), bf(TOKENS, WIDTH), bf(WIDTH, 3 * WIDTH), bf(WIDTH, WIDTH),
            bf(PACKED, TOKENS), bf(TOKENS, PACKED), bf(TOKENS, PACKED), bf(PACKED, TOKENS),
            bf(PACKED, WIDTH), bf(PACKED, WIDTH), bf(PACKED, WIDTH), bf(PACKED, WIDTH),
            pltpu.VMEM((2, 6, 4, 24), jnp.int32), f32(144, 128), bf(TOKENS, 128),
            bf(TOKENS, WIDTH), bf(TOKENS, WIDTH), f32(TOKENS, WIDTH), bf(TOKENS, WIDTH), f32(TOKENS, 1),
            bf(TOKENS, 3 * WIDTH), f32(4, 4, 2, SPAN, SPAN), bf(TOKENS, WIDTH), bf(TOKENS, WIDTH),
            bf(TOKENS, 3 * WIDTH), bf(2, WIDTH, TOKENS),
            bf(PACKED, WIDTH), bf(PACKED, WIDTH), bf(PACKED, WIDTH), bf(PACKED, WIDTH),
            f32(16, 2, 8, 32, 128), f32(16, 8, 32, 128), bf(16, 2, 4, 32, 128), bf(3, 16, 2, 32, 128),
            f32(4, 4, 2, 32, 128), f32(15, 2, 32, 128), f32(2, 32, 128), f32(2, 2, 32, 128),
            bf(TOKENS, WIDTH), bf(TOKENS, WIDTH),
            pltpu.SemaphoreType.DMA((12,)),
            pltpu.SemaphoreType.DMA((4, 6)), pltpu.SemaphoreType.DMA((4, 6)),
            pltpu.SemaphoreType.DMA((2,)), pltpu.SemaphoreType.DMA((2,)),
            pltpu.SemaphoreType.DMA((51,)), pltpu.SemaphoreType.DMA((51,)),
            pltpu.SemaphoreType.DMA((2,)),
        ],
        compiler_params=pltpu.CompilerParams(
            vmem_limit_bytes=56 << 20, collective_id=0, has_side_effects=True),
        cost_estimate=pl.CostEstimate(flops=6 * 10**9, bytes_accessed=10**7, transcendentals=0),
    )(
        tokens.reshape(TOKENS, WIDTH), cotangent.reshape(TOKENS, WIDTH), region_ids.transpose(1, 0, 2), norm_gain.reshape(1, WIDTH),
        qkv_weight, out_weight, pack, window, unpack, unwindow, row_of, column_of,
    )
    result, grad, gq, go = pl.pallas_call(
        hand_over,
        out_shape=tuple(jax.ShapeDtypeStruct(a.shape, a.dtype) for a in sums),
        in_specs=[vm] * 4,
        out_specs=(vm,) * 4,
    )(*sums)
    return (result.reshape(tokens.shape), grad.reshape(tokens.shape), gq, go.T)


def solution(mesh):
    placed = (
        P(None, "lat", "lon", None),
        P(None, "lat", "lon", None),
        P(None, "lat", "lon"),
        P(),
        P(),
        P(),
    )
    return jax.shard_map(
        on_device,
        mesh=mesh,
        in_specs=placed,
        out_specs=(
            P(None, "lat", "lon", None),
            P(None, "lat", "lon", None),
            P("lat", "lon"),
            P("lat", "lon"),
        ),
        check_vma=False,
    )
```

```python
import functools

import jax
import jax.numpy as jnp
import numpy as np
from jax import lax
from jax.experimental import pallas as pl
from jax.experimental.pallas import tpu as pltpu
from jax.sharding import PartitionSpec as P

SPAN = 144
TOKENS = 576
PACKED = 640
WIDTH = 512
NN = (((1,), (0,)), ((), ()))
NT = (((1,), (1,)), ((), ()))
BF = jnp.bfloat16
F32 = jnp.float32
MESH = pl.DeviceIdType.MESH

SECTIONS = (
    ("local", 0, 224, (0, 0)),
    ("lat+", 224, 112, (1, 0)),
    ("lat-", 336, 112, (-1, 0)),
    ("lon+", 448, 48, (0, 1)),
    ("lon-", 496, 48, (0, -1)),
    ("diag+", 544, 48, (1, 1)),
    ("diag-", 592, 48, (-1, -1)),
)
GOES = {
    (0, 0, 1): "local", (0, 1, 1): "lat+", (0, 0, 0): "local",
    (0, 0, 2): "lon+", (0, 1, 0): "lat+", (0, 1, 2): "diag+",
    (1, 1, 1): "local", (1, 0, 1): "lat-", (1, 1, 2): "local",
    (1, 1, 0): "lon-", (1, 0, 2): "lat-", (1, 0, 0): "diag-",
}

def constants():
    pack = np.zeros((PACKED, TOKENS), np.float32)
    window = np.zeros((TOKENS, PACKED), np.float32)
    first = {name: row for name, row, _, _ in SECTIONS}
    filled = dict.fromkeys(first, 0)
    for t in range(TOKENS):
        l, a, o = t // 144, t // 24 % 6, t % 24
        level = (l + 1) % 4
        piece = 0 if o < 6 else 1 if o < 18 else 2
        name = GOES[level // 2, a // 3, piece]
        row = first[name] + filled[name]
        filled[name] += 1
        pack[row, t] = 1
        column = (o + 6) % 12
        which = level // 2 * 2 + (0 if piece == 1 else 1)
        window[which * SPAN + level % 2 * 72 + (a + 3) % 6 * 12 + column, row] = 1
    row_of = np.zeros((TOKENS, 144), np.float32)
    column_of = np.zeros((TOKENS, 128), np.float32)
    for which in range(4):
        source = (0, 0, 1, 2)[which]
        for n in range(SPAN):
            t = which * SPAN + n
            row_of[t, (source * 6 + n // 12 % 6) * 8 + n // 72 + (2 if source else 0)] = 1
            column_of[t, n % 12 + (12 if which % 2 == 0 else 0)] = 1
    made = pack, window, pack.T, window.T, row_of, column_of
    return [jnp.asarray(m, BF) for m in made]


def dot(a, b, dims=NN):
    return lax.dot_general(a, b, dims, preferred_element_type=F32)


def kernel(x_hbm, cot_hbm, region_hbm, gain_hbm, w_hbm, wo_hbm,
           pack_hbm, window_hbm, unpack_hbm, unwindow_hbm, row_hbm, column_hbm,
           result_hbm, grad_hbm, gq_ref, go_ref,
           region_ref, gain_ref, row_ref, column_ref,
           x_ref, cot_ref, w_ref, wo_ref, pack_ref, window_ref, unpack_ref, unwindow_ref,
           px_ref, pc_ref, rx_ref, rc_ref, regions_ref, rr_ref, hot_ref,
           xw_ref, cw_ref, normed_ref, nbf_ref, inv_ref, proj_ref, aw_ref, att_ref, ga_ref, gp_ref, tr_ref,
           po_ref, pg_ref, ro_ref, rg_ref,
           gw_ref, r0_ref, zs_ref, zr_ref, ps_ref, pr_ref, fin_ref, all_ref, result_ref, grad_ref,
           load_sem, halo_send, halo_recv, region_send, region_recv, rs_send, rs_recv, out_sem):
    lat, lon = lax.axis_index("lat"), lax.axis_index("lon")
    core = lon % 2
    at = (lon // 8 * 2 + lat // 4, lon // 2 % 4, lat % 4)

    def near(step):
        return ((lat + step[0] + 8) % 8, (lon + step[1] + 16) % 16)

    def chip(x, y, z, c):
        return (x % 2 * 4 + z, (x // 2 * 4 + y) * 2 + c)

    def ahead(dx, dy, dz):
        return chip((at[0] + dx) % 4, (at[1] + dy) % 4, (at[2] + dz) % 4, core)

    steps = [(dx, dy) for dx in range(4) for dy in range(4) if dx or dy]
    partners = [near(step) for _, _, _, step in SECTIONS[1:]]
    partners += [chip(*at, 1 - core)]
    partners += [ahead(0, 0, k) for k in (1, 2, 3)]
    partners += [ahead(dx, dy, 0) for dx, dy in steps]
    loads = [
        pltpu.make_async_copy(src, dst, load_sem.at[n])
        for n, (src, dst) in enumerate((
            (pack_hbm, pack_ref), (x_hbm, x_ref), (cot_hbm, cot_ref), (window_hbm, window_ref), (w_hbm, w_ref),
            (wo_hbm, wo_ref), (unwindow_hbm, unwindow_ref), (unpack_hbm, unpack_ref),
            (region_hbm, region_ref), (row_hbm, row_ref), (column_hbm, column_ref), (gain_hbm, gain_ref),
        ))
    ]
    for n in (0, 1, 2, 8, 9, 10, 11, 3, 4, 5, 6, 7):
        loads[n].start()

    barrier = pltpu.get_barrier_semaphore()
    for partner in partners:
        pl.semaphore_signal(barrier, inc=1, device_id=partner, device_id_type=MESH)

    def halo(which, src, dst, back):
        made = []
        for n, (_, row, rows, step) in enumerate(SECTIONS[1:]):
            to = near((-step[0], -step[1])) if back else near(step)
            made.append(pltpu.make_async_remote_copy(
                src_ref=src.at[pl.ds(row, rows)], dst_ref=dst.at[pl.ds(row, rows)],
                send_sem=halo_send.at[which, n], recv_sem=halo_recv.at[which, n],
                device_id=to, device_id_type=MESH))
        return made

    loads[0].wait()
    loads[1].wait()
    def packed(src, dst, row, rows):
        dst[pl.ds(row, rows), :] = dot(pack_ref[pl.ds(row, rows), :], src[...]).astype(BF)

    go_x = halo(0, px_ref, rx_ref, False)
    packed(x_ref, px_ref, 224, 224)
    pl.semaphore_wait(barrier, len(partners))
    for copy in go_x[:2]:
        copy.start()
    packed(x_ref, px_ref, 448, 192)
    for copy in go_x[4:] + go_x[2:4]:
        copy.start()
    go_regions = [
        pltpu.make_async_remote_copy(
            src_ref=region_hbm, dst_ref=regions_ref.at[n],
            send_sem=region_send.at[n], recv_sem=region_recv.at[n],
            device_id=near(step), device_id_type=MESH)
        for n, step in enumerate(((-1, 0), (-1, -1)))
    ]
    for copy in go_regions:
        copy.start()
    loads[2].wait()
    go_cot = halo(1, pc_ref, rc_ref, False)
    packed(cot_ref, pc_ref, 224, 416)
    for copy in go_cot[4:] + go_cot[:4]:
        copy.start()
    packed(x_ref, rx_ref, 0, 224)
    packed(cot_ref, rc_ref, 0, 224)

    for load in loads[8:]:
        load.wait()
    for copy in go_regions:
        copy.wait_recv()
    rr_ref[...] = jnp.zeros_like(rr_ref)
    for n in range(18):
        piece = region_ref[n % 6] if n < 6 else regions_ref[n // 6 - 1, n % 6]
        rr_ref[pl.ds(8 * n, 4), pl.ds(0, 24)] = piece.astype(F32)
    picked = dot(row_ref[...], rr_ref[...].astype(BF)) * column_ref[...].astype(F32)
    value = dot(picked.astype(BF), jnp.ones((128, 128), BF))
    lanes = lax.broadcasted_iota(jnp.int32, (TOKENS, 128), 1).astype(F32)
    hot_ref[...] = jnp.where(value == lanes, 1.0, 0.0).astype(BF)

    gain = gain_ref[...]
    loads[3].wait()
    for copy in go_x:
        copy.wait_recv()
    for w in range(4):
        rows = pl.ds(w * SPAN, SPAN)
        x = dot(window_ref[rows, :], rx_ref[...])
        xw_ref[rows, :] = x.astype(BF)
        centered = x - jnp.mean(x, -1, keepdims=True)
        var = jnp.mean(centered * centered, -1, keepdims=True)
        inv = lax.rsqrt(var + 1e-5)
        normed = centered * inv
        normed_ref[rows, :] = normed
        inv_ref[rows, :] = inv
        nbf_ref[rows, :] = (normed * gain).astype(BF)
    loads[4].wait()
    for c in range(6):
        cols = pl.ds(c * 256, 256)
        proj_ref[:, cols] = dot(nbf_ref[...], w_ref[:, cols]).astype(BF)

    lane = lax.broadcasted_iota(jnp.int32, (1, 128), 1)
    masks = [jnp.where((lane < 64) == (h == 0), 1.0, 0.0).astype(BF) for h in range(2)]
    eighths = [(m * 0.125).astype(BF) for m in masks]

    def forward(p):
        col = p * 128
        for w in range(4):
            rows = pl.ds(w * SPAN, SPAN)
            q2 = proj_ref[rows, pl.ds(col, 128)]
            k2 = proj_ref[rows, pl.ds(512 + col, 128)]
            v2 = proj_ref[rows, pl.ds(1024 + col, 128)]
            hot = hot_ref[rows, :]
            qx = jnp.concatenate([q2, hot * jnp.array(-1e30, BF)], 1)
            off = (1.0 - hot.astype(F32)).astype(BF)
            att = []
            for h in range(2):
                s = dot(qx, jnp.concatenate([k2 * eighths[h], off], 1), NT)
                e = jnp.exp(s - jnp.max(s, -1, keepdims=True))
                a = e * (1.0 / jnp.sum(e, -1, keepdims=True))
                aw_ref[p, w, h] = a
                att.append(dot(a.astype(BF), v2))
            att_ref[rows, pl.ds(col, 128)] = jnp.where(lane < 64, att[0], att[1]).astype(BF)

    for p in range(4):
        forward(p)

    loads[5].wait()
    for w in range(4):
        rows = pl.ds(w * SPAN, SPAN)
        branch = dot(att_ref[rows, :], wo_ref[...])
        xw_ref[rows, :] = (xw_ref[rows, :].astype(F32) + branch).astype(BF)
    loads[6].wait()
    po_ref[...] = dot(unwindow_ref[...], xw_ref[...]).astype(BF)
    go_out = halo(2, po_ref, ro_ref, True)
    for copy in go_out[4:] + go_out[:4]:
        copy.start()
    ro_ref[pl.ds(0, 224), :] = po_ref[pl.ds(0, 224), :]

    for copy in go_cot:
        copy.wait_recv()
    cw_ref[...] = dot(window_ref[...], rc_ref[...]).astype(BF)
    for c in range(2):
        ga_ref[:, pl.ds(c * 256, 256)] = dot(cw_ref[...], wo_ref[pl.ds(c * 256, 256), :], NT).astype(BF)

    def backward(p):
        col = p * 128
        for w in range(4):
            rows = pl.ds(w * SPAN, SPAN)
            q2 = proj_ref[rows, pl.ds(col, 128)]
            k2 = proj_ref[rows, pl.ds(512 + col, 128)]
            v2 = proj_ref[rows, pl.ds(1024 + col, 128)]
            g2 = ga_ref[rows, pl.ds(col, 128)]
            qt = (q2 * jnp.array(0.125, BF)).T
            gt = g2.T
            gq = None
            gkt = []
            gvt = []
            for h in range(2):
                a = aw_ref[p, w, h]
                gw = dot(g2, v2 * masks[h], NT)
                prod = gw * a
                inner = jnp.sum(prod, -1, keepdims=True)
                ds = (prod - a * inner).astype(BF)
                part = dot(ds, k2 * eighths[h])
                gq = part if gq is None else gq + part
                gkt.append(dot(qt[64 * h:64 * h + 64], ds))
                gvt.append(dot(gt[64 * h:64 * h + 64], a.astype(BF)))
            gp_ref[rows, pl.ds(col, 128)] = gq.astype(BF)
            gp_ref[rows, pl.ds(512 + col, 128)] = jnp.concatenate(gkt, 0).astype(BF).T
            gp_ref[rows, pl.ds(1024 + col, 128)] = jnp.concatenate(gvt, 0).astype(BF).T
            if w == 2:
                z_sends.append(z_stage(p - 1 if p else 4))

    def group(g):
        return pl.ds(3 * g, 3 if g < 4 else 4)

    def swap(g):
        return pltpu.make_async_remote_copy(
            src_ref=gw_ref.at[group(g), 1 - core], dst_ref=r0_ref.at[group(g)],
            send_sem=rs_send.at[g], recv_sem=rs_recv.at[g],
            device_id=chip(*at, 1 - core), device_id_type=MESH)

    def z_stage(g):
        swaps[g].wait_recv()
        for b in range(3 * g, 3 * g + (3 if g < 4 else 4)):
            zs_ref[b] = (gw_ref[b, core] + r0_ref[b]).astype(BF).reshape(2, 4, 32, 128)
        copies = []
        for k in (1, 2, 3):
            n = 2 + 3 * g + k
            copies.append(pltpu.make_async_remote_copy(
                src_ref=zs_ref.at[group(g), :, (at[2] + k) % 4], dst_ref=zr_ref.at[k - 1, group(g)],
                send_sem=rs_send.at[n + 2], recv_sem=rs_recv.at[n + 2],
                device_id=ahead(0, 0, k), device_id_type=MESH))
            copies[-1].start()
        return copies

    def gradient(w):
        rows = pl.ds(w * SPAN, SPAN)
        gh = dot(gp_ref[rows, :], w_ref[...], NT) * gain
        normed = normed_ref[rows, :]
        gs = inv_ref[rows, :] * (gh - jnp.mean(gh, -1, keepdims=True)
                                 - normed * jnp.mean(gh * normed, -1, keepdims=True))
        nbf_ref[rows, :] = gs.astype(BF)

    tr_ref[0] = nbf_ref[...].T
    tr_ref[1] = att_ref[...].T
    swaps = {g: swap(g) for g in range(5)}
    z_sends = []

    def keep(b, grads):
        halves = grads.reshape(8, 2, 32, 128)
        gw_ref[b, 0] = halves[:, 0]
        gw_ref[b, 1] = halves[:, 1]

    for m in range(4):
        keep(12 + m, pltpu.roll(dot(tr_ref[1], cw_ref[:, pl.ds(128 * m, 128)]), 64, 1))
    swaps[4].start()
    for p in range(4):
        backward(p)
        pieces = jnp.concatenate([gp_ref[:, pl.ds(512 * t + 128 * p, 128)] for t in range(3)], 1)
        grads = dot(tr_ref[0], pieces)
        for t in range(3):
            keep(3 * p + t, grads[:, 128 * t:128 * t + 128])
        swaps[p].start()

    def summed(b):
        total = zs_ref[b, :, at[2]].astype(F32)
        for k in range(3):
            total = total + zr_ref[k, b].astype(F32)
        return total

    def place(pairs):
        for copies in [z_sends[p + 1] for p in pairs] + (z_sends[:1] if 0 in pairs else []):
            for copy in copies:
                copy.wait_recv()
        for b in range(12):
            if b % 4 not in pairs:
                continue
            m, whole = b // 3, summed(b % 4 * 3 + b // 4)
            if b % 3 == 1:
                out = summed(12 + m)
                targets = ((0, 1, jnp.where(lane < 64, whole, out)), (1, 1, jnp.where(lane < 64, out, whole)))
            else:
                targets = ((b % 3 // 2, 0, whole),)
            for n, half, part in targets:
                for x_lo in range(2):
                    ps_ref[m // 2 * 2 + x_lo, m % 2 * 2 + n, half] = part[x_lo]

    planes = []
    for n, (dx, dy) in enumerate(steps):
        planes.append([pltpu.make_async_remote_copy(
            src_ref=ps_ref.at[(at[0] + dx) % 4, (at[1] + dy) % 4, half], dst_ref=pr_ref.at[n, half],
            send_sem=rs_send.at[20 + 2 * n + half], recv_sem=rs_recv.at[20 + 2 * n + half],
            device_id=ahead(dx, dy, 0), device_id_type=MESH) for half in range(2)])

    def exchange(pairs):
        place(pairs)
        for half in range(2):
            for n in range(15):
                x_hi, y = (at[0] + steps[n][0]) % 4 // 2, (at[1] + steps[n][1]) % 4
                first = x_hi == (0 if half else (y + 1) % 4 // 2)
                low = y < 2
                if 0 in pairs:
                    mine = first
                elif 2 in pairs:
                    mine = jnp.logical_and(jnp.logical_not(first), jnp.logical_not(low) if half else low)
                else:
                    mine = jnp.logical_and(jnp.logical_not(first), low if half else jnp.logical_not(low))
                pl.when(mine)(planes[n][half].start)

    gradient(0)
    gradient(1)
    gradient(2)
    z_sends.append(z_stage(3))
    exchange((0, 1))
    gradient(3)
    pg_ref[...] = dot(unwindow_ref[...], nbf_ref[...]).astype(BF)
    go_grad = halo(3, pg_ref, rg_ref, True)
    for copy in go_grad[4:] + go_grad[:4]:
        copy.start()
    rg_ref[pl.ds(0, 224), :] = pg_ref[pl.ds(0, 224), :]

    loads[7].wait()
    for copy in go_out:
        copy.wait_recv()
    result_ref[...] = dot(unpack_ref[...], ro_ref[...]).astype(BF)
    outs = [pltpu.make_async_copy(result_ref, result_hbm, out_sem.at[0]),
            pltpu.make_async_copy(grad_ref, grad_hbm, out_sem.at[1])]
    outs[0].start()

    exchange((2,))
    exchange((3,))

    for copy in go_grad:
        copy.wait_recv()
    grad_ref[...] = (cot_ref[...].astype(F32) + dot(unpack_ref[...], rg_ref[...])).astype(BF)
    outs[1].start()
    for copies in planes:
        for copy in copies:
            copy.wait_recv()
    total = ps_ref[at[0], at[1]]
    for n in range(15):
        total = total + pr_ref[n]
    fin_ref[...] = total
    last = pltpu.make_async_remote_copy(
        src_ref=fin_ref, dst_ref=all_ref.at[core], send_sem=rs_send.at[50], recv_sem=rs_recv.at[50],
        device_id=chip(*at, 1 - core), device_id_type=MESH)
    last.start()
    all_ref[core] = fin_ref[...]
    last.wait_recv()
    whole = jnp.concatenate([all_ref[:, half].reshape(64, 128) for half in range(2)], 1)
    whole = jnp.where(at[1] % 2 == 1, pltpu.roll(whole, 64, 1), whole)
    gq_ref[...] = jnp.where(core == 1, pltpu.roll(whole, 160, 1), whole)[:, :96]
    ours = whole[:, 128:]
    go_ref[...] = jnp.where(core == 1, pltpu.roll(ours, 32, 1), pltpu.roll(ours, 64, 1)).T[:32]

    started = go_x + go_regions + go_cot + go_out + go_grad + list(swaps.values()) + [last]
    for copies in z_sends + planes:
        started += copies
    for copy in started:
        copy.wait_send()
    for copy in outs:
        copy.wait()


def hand_over(*refs):
    for n in range(4):
        refs[4 + n][...] = refs[n][...]


def on_device(tokens, cotangent, region_ids, norm_gain, qkv_weight, out_weight):
    pack, window, unpack, unwindow, row_of, column_of = constants()
    vm = pl.BlockSpec(memory_space=pltpu.VMEM)
    hbm = pl.BlockSpec(memory_space=pl.ANY)

    def bf(*shape):
        return pltpu.VMEM(shape, BF)

    def f32(*shape):
        return pltpu.VMEM(shape, F32)

    sums = pl.pallas_call(
        kernel,
        out_shape=(
            jax.ShapeDtypeStruct((TOKENS, WIDTH), BF),
            jax.ShapeDtypeStruct((TOKENS, WIDTH), BF),
            jax.ShapeDtypeStruct((64, 96), F32),
            jax.ShapeDtypeStruct((32, 64), F32),
        ),
        in_specs=[hbm] * 12,
        out_specs=(hbm, hbm, vm, vm),
        scratch_shapes=[
            pltpu.VMEM((6, 4, 24), jnp.int32), f32(1, WIDTH), bf(TOKENS, 144), bf(TOKENS, 128),
            bf(TOKENS, WIDTH), bf(TOKENS, WIDTH), bf(WIDTH, 3 * WIDTH), bf(WIDTH, WIDTH),
            bf(PACKED, TOKENS), bf(TOKENS, PACKED), bf(TOKENS, PACKED), bf(PACKED, TOKENS),
            bf(PACKED, WIDTH), bf(PACKED, WIDTH), bf(PACKED, WIDTH), bf(PACKED, WIDTH),
            pltpu.VMEM((2, 6, 4, 24), jnp.int32), f32(144, 128), bf(TOKENS, 128),
            bf(TOKENS, WIDTH), bf(TOKENS, WIDTH), f32(TOKENS, WIDTH), bf(TOKENS, WIDTH), f32(TOKENS, 1),
            bf(TOKENS, 3 * WIDTH), f32(4, 4, 2, SPAN, SPAN), bf(TOKENS, WIDTH), bf(TOKENS, WIDTH),
            bf(TOKENS, 3 * WIDTH), bf(2, WIDTH, TOKENS),
            bf(PACKED, WIDTH), bf(PACKED, WIDTH), bf(PACKED, WIDTH), bf(PACKED, WIDTH),
            f32(16, 2, 8, 32, 128), f32(16, 8, 32, 128), bf(16, 2, 4, 32, 128), bf(3, 16, 2, 32, 128),
            f32(4, 4, 2, 32, 128), f32(15, 2, 32, 128), f32(2, 32, 128), f32(2, 2, 32, 128),
            bf(TOKENS, WIDTH), bf(TOKENS, WIDTH),
            pltpu.SemaphoreType.DMA((12,)),
            pltpu.SemaphoreType.DMA((4, 6)), pltpu.SemaphoreType.DMA((4, 6)),
            pltpu.SemaphoreType.DMA((2,)), pltpu.SemaphoreType.DMA((2,)),
            pltpu.SemaphoreType.DMA((51,)), pltpu.SemaphoreType.DMA((51,)),
            pltpu.SemaphoreType.DMA((2,)),
        ],
        compiler_params=pltpu.CompilerParams(
            vmem_limit_bytes=56 << 20, collective_id=0, has_side_effects=True),
        cost_estimate=pl.CostEstimate(flops=6 * 10**9, bytes_accessed=10**7, transcendentals=0),
    )(
        tokens.reshape(TOKENS, WIDTH), cotangent.reshape(TOKENS, WIDTH), region_ids.transpose(1, 0, 2), norm_gain.reshape(1, WIDTH),
        qkv_weight, out_weight, pack, window, unpack, unwindow, row_of, column_of,
    )
    result, grad, gq, go = pl.pallas_call(
        hand_over,
        out_shape=tuple(jax.ShapeDtypeStruct(a.shape, a.dtype) for a in sums),
        in_specs=[vm] * 4,
        out_specs=(vm,) * 4,
    )(*sums)
    return (result.reshape(tokens.shape), grad.reshape(tokens.shape), gq, go.T)


def solution(mesh):
    placed = (
        P(None, "lat", "lon", None),
        P(None, "lat", "lon", None),
        P(None, "lat", "lon"),
        P(),
        P(),
        P(),
    )
    return jax.shard_map(
        on_device,
        mesh=mesh,
        in_specs=placed,
        out_specs=(
            P(None, "lat", "lon", None),
            P(None, "lat", "lon", None),
            P("lat", "lon"),
            P("lat", "lon"),
        ),
        check_vma=False,
    )
```
